256 devices in a mesh: slab: 8 (over y, core), blk: 32 (over x, z).
Axes of the slice: x: 4, y: 4, z: 8, core: 2. Of those that a mesh axis runs over, the one named last changes fastest.
Arguments:
- fine_in: bfloat16 [3072, 64, 512], P(('slab', 'blk')), may hold values from -6 to 6
- latent: bfloat16 [8, 32, 16, 256], P('slab', 'blk'), may hold values from -6 to 6
- w_fine: bfloat16 [448, 64], replicated, may hold values from -0.25 to 0.25
- w_down: bfloat16 [512, 256], replicated, may hold values from -2 to 2
- w_coarse: bfloat16 [6912, 256], replicated, may hold values from -0.078125 to 0.078125
- w_up: bfloat16 [256, 512], replicated, may hold values from -0.09375 to 0.09375
- neighbors: int32 [3072, 6], P(('slab', 'blk')), may hold values from -1 to 3071, as said below
- pool_owner: int32 [3072, 1], P(('slab', 'blk')), may hold values from 0 to 31; in each aligned block of 12 rows (0 to 11, 12 to 23, ...) at most 2 rows name the same one
- pool_cell: int32 [3072], P(('slab', 'blk')), may hold values from 0 to 15
- cot_fine: bfloat16 [3072, 64, 512], P(('slab', 'blk')), may hold values from -6 to 6
- cot_coarse: bfloat16 [8, 32, 16, 256], P('slab', 'blk'), may hold values from -6 to 6
Outputs:
- fine_out: bfloat16 [3072, 64, 512], P(('slab', 'blk'))
- coarse_out: bfloat16 [8, 32, 16, 256], P('slab', 'blk')
- grad_fine: bfloat16 [3072, 64, 512], P(('slab', 'blk'))
- grad_latent: bfloat16 [8, 32, 16, 256], P('slab', 'blk')
- weight_grads: float32 [2060288], P(('slab', 'blk'))
The draws below stay inside these ranges and needn't reach their ends.
Inputs may be any that keep to these rules, and one draw needn't show every extreme that they name: Blocks 12 k to 12 k + 11 belong to device k in slab+blk order. neighbors[b, d] = n >= 0 exactly when neighbors[n, d xor 1] = b; n lies on the same device as b or on the previous or next device; from each device to each of its neighbouring devices go at most 6 faces, exactly 6 except from the ends. `pool_owner`: among the 12 blocks of one device at most 2 name one owner, and that bound is reached.
All inputs are finite; a program needn't handle non-finite values.
Results may differ from the reference program's by a relative error of at most 0.013.
Values may be sent and summed in bfloat16 or wider, within the bound.
A program may use at most 128 MiB of HBM per device.

```python
import math
import jax
import jax.numpy as jnp
import numpy as np
from jax import lax

C = 64
CH = 256
VOX = 512
NBD = 12
CZD = 1
CYD = 1
NX = 16
FB = 6
PC = 2
NBALL = 3072
CELLS = 16
NZ = 8
NY = 32
N_BLK = 32


def draw_neighbors(key, part):
    key = jax.random.fold_in(key, 17)
    owners_all = NBALL // NBD
    everything = jnp.arange(NBALL, dtype=jnp.int32)
    device_of = everything // NBD
    within = everything % NBD
    order_key, rest_key = jax.random.split(key)
    remote_order = jax.random.permutation(order_key, 3 * NBD).reshape(3, NBD)
    columns_list = []
    for axis_id in range(3):
        perm_key, keep_key = jax.random.split(jax.random.fold_in(rest_key, axis_id))
        mapping = jax.random.permutation(perm_key, NBD).astype(jnp.int32)
        partner = mapping[within]
        remote = remote_order[axis_id][within] < FB
        retained = jax.random.randint(keep_key, (NBALL,), 0, 4) > 0
        usable = jnp.where(remote, device_of < owners_all - 1, retained & (partner != within))
        target = (device_of + remote.astype(jnp.int32)) * NBD + partner
        forward = jnp.where(usable, target, -1).astype(jnp.int32)
        backward = jnp.full((NBALL,), -1, jnp.int32).at[jnp.where(usable, target, NBALL)].set(everything, mode='drop')
        columns_list.append(backward)
        columns_list.append(forward)
    return jnp.stack(columns_list, axis=1).astype(jnp.int32)


def set_ends(drawn, rng, low, high):
    longest = drawn.shape.index(max(drawn.shape))
    spots = []
    for shift in (0, 1):
        where = [jax.random.randint(jax.random.fold_in(rng, axis), (), 0, length) for axis, length in enumerate(drawn.shape)]
        where[longest] = (where[longest] + shift) % drawn.shape[longest]
        spots.append(tuple(where))
    return drawn.at[spots[0]].set(low).at[spots[1]].set(high)


def steps_of(rng, dims, cuts, low, top_value):
    def one(axis_at, shards_of):
        steps = jax.random.uniform(jax.random.fold_in(jax.random.fold_in(rng, 6), axis_at), (shards_of,), jnp.float32, low / len(cuts), top_value / len(cuts))
        return jnp.repeat(jnp.exp(steps), dims[axis_at] // shards_of).reshape((-1,) + (1,) * (len(dims) - axis_at - 1))

    gain = one(*cuts[0])
    for cut in cuts[1:]:
        gain = gain * one(*cut)
    return gain


def deal_out(own_key, own, number, rows, number_of, top, most, lean):
    order = jax.random.permutation(own_key, number_of)
    packed, usual = portions_of(number_of, rows * top, most, lean, True), portions_of(number_of, rows * top, most, lean, False)
    places = jnp.arange(number_of)

    def named(tallies, offset_by):
        used = int((tallies > 0).sum())
        fixed = max(1, used // 4)
        moved = fixed + (places - fixed + offset_by * (used - fixed)) % max(1, number_of - fixed)
        return jnp.zeros((number_of,), jnp.int32).at[order[jnp.where(places < fixed, places, moved)]].set(jnp.asarray(tallies, jnp.int32))

    tallies = jnp.where(number % 4 == 0, named(packed, number // 4), named(usual, number - number // 4 - 1))
    mixed = jax.random.permutation(jax.random.fold_in(own, 3), number_of)
    source_of, receiver = mixed[0:number_of // 2 * 2:2], mixed[1:number_of // 2 * 2:2]
    margin = jnp.minimum(tallies[source_of] - 1, most - tallies[receiver]) // 2
    margin = jnp.where((source_of == order[0]) | (receiver == order[0]) | (tallies[receiver] == 0), 0, jnp.maximum(margin, 0))
    moved = jax.random.randint(jax.random.fold_in(own, 4), (number_of // 2,), 0, 1 << 20) % (margin + 1)
    tallies = tallies.at[source_of].add(-moved).at[receiver].add(moved)
    labels = jnp.searchsorted(jnp.cumsum(tallies), jnp.arange(rows * top), side="right").astype(jnp.int32)
    grid = labels.reshape(top, rows).T
    grid = grid[jax.random.permutation(jax.random.fold_in(own, 1), rows)]
    offset_by = jax.random.randint(jax.random.fold_in(own, 2), (rows, 1), 0, top)
    return jnp.take_along_axis(grid, (jnp.arange(top)[None, :] + offset_by) % top, axis=1)


def portions_of(amount, total, limit, slope, full):
    weights = [(1 << 20) // math.isqrt(grade ** slope) + 1 for grade in range(1, amount + 1)]
    largest = limit if full else min(limit, max(-(-total // amount), total * weights[0] // sum(weights)))
    least = 1 if total - largest >= amount - 1 else 0
    holding, spare = [largest] + [least] * (amount - 1), total - largest - least * (amount - 1)
    while spare > 0:
        movable = [i for i in range(1, amount) if holding[i] < largest] or [i for i in range(1, amount) if holding[i] < limit]
        pool, left = sum([weights[i] for i in movable]), spare
        for i in movable:
            extra = min(limit - holding[i], max(1, left * weights[i] // pool), spare)
            holding[i] = holding[i] + extra
            spare = spare - extra
    return np.array(holding)


def centred(stream_key, dims, deviation, limit, shards=(), kind=jnp.bfloat16):
    entries = jax.random.normal(stream_key, dims, jnp.float32) * deviation
    if len(shards) > 0:
        entries = steps_of(stream_key, dims, shards, -0.22, 0.18) * entries
    return jnp.clip(entries, min=-limit, max=limit).astype(kind)


def setup_inputs(seed: int = 0) -> dict:
    keys = jax.random.split(jax.random.key(seed), 12)
    fine_in = centred(keys[0], (NBALL, C, VOX), 1.0, 6.0, ((0, 256),))
    latent = centred(keys[1], (NZ, NY, NX, CH), 1.0, 6.0, ((0, 8), (1, 32)))
    w_fine = centred(keys[2], (7 * C, C), (7 * C) ** -0.5, 0.25)
    w_down = centred(keys[3], (8 * C, CH), (C // 8) ** -0.5, 2.0)
    w_coarse = centred(keys[4], (27 * CH, CH), (27 * CH) ** -0.5, 0.078125)
    w_up = centred(keys[5], (CH, 8 * C), (16 * CH) ** -0.5, 0.09375)
    neighbors = draw_neighbors(jax.random.fold_in(keys[11], 71), 0)
    pool_owner_keys = jax.random.split(jax.random.fold_in(keys[7], 1), NBALL // NBD)
    pool_owner_turns = jax.random.permutation(jax.random.fold_in(keys[7], 3), NBALL // NBD)
    pool_owner = jax.vmap(lambda own, number: deal_out(jax.random.fold_in(keys[7], 2), own, number, NBD, N_BLK, 1, PC, 2))(pool_owner_keys, pool_owner_turns).reshape((NBALL, 1))
    pool_cell = set_ends(jax.random.randint(keys[8], (NBALL,), 0, CELLS), jax.random.fold_in(keys[8], 1), 0, CELLS - 1).astype(jnp.int32)
    cot_fine = centred(keys[9], (NBALL, C, VOX), 1.0, 6.0, ((0, 256),))
    cot_coarse = centred(keys[10], (NZ, NY, NX, CH), 1.0, 6.0, ((0, 8), (1, 32)))
    return dict(fine_in=fine_in, latent=latent, w_fine=w_fine, w_down=w_down, w_coarse=w_coarse, w_up=w_up, neighbors=neighbors, pool_owner=pool_owner, pool_cell=pool_cell, cot_fine=cot_fine, cot_coarse=cot_coarse)


OPPOSITE = (1, 0, 3, 2, 5, 4)

def octant_sum(tensor):
    count_b, channels = (tensor.shape[0], tensor.shape[1])
    grouped = tensor.astype(jnp.float32).reshape(count_b, channels, 2, 4, 2, 4, 2, 4)
    return lax.optimization_barrier(jnp.sum(grouped, axis=(3, 5, 7))).reshape(count_b, channels * 8)

def octant_expand(values, channels):
    count_b = values.shape[0]
    spread = values.reshape(count_b, channels, 2, 1, 2, 1, 2, 1)
    return jnp.broadcast_to(spread, (count_b, channels, 2, 4, 2, 4, 2, 4)).reshape(count_b, channels, 512)

def block_faces(tensor):
    count_b, channels = (tensor.shape[0], tensor.shape[1])
    cubes = tensor.reshape(count_b, channels, 8, 8, 8)
    layers = []
    for axis_id in range(3):
        for side_id in range(2):
            boundary = lax.index_in_dim(cubes, 7 * side_id, axis_id + 2, keepdims=False)
            layers.append(boundary.reshape(count_b, channels, 64))
    return jnp.stack(layers, axis=1)

def shifted(tensor, nearby_faces):
    count_b, channels = (tensor.shape[0], tensor.shape[1])
    cubes = tensor.reshape(count_b, channels, 8, 8, 8)
    moved_list = []
    for axis_id in range(3):
        for side_id in range(2):
            shape_list = [count_b, channels, 8, 8, 8]
            shape_list[axis_id + 2] = 1
            boundary = nearby_faces[:, 2 * axis_id + side_id].reshape(shape_list)
            if side_id == 1:
                inside = lax.slice_in_dim(cubes, 1, 8, axis=axis_id + 2)
                displaced = jnp.concatenate([inside, boundary], axis=axis_id + 2)
            else:
                inside = lax.slice_in_dim(cubes, 0, 7, axis=axis_id + 2)
                displaced = jnp.concatenate([boundary, inside], axis=axis_id + 2)
            moved_list.append(displaced.reshape(count_b, channels, 512))
    return moved_list

def silu_slope(values):
    sigmoid = jax.nn.sigmoid(values)
    return sigmoid * (1.0 + values * (1.0 - sigmoid))

def coarse_conv(padded, weight):
    planes, rows_y, columns = (padded.shape[0] - 2, padded.shape[1] - 2, padded.shape[2] - 2)
    width_c = padded.shape[3]
    result = jnp.zeros((planes * rows_y * columns, weight.shape[1]), jnp.float32)
    for step_z in range(3):
        for step_y in range(3):
            joined = jnp.concatenate([padded[step_z:step_z + planes, step_y:step_y + rows_y, step_x:step_x + columns] for step_x in range(3)], axis=-1).reshape(-1, 3 * width_c)
            offset = (step_z * 3 + step_y) * 3 * width_c
            result = result + jnp.dot(joined, weight[offset:offset + 3 * width_c], preferred_element_type=jnp.float32)
    return result.reshape(planes, rows_y, columns, weight.shape[1])

def coarse_transpose(padded_grad, weight):
    planes, rows_y, columns = (padded_grad.shape[0] - 2, padded_grad.shape[1] - 2, padded_grad.shape[2] - 2)
    width_c = padded_grad.shape[3]
    result = jnp.zeros((planes * rows_y * columns, width_c), jnp.float32)
    for step_z in range(3):
        for step_y in range(3):
            joined = jnp.concatenate([padded_grad[2 - step_z:2 - step_z + planes, 2 - step_y:2 - step_y + rows_y, 2 - step_x:2 - step_x + columns] for step_x in range(3)], axis=-1).reshape(-1, 3 * width_c)
            offset = (step_z * 3 + step_y) * 3 * width_c
            block_w = weight[offset:offset + 3 * width_c].reshape(3, width_c, width_c).transpose(0, 2, 1).reshape(3 * width_c, width_c)
            result = result + jnp.dot(joined, block_w, preferred_element_type=jnp.float32)
    return result.reshape(planes, rows_y, columns, width_c)

def coarse_weight_grad(padded, grad_pre):
    planes, rows_y, columns = (padded.shape[0] - 2, padded.shape[1] - 2, padded.shape[2] - 2)
    width_c = padded.shape[3]
    flat_grad = grad_pre.reshape(-1, grad_pre.shape[3])
    pieces = []
    for step_z in range(3):
        for step_y in range(3):
            joined = jnp.concatenate([padded[step_z:step_z + planes, step_y:step_y + rows_y, step_x:step_x + columns] for step_x in range(3)], axis=-1).reshape(-1, 3 * width_c)
            pieces.append(lax.dot_general(joined, flat_grad, (((0,), (0,)), ((), ())), preferred_element_type=jnp.float32))
    return jnp.concatenate(pieces, axis=0)

def fine_conv(tap_list, weight):
    channels = tap_list[0].shape[1]
    result = jnp.zeros(tap_list[0].shape, jnp.float32)
    for tap_id in range(7):
        block_w = weight[tap_id * channels:(tap_id + 1) * channels].astype(jnp.float32)
        result = result + jnp.einsum('bkv,ko->bov', tap_list[tap_id].astype(jnp.float32), block_w)
    return result

def fine_transpose(grad_pre, back_list, weight):
    channels = grad_pre.shape[1]
    result = jnp.einsum('bov,ko->bkv', grad_pre.astype(jnp.float32), weight[0:channels].astype(jnp.float32))
    for direction in range(6):
        block_w = weight[(direction + 1) * channels:(direction + 2) * channels].astype(jnp.float32)
        result = result + jnp.einsum('bov,ko->bkv', back_list[OPPOSITE[direction]].astype(jnp.float32), block_w)
    return result

def fine_weight_grad(tap_list, grad_pre):
    pieces = []
    for tap_id in range(7):
        pieces.append(jnp.einsum('bkv,bov->ko', tap_list[tap_id].astype(jnp.float32), grad_pre.astype(jnp.float32)))
    return jnp.concatenate(pieces, axis=0)

def reference(fine_in, latent, w_fine, w_down, w_coarse, w_up, neighbors, pool_owner, pool_cell, cot_fine, cot_coarse):
    channels = fine_in.shape[1]
    total_blocks = fine_in.shape[0]
    opposite = jnp.array(OPPOSITE, jnp.int32)
    present = neighbors >= 0
    safe_ids = jnp.maximum(neighbors, 0).astype(jnp.int32)

    def nearby(tensor):
        face_rows = block_faces(tensor)
        picked = face_rows[safe_ids, opposite[None, :]]
        return jnp.where(present[:, :, None, None], picked, jnp.zeros_like(picked))
    tap_list = [fine_in] + shifted(fine_in, nearby(fine_in))
    pre_fine = fine_conv(tap_list, w_fine)
    fine_mid = (fine_in.astype(jnp.float32) + jax.nn.silu(pre_fine)).astype(jnp.bfloat16)
    octant_means = (octant_sum(fine_mid) / 64.0).astype(jnp.bfloat16)
    pooled = jnp.dot(octant_means, w_down, preferred_element_type=jnp.float32).astype(jnp.bfloat16)
    block_ids = jnp.arange(total_blocks, dtype=jnp.int32)
    slab_of = block_ids // (NBD * N_BLK)
    plane_of = slab_of * CZD + pool_cell // (CYD * NX)
    row_of = pool_owner[:, 0] * CYD + pool_cell // NX % CYD
    column_of = pool_cell % NX
    coarse_in = latent.astype(jnp.float32).at[plane_of, row_of, column_of].add(pooled.astype(jnp.float32)).astype(jnp.bfloat16)
    padded = jnp.pad(coarse_in, ((1, 1), (1, 1), (1, 1), (0, 0)))
    pre_coarse = coarse_conv(padded, w_coarse)
    coarse_out = (coarse_in.astype(jnp.float32) + jax.nn.silu(pre_coarse)).astype(jnp.bfloat16)
    lifted = coarse_out[plane_of, row_of, column_of]
    raised = jnp.dot(lifted, w_up, preferred_element_type=jnp.float32)
    fine_out = (fine_mid.astype(jnp.float32) + octant_expand(raised, channels)).astype(jnp.bfloat16)
    d_raised = octant_sum(cot_fine).astype(jnp.bfloat16)
    grad_up = lax.dot_general(lifted, d_raised, (((0,), (0,)), ((), ())), preferred_element_type=jnp.float32)
    d_lifted = lax.dot_general(d_raised, w_up, (((1,), (1,)), ((), ())), preferred_element_type=jnp.float32).astype(jnp.bfloat16)
    d_coarse_out = cot_coarse.astype(jnp.float32).at[plane_of, row_of, column_of].add(d_lifted.astype(jnp.float32))
    d_pre_coarse = (d_coarse_out * silu_slope(pre_coarse)).astype(jnp.bfloat16)
    grad_coarse_w = coarse_weight_grad(padded, d_pre_coarse)
    padded_grad = jnp.pad(d_pre_coarse, ((1, 1), (1, 1), (1, 1), (0, 0)))
    d_coarse_in = d_coarse_out + coarse_transpose(padded_grad, w_coarse)
    grad_latent = d_coarse_in.astype(jnp.bfloat16)
    d_pooled = grad_latent[plane_of, row_of, column_of]
    grad_down = lax.dot_general(octant_means, d_pooled, (((0,), (0,)), ((), ())), preferred_element_type=jnp.float32)
    d_means = lax.dot_general(d_pooled, w_down, (((1,), (1,)), ((), ())), preferred_element_type=jnp.float32)
    d_mid = cot_fine.astype(jnp.float32) + octant_expand(d_means, channels) / 64.0
    d_pre_fine = (d_mid * silu_slope(pre_fine)).astype(jnp.bfloat16)
    back_list = shifted(d_pre_fine, nearby(d_pre_fine))
    grad_fine = (d_mid + fine_transpose(d_pre_fine, back_list, w_fine)).astype(jnp.bfloat16)
    grad_fine_w = fine_weight_grad(tap_list, d_pre_fine)
    all_cells = NZ * NY * NX
    weight_grads = jnp.concatenate([grad_fine_w.reshape(-1) / math.sqrt(total_blocks * 512), grad_down.reshape(-1) / math.sqrt(total_blocks), grad_coarse_w.reshape(-1) / math.sqrt(all_cells), grad_up.reshape(-1) / math.sqrt(total_blocks)])
    return (fine_out, coarse_out, grad_fine, grad_latent, weight_grads)
```

```python
import functools
import math

import jax
import jax.numpy as jnp
import numpy as np
from jax import lax
from jax.experimental import pallas as pl
from jax.experimental.pallas import tpu as pltpu
from jax.sharding import PartitionSpec as P

NB = 12
CH = 64
VOX = 512
WID = 256
CELLS = 16
FB = 6
OPPOSITE = (1, 0, 3, 2, 5, 4)
STRIDES = (64, 8, 1)
FACES = NB * 6
PREV0 = FACES
NEXT0 = FACES + 3
ZERO = FACES + 6
SLOTS = FACES + 7
OFFSETS = ((-1, -1), (-1, 0), (-1, 1), (0, -1), (0, 1), (1, -1), (1, 0), (1, 1))
SHARD = 8048
SLAB_ROWS = 1006
MESH = pl.DeviceIdType.MESH
F32 = jnp.float32
BF16 = jnp.bfloat16


def tables():
    voxel = np.arange(VOX)
    coords = (voxel // 64, voxel // 8 % 8, voxel % 8)
    octant = 4 * (coords[0] // 4) + 2 * (coords[1] // 4) + coords[2] // 4
    pull = np.zeros((VOX, 6 * 128), np.float32)
    place = np.zeros((6, 128, VOX), np.float32)
    keep = np.ones((6, 1, VOX), np.float32)
    for axis in range(3):
        others = [coords[other] for other in range(3) if other != axis]
        index = others[0] * 8 + others[1]
        for side in range(2):
            d = 2 * axis + side
            on = coords[axis] == 7 * side
            keep[d, 0, on] = 0.0
            for half in range(2):
                pull[voxel[on], 128 * d + 64 * half + index[on]] = 1.0
                place[d, 64 * half + index[on], voxel[on]] = 1.0
    spread = (octant[:, None] == np.arange(VOX)[None, :] // 64).astype(np.float32)
    major = np.arange(VOX)
    perm = np.zeros((VOX, VOX), np.float32)
    perm[major, 8 * (major % 64) + major // 64] = 1.0
    bf = lambda a: jnp.asarray(a, BF16)
    return bf(pull), bf(place), jnp.asarray(keep), bf(spread), bf(spread.T), bf(perm), bf(perm.T)


def dot(a, b):
    return jnp.dot(a, b, preferred_element_type=F32)


def dot_nt(a, b):
    return lax.dot_general(a, b, (((1,), (1,)), ((), ())), preferred_element_type=F32)


def dot_tn(a, b):
    return lax.dot_general(a, b, (((0,), (0,)), ((), ())), preferred_element_type=F32)


def iota(shape, dim):
    return lax.broadcasted_iota(jnp.int32, shape, dim)


def kernel(
    n_slab, n_blk,
    fine, cot, latent, cotc, w_fine, w_down, w_up, w_coarse_hbm, send_sm, code_sm, owner, cell,
    pull, place, keep, spread, spread_t, perm, perm_t,
    fine_out, coarse_out, grad_fine, grad_latent, grads_out,
    w_coarse, faces1, faces2, pack1, pack2, near, placed, taps, pre, mid, dpf, big, ysum, yrow,
    wbig, pk, arr, rpk, rarr, rim1, rim2, rimsrc1, rimsrc2, gacc, land1, land2,
    gsrc, gat, xq, gbuf, wland, ssrc, sland, fsrc, fland, units, uland, gsum,
    wsem, fsend, frecv, asend, arecv, rsend, rrecv, gsend, grecv, vsend, vrecv, usend, urecv,
):
    me_s = lax.axis_index("slab")
    me_b = lax.axis_index("blk")
    total = n_slab * n_blk
    pos = me_s * n_blk + me_b
    after = lax.rem(pos + 1, total)
    before = lax.rem(pos + total - 1, total)
    rel = lambda i: (me_s, lax.rem(me_b + i, n_blk))
    column = lambda i: (lax.rem(me_s + i, n_slab), me_b)
    flat = lambda k: (lax.div(k, n_blk), lax.rem(k, n_blk))
    near_id = lambda a, b: (lax.rem(me_s + a + n_slab, n_slab), lax.rem(me_b + b + n_blk, n_blk))

    load_w = pltpu.make_async_copy(w_coarse_hbm, w_coarse, wsem)
    load_w.start()

    barrier = pltpu.get_barrier_semaphore()

    def greet(i, carry):
        pl.semaphore_signal(barrier, inc=1, device_id=rel(i), device_id_type=MESH)
        return carry

    lax.fori_loop(1, n_blk, greet, 0)
    for i in range(1, n_slab):
        pl.semaphore_signal(barrier, inc=1, device_id=column(i), device_id_type=MESH)
    for a, b in OFFSETS:
        if a != 0 and b != 0:
            pl.semaphore_signal(barrier, inc=1, device_id=near_id(a, b), device_id_type=MESH)
    for k in (before, after):
        pl.semaphore_signal(barrier, inc=1, device_id=flat(k), device_id_type=MESH)

    lane64 = iota((CH, 128), 1) // 64
    eye = (iota((CH, VOX), 1) % 64 == iota((CH, VOX), 0)).astype(F32)

    def make_faces(src, faces, pack):
        faces[ZERO] = jnp.zeros((CH, 128), BF16)

        def pull_group(g, carry):
            rows = src[pl.ds(g * 4, 4)].reshape(4 * CH, VOX)
            out = dot(rows, pull[...]).astype(BF16)
            for bb in range(4):
                for d in range(6):
                    faces[(g * 4 + bb) * 6 + d] = out[CH * bb : CH * bb + CH, 128 * d : 128 * d + 128]
            return carry

        lax.fori_loop(0, NB // 4, pull_group, 0)
        for s in range(2):
            for q in range(3):
                first = faces[send_sm[s * FB + 2 * q]].astype(F32)
                second = faces[send_sm[s * FB + 2 * q + 1]].astype(F32)
                pack[s, q] = jnp.where(lane64 == 0, first, second).astype(BF16)

    def face_copies(land, pack, k):
        return [
            pltpu.make_async_remote_copy(
                src_ref=pack.at[0], dst_ref=land.at[pl.ds(3, 3)],
                send_sem=fsend.at[2 * k], recv_sem=frecv.at[2 * k],
                device_id=flat(before), device_id_type=MESH,
            ),
            pltpu.make_async_remote_copy(
                src_ref=pack.at[1], dst_ref=land.at[pl.ds(0, 3)],
                send_sem=fsend.at[2 * k + 1], recv_sem=frecv.at[2 * k + 1],
                device_id=flat(after), device_id_type=MESH,
            ),
        ]

    def roll_taps(src):
        def body(b, carry):
            x = src[b]
            wide = x.astype(F32)
            taps[b, 0:CH, :] = x
            for d in range(6):
                stride = STRIDES[d // 2]
                moved = pltpu.roll(wide, stride if d % 2 == 0 else VOX - stride, 1)
                taps[b, CH * (d + 1) : CH * (d + 2), :] = (moved * keep[d]).astype(BF16)
            return carry

        lax.fori_loop(0, NB, body, 0)

    def place_faces(faces, land):
        faces[PREV0 : PREV0 + 6] = land[...]
        for d in range(6):
            def gather(b, carry):
                code = code_sm[b * 6 + d]
                x = faces[lax.shift_right_logical(code, 1)].astype(F32)
                near[b] = jnp.where(lane64 == lax.bitwise_and(code, 1), x, 0.0).astype(BF16)
                return carry

            lax.fori_loop(0, NB, gather, 0)

            def put(g, carry):
                rows = near[pl.ds(g * 4, 4)].reshape(4 * CH, 128)
                placed[d, pl.ds(g * 4, 4)] = dot(rows, place[d]).astype(BF16).reshape(4, CH, VOX)
                return carry

            lax.fori_loop(0, NB // 4, put, 0)

    def full_taps(b):
        for d in range(6):
            rows = pl.ds(CH * (d + 1), CH)
            taps[b, rows, :] = taps[b, rows, :] + placed[d, b]
        return taps[b]

    def octant_rows(src):
        for g in range(NB // 4):
            rows = src[4 * g : 4 * g + 4].reshape(4 * CH, VOX)
            sums = dot(rows, spread[...])
            for bb in range(4):
                part = sums[CH * bb : CH * bb + CH] * eye
                ysum[4 * g + bb : 4 * g + bb + 1, :] = jnp.sum(part, axis=0, keepdims=True)
        return ysum[...]

    def expand(g):
        parts = []
        for bb in range(4):
            row = yrow[pl.ds(4 * g + bb, 1), :]
            parts.append((row * eye).astype(BF16))
        return dot(jnp.concatenate(parts, axis=0), spread_t[...])

    make_faces(fine, faces1, pack1)
    pl.semaphore_wait(barrier, n_blk - 1 + n_slab - 1 + 4 + 2)
    copies1 = face_copies(land1, pack1, 0)
    for copy in copies1:
        copy.start()

    roll_taps(fine)
    ysum[...] = jnp.zeros((CELLS, VOX), F32)
    d_raised = dot(octant_rows(cot).astype(BF16), perm[...]).astype(BF16)
    d_lifted = dot_nt(d_raised, w_up[...]).astype(BF16)
    ident = (iota((CH, CH), 0) == iota((CH, CH), 1)).astype(BF16)
    w_fwd = dot_nt(ident, w_fine[...]).astype(BF16)
    for e in range(7):
        d = 0 if e == 0 else OPPOSITE[e - 1] + 1
        wbig[:, CH * e : CH * e + CH] = w_fine[CH * d : CH * d + CH, :].astype(F32)

    own_col = owner[...]
    cell_col = cell[...]
    eye16 = iota((CELLS, 128), 0) == iota((CELLS, 128), 1)
    own_row = jnp.sum(jnp.where(eye16, own_col, 0), axis=0, keepdims=True)
    same = (own_col == own_row) & (iota((CELLS, 128), 1) < iota((CELLS, 128), 0))
    slot = jnp.sum(same.astype(jnp.int32), axis=1, keepdims=True)
    ahead = lax.rem(own_col - me_b + n_blk, n_blk)
    start = jnp.where(iota((CELLS, 1), 0) < NB, ahead * 16 + 5 * slot, -1000)
    start_col = jnp.concatenate([start + j for j in range(5)] + [start * 0 - 1000] * 3, axis=0)
    packet_rows = n_blk * 16
    route_t = (iota((128, packet_rows), 1) == start_col).astype(BF16)
    eye128 = iota((128, 128), 0) == iota((128, 128), 1)
    start_row = jnp.sum(jnp.where(eye128, start_col, 0), axis=0, keepdims=True)
    route = (iota((packet_rows, 128), 0) == start_row).astype(BF16)
    cell_hot = ((iota((CELLS, 128), 1) == cell_col) & (iota((CELLS, 128), 0) < NB)).astype(F32)

    for copy in copies1:
        copy.wait_recv()
    place_faces(faces1, land1)

    def fine_forward(b, carry):
        value = dot(w_fwd, full_taps(b))
        pre[b] = value
        mid[b] = (fine[b].astype(F32) + value * jax.nn.sigmoid(value)).astype(BF16)
        return carry

    lax.fori_loop(0, NB, fine_forward, 0)
    means = dot((octant_rows(mid) * (1.0 / 64.0)).astype(BF16), perm[...]).astype(BF16)
    pooled = dot(means, w_down[...]).astype(BF16).astype(F32)
    lift32 = d_lifted.astype(F32)
    payload = jnp.concatenate(
        [pooled[:, :128], pooled[:, 128:], lift32[:, :128], lift32[:, 128:], cell_hot,
         jnp.zeros((48, 128), F32)], axis=0).astype(BF16)
    pk[...] = dot(route, payload).astype(BF16).reshape(n_blk, 16, 128)
    arr[0] = pk[0]

    def row_copy(src, dst, i, back, k):
        return pltpu.make_async_remote_copy(
            src_ref=src.at[i], dst_ref=dst.at[i], send_sem=asend.at[k], recv_sem=arecv.at[k],
            device_id=rel(n_blk - i if back else i), device_id_type=MESH,
        )

    def row_wait(buf, sem):
        pltpu.make_async_copy(buf.at[pl.ds(1, n_blk - 1)], buf.at[pl.ds(1, n_blk - 1)], sem).wait()

    def send_rows(src, dst, back, k):
        def body(i, carry):
            row_copy(src, dst, i, back, k).start()
            return carry

        lax.fori_loop(1, n_blk, body, 0)

    send_rows(pk, arr, False, 0)
    load_w.wait()
    row_wait(arr, arecv.at[0])

    arrived = arr[...].reshape(packet_rows, 128)
    wide = arrived.astype(F32)
    row_of = iota((packet_rows, 128), 0) % 16
    hot = jnp.where((row_of == 4) | (row_of == 9), wide, 0.0)
    hot_t = hot.T[:CELLS].astype(BF16)
    lined = jnp.concatenate([pltpu.roll(wide, 4 - j, 0) for j in range(4)], axis=1).astype(BF16)
    added = dot(hot_t, lined)
    hot16 = hot.astype(BF16)

    d_cout = cotc[...].astype(F32) + added[:, WID:]
    c_in = (latent[...].astype(F32) + added[:, :WID]).astype(BF16)

    def rim_copies(src, dst, k):
        return [
            pltpu.make_async_remote_copy(
                src_ref=src, dst_ref=dst.at[7 - i], send_sem=rsend.at[8 * k + i],
                recv_sem=rrecv.at[8 * k + 7 - i], device_id=near_id(a, b), device_id_type=MESH,
            )
            for i, (a, b) in enumerate(OFFSETS)
        ]

    def rim_tile(dst, own, a, b):
        if a == 0 and b == 0:
            return own.astype(F32)
        zz, yy = me_s + a, me_b + b
        inside = (zz >= 0) & (zz < n_slab) & (yy >= 0) & (yy < n_blk)
        tile = dst[OFFSETS.index((a, b))].astype(F32)
        return tile * jnp.where(inside, 1.0, 0.0)

    sub = iota((CELLS, WID), 0)

    def along_x(tile, step):
        if step == 0:
            return tile
        moved = pltpu.roll(tile, 1 if step == -1 else CELLS - 1, 0)
        return jnp.where(sub == (0 if step == -1 else CELLS - 1), 0.0, moved)

    rimsrc1[...] = c_in
    copies2 = rim_copies(rimsrc1, rim1, 0)
    for copy in copies2:
        copy.start()
    for copy in copies2:
        copy.wait_recv()
    acc = jnp.zeros((CELLS, WID), F32)
    for p in range(3):
        for q in range(3):
            tile = rim_tile(rim1, c_in, p - 1, q - 1)
            row = jnp.concatenate([along_x(tile, r - 1) for r in range(3)], axis=1).astype(BF16)
            base = (p * 3 + q) * 3 * WID
            acc = acc + dot(row, w_coarse[base : base + 3 * WID, :])
    sig = jax.nn.sigmoid(acc)
    c_out = (c_in.astype(F32) + acc * sig).astype(BF16)
    coarse_out[...] = c_out
    d_pre = (d_cout * (sig * (1.0 + acc * (1.0 - sig)))).astype(BF16)
    rimsrc2[...] = d_pre
    copies3 = rim_copies(rimsrc2, rim2, 1)
    for copy in copies3:
        copy.start()

    gsrc[...] = jnp.concatenate(
        [rim_tile(rim1, c_in, 0, q - 1) for q in range(3)] + [d_pre.astype(F32)], axis=1
    ).astype(BF16)
    own_gather = pltpu.make_async_copy(gsrc, gat.at[me_s], grecv)
    own_gather.start()
    gathers = [
        pltpu.make_async_remote_copy(
            src_ref=gsrc, dst_ref=gat.at[me_s], send_sem=gsend.at[i - 1], recv_sem=grecv,
            device_id=column(i), device_id_type=MESH,
        )
        for i in range(1, n_slab)
    ]
    for copy in gathers:
        copy.start()
    for copy in copies3:
        copy.wait_recv()
    acc = d_cout
    for p in range(3):
        for q in range(3):
            tile = rim_tile(rim2, d_pre, 1 - p, 1 - q)
            for r in range(3):
                base = ((p * 3 + q) * 3 + r) * WID
                moved = along_x(tile, 1 - r).astype(BF16)
                acc = acc + dot_nt(moved, w_coarse[base : base + WID, :])
    g_lat = acc.astype(BF16)
    grad_latent[...] = g_lat

    grid = jnp.concatenate([c_out.astype(F32), g_lat.astype(F32)], axis=1)
    grid = jnp.concatenate([grid, jnp.zeros((128 - CELLS, 2 * WID), F32)], axis=0).astype(BF16)
    picked = dot(hot16, grid)
    back = jnp.zeros((packet_rows, 128), F32)
    for j in range(4):
        back = back + pltpu.roll(picked[:, 128 * j : 128 * j + 128], packet_rows - 4 + j, 0)
    rpk[...] = back.astype(BF16).reshape(n_blk, 16, 128)
    rarr[0] = rpk[0]
    send_rows(rpk, rarr, True, 1)

    base_row = me_s * SLAB_ROWS + 144
    first_tap = base_row // WID - 3
    skew = base_row % WID
    pltpu.make_async_copy(gat, gat, grecv).wait()
    everything = gat[...].reshape(n_slab * CELLS, 4 * WID).astype(F32)
    for q in range(3):
        xq[q] = everything[:, q * WID : q * WID + WID].T.astype(BF16)
    d_all = everything[:, 3 * WID :].astype(BF16)
    from_row = iota((128, 128), 0)
    to_row = iota((128, 128), 1)

    def tap_rows(i, carry):
        t = first_tap + i
        inside = (t >= 0) & (t < 27)
        tc = jnp.clip(t, 0, 26)
        p, q, r = tc // 9, tc // 3 % 3, tc % 3
        shift = (from_row // 16 == to_row // 16 + p - 1) & (
            from_row % 16 == to_row % 16 + r - 1)
        moved = dot(xq[q], shift.astype(BF16)).astype(BF16)
        gbuf[pl.ds(pl.multiple_of(i * WID, WID), WID), :] = (
            dot(moved, d_all) * jnp.where(inside, 1.0 / math.sqrt(CELLS * total), 0.0)
        ).astype(BF16)
        return carry

    lax.fori_loop(0, 5, tap_rows, 0)

    def window_of(k):
        unit = (16 * skew + 503 * k) // 256
        return gbuf.at[pl.ds(pl.multiple_of(16 * unit, 16), 48)]

    def send_window(i, carry):
        pltpu.make_async_remote_copy(
            src_ref=window_of(lax.rem(me_b + i, n_blk)), dst_ref=wland.at[i],
            send_sem=vsend.at[0], recv_sem=vrecv.at[0], device_id=rel(i), device_id_type=MESH,
        ).start()
        return carry

    lax.fori_loop(1, n_blk, send_window, 0)
    row_wait(rarr, arecv.at[1])
    rows = dot(route_t, rarr[...].reshape(packet_rows, 128))
    lifted = jnp.concatenate([rows[0:16], rows[16:32]], axis=1).astype(BF16)
    d_pooled = jnp.concatenate([rows[32:48], rows[48:64]], axis=1).astype(BF16)

    d_means = dot_nt(d_pooled, w_down[...]) * (1.0 / 64.0)
    yrow[...] = dot(d_means.astype(BF16), perm_t[...])

    def fine_slope(g, carry):
        spreadv = expand(g).reshape(4, CH, VOX)
        for bb in range(4):
            b = 4 * g + bb
            d_mid = cot[b].astype(F32) + spreadv[bb]
            big[b] = d_mid
            value = pre[b]
            s = jax.nn.sigmoid(value)
            dpf[b] = (d_mid * (s * (1.0 + value * (1.0 - s)))).astype(BF16)
        return carry

    lax.fori_loop(0, NB // 4, fine_slope, 0)
    make_faces(dpf, faces2, pack2)
    copies4 = face_copies(land2, pack2, 1)
    for copy in copies4:
        copy.start()
    roll_taps(dpf)
    yrow[...] = dot(dot(lifted, w_up[...]).astype(BF16), perm_t[...])

    def fine_up(g, carry):
        spreadv = expand(g).reshape(4, CH, VOX)
        for bb in range(4):
            b = 4 * g + bb
            fine_out[b] = (mid[b].astype(F32) + spreadv[bb]).astype(BF16)
        return carry

    lax.fori_loop(0, NB // 4, fine_up, 0)
    rows_scale = 1.0 / math.sqrt(NB * total)
    twice = (iota((WID, VOX), 1) // 2 == iota((WID, VOX), 0)).astype(BF16)
    lifted2 = dot(lifted, twice).astype(BF16)
    up = jnp.where(iota((VOX, WID), 0) % 2 == 0, dot_tn(lifted2, d_raised[:, :WID]),
                   dot_tn(lifted2, d_raised[:, WID:])) * rows_scale
    down = dot_tn(means, d_pooled) * rows_scale
    ssrc[:, 0:16, :] = down.astype(BF16).reshape(n_blk, 16, WID)
    ssrc[:, 16:32, :] = up.astype(BF16).reshape(n_blk, 16, WID)

    def send_small(i, carry):
        pltpu.make_async_remote_copy(
            src_ref=ssrc.at[lax.rem(me_b + i, n_blk)], dst_ref=sland.at[i],
            send_sem=vsend.at[1], recv_sem=vrecv.at[1], device_id=rel(i), device_id_type=MESH,
        ).start()
        return carry

    lax.fori_loop(1, n_blk, send_small, 0)
    w_bwd = wbig[...].astype(BF16)
    gacc[...] = jnp.zeros((7 * CH, CH), F32)
    for copy in copies4:
        copy.wait_recv()
    place_faces(faces2, land2)

    def fine_backward(b, carry):
        t = full_taps(b)
        grad_fine[b] = (big[b] + dot(w_bwd, t)).astype(BF16)
        gacc[...] += dot_nt(t, fine[b])
        return carry

    lax.fori_loop(0, NB, fine_backward, 0)
    fine_bf = (gacc[...] * (1.0 / math.sqrt(NB * total * VOX))).astype(BF16)
    quarters = []
    for m in range(4):
        pick = (iota((16, CH), 1) == 4 * iota((16, CH), 0) + m).astype(BF16)
        quarters.append(dot_nt(pick, fine_bf))
    for e in range(7):
        d = 0 if e == 0 else OPPOSITE[e - 1] + 1
        fsrc[d] = jnp.concatenate(
            [quarter[:, CH * e : CH * e + CH] for quarter in quarters], axis=1).astype(BF16)
    fine_copies = [
        pltpu.make_async_remote_copy(
            src_ref=fsrc.at[t], dst_ref=fland.at[me_b], send_sem=usend.at[6 + t],
            recv_sem=vrecv.at[2], device_id=(me_s, t), device_id_type=MESH,
        )
        for t in range(7)
    ]
    for t in range(7):
        pl.when(me_b != t)(fine_copies[t].start)

    @pl.when(me_b < 7)
    def _():
        pltpu.make_async_copy(fsrc.at[lax.rem(me_b, 7)], fland.at[me_b], vrecv.at[2]).start()

    def unit_copies(kind, unit, base, slab, active):
        num = 256 * (unit - 2) - base
        low = (num + 502 + 503 * 8) // 503 - 8
        made = []
        for i in range(2):
            k = low + i
            begin = (base + 503 * k + 2560) // 256 - 10
            good = active & (k >= 0) & (k < n_blk) & (begin <= unit)
            mine = (me_s == slab) & (me_b == k)
            at = jnp.clip(unit - begin, 0, 2)
            away = pltpu.make_async_remote_copy(
                src_ref=units.at[kind], dst_ref=uland.at[at, me_s],
                send_sem=usend.at[2 * kind + i], recv_sem=urecv.at[at],
                device_id=(slab, jnp.clip(k, 0, n_blk - 1)), device_id_type=MESH,
            )
            home = pltpu.make_async_copy(units.at[kind], uland.at[at, me_s], urecv.at[at])
            pl.when(good & mine)(home.start)
            pl.when(good & jnp.logical_not(mine))(away.start)
            made.append((good & jnp.logical_not(mine), away))
        return made

    def window_wait(buf, sem):
        pltpu.make_async_copy(buf.at[pl.ds(1, n_blk - 1)], buf.at[pl.ds(1, n_blk - 1)], sem).wait()

    window_wait(sland, vrecv.at[1])
    both = lax.fori_loop(
        1, n_blk, lambda i, c: c + sland[i].astype(F32), ssrc[me_b].astype(F32)).astype(BF16)
    units[0] = both[0:16]
    units[1] = both[16:32]
    sent = unit_copies(0, me_b + 16, 2304, 0, me_b >= 0)
    sent = sent + unit_copies(1, me_b + 32, 288, n_slab - 1, me_b >= 0)

    window_wait(wland, vrecv.at[0])
    gsum[...] = lax.fori_loop(
        1, n_blk, lambda i, c: c + wland[i].astype(F32), window_of(me_b)[...].astype(F32))

    @pl.when(me_b < 7)
    def _():
        pltpu.make_async_copy(fland, fland, vrecv.at[2]).wait()
        units[2] = lax.fori_loop(
            1, n_blk, lambda i, c: c + fland[i].astype(F32), fland[0].astype(F32)).astype(BF16)

    sent = sent + unit_copies(2, me_b + 9, 2304, 0, me_b < 7)
    my_unit = (16 * skew + 503 * me_b) // 256
    for u in range(3):
        unit = my_unit + u
        small = ((me_s == 0) & (unit < 48)) | (
            (me_s == n_slab - 1) & (unit >= 32) & (unit < 64))

        @pl.when(small)
        def _():
            pltpu.make_async_copy(uland.at[u], uland.at[u], urecv.at[u]).wait()
            rows = slice(16 * u, 16 * u + 16)
            gsum[rows, :] += jnp.sum(uland[u].astype(F32), axis=0)

    down_by = skew + 503 * me_b // 16 - 16 * my_unit
    left_by = 16 * (503 * me_b % 16)
    value = pltpu.roll(gsum[...], lax.rem(48 - down_by, 48), 0)
    value = pltpu.roll(value, lax.rem(WID - left_by, WID), 1)
    below = pltpu.roll(value, 47, 0)
    grads_out[...] = jnp.where(
        iota((32, WID), 1) < WID - left_by, value[:32], below[:32])

    for copy in copies1 + copies4 + copies2 + copies3:
        copy.wait_send()
    row_wait(pk, asend.at[0])
    row_wait(rpk, asend.at[1])
    for copy in gathers:
        copy.wait_send()
    window_wait(wland, vsend.at[0])
    window_wait(sland, vsend.at[1])
    for t in range(7):
        pl.when(me_b != t)(fine_copies[t].wait_send)
    for good, copy in sent:
        pl.when(good)(copy.wait_send)


def fused(n_slab, n_blk, *operands):
    vmem = pl.BlockSpec(memory_space=pltpu.VMEM)
    smem = pl.BlockSpec(memory_space=pltpu.SMEM)
    hbm = pl.BlockSpec(memory_space=pl.ANY)
    sds = jax.ShapeDtypeStruct
    fine_like = sds((NB, CH, VOX), BF16)
    cells = sds((CELLS, WID), BF16)
    dma = pltpu.SemaphoreType.DMA
    rows = (n_blk, 16, 128)
    return pl.pallas_call(
        functools.partial(kernel, n_slab, n_blk),
        name="window",
        out_shape=(
            fine_like, cells, fine_like, cells, sds((32, WID), F32),
        ),
        in_specs=[vmem] * 7 + [hbm] + [smem] * 2 + [vmem] * 9,
        out_specs=(vmem,) * 5,
        scratch_shapes=[
            pltpu.VMEM((27 * WID, WID), BF16),
            pltpu.VMEM((SLOTS, CH, 128), BF16),
            pltpu.VMEM((SLOTS, CH, 128), BF16),
            pltpu.VMEM((2, 3, CH, 128), BF16),
            pltpu.VMEM((2, 3, CH, 128), BF16),
            pltpu.VMEM((NB, CH, 128), BF16),
            pltpu.VMEM((6, NB, CH, VOX), BF16),
            pltpu.VMEM((NB, 7 * CH, VOX), BF16),
            pltpu.VMEM((NB, CH, VOX), F32),
            pltpu.VMEM((NB, CH, VOX), BF16),
            pltpu.VMEM((NB, CH, VOX), BF16),
            pltpu.VMEM((NB, CH, VOX), F32),
            pltpu.VMEM((CELLS, VOX), F32),
            pltpu.VMEM((CELLS, VOX), F32),
            pltpu.VMEM((CH, 7 * CH), F32),
            pltpu.VMEM(rows, BF16),
            pltpu.VMEM(rows, BF16),
            pltpu.VMEM(rows, BF16),
            pltpu.VMEM(rows, BF16),
            pltpu.VMEM((8, CELLS, WID), BF16),
            pltpu.VMEM((8, CELLS, WID), BF16),
            pltpu.VMEM((CELLS, WID), BF16),
            pltpu.VMEM((CELLS, WID), BF16),
            pltpu.VMEM((7 * CH, CH), F32),
            pltpu.VMEM((6, CH, 128), BF16),
            pltpu.VMEM((6, CH, 128), BF16),
            pltpu.VMEM((CELLS, 4 * WID), BF16),
            pltpu.VMEM((n_slab, CELLS, 4 * WID), BF16),
            pltpu.VMEM((3, WID, 128), BF16),
            pltpu.VMEM((5 * WID, WID), BF16),
            pltpu.VMEM((n_blk, 48, WID), BF16),
            pltpu.VMEM((n_blk, 32, WID), BF16),
            pltpu.VMEM((n_blk, 32, WID), BF16),
            pltpu.VMEM((7, 16, WID), BF16),
            pltpu.VMEM((n_blk, 16, WID), BF16),
            pltpu.VMEM((3, 16, WID), BF16),
            pltpu.VMEM((3, n_slab, 16, WID), BF16),
            pltpu.VMEM((48, WID), F32),
            dma, dma((4,)), dma((4,)), dma((2,)), dma((2,)), dma((16,)), dma((16,)),
            dma((n_slab - 1,)), dma, dma((2,)), dma((3,)), dma((13,)), dma((3,)),
        ],
        compiler_params=pltpu.CompilerParams(
            collective_id=0, has_side_effects=True, vmem_limit_bytes=56 * 1024 * 1024
        ),
    )(*operands)


def face_routes(neighbors, position):
    opposite = jnp.array(OPPOSITE, jnp.int32)
    present = neighbors >= 0
    relation = jnp.where(present, neighbors // NB - position, 5).reshape(-1)
    lookup = (jnp.where(present, neighbors % NB, 0) * 6 + opposite[None, :]).reshape(-1)
    ids = jnp.arange(FACES, dtype=jnp.int32)
    send = []
    code = jnp.where(relation == 0, 2 * lookup, 2 * ZERO)
    for step, base in ((-1, PREV0), (1, NEXT0)):
        chosen = relation == step
        place = jnp.sum((chosen[None, :] & (ids[None, :] < ids[:, None])).astype(jnp.int32), axis=1)
        hit = chosen[None, :] & (place[None, :] == jnp.arange(FB, dtype=jnp.int32)[:, None])
        send.append(ZERO + jnp.sum(jnp.where(hit, ids[None, :] - ZERO, 0), axis=1))
        rank = jnp.sum(
            ((lookup[None, :] < lookup[:, None]) & chosen[None, :]).astype(jnp.int32), axis=1)
        code = jnp.where(chosen, 2 * base + rank, code)
    return jnp.concatenate(send), code


def shards(
    n_slab, n_blk,
    fine_in, latent, w_fine, w_down, w_coarse, w_up, neighbors, pool_owner, pool_cell, cot_fine,
    cot_coarse,
):
    position = lax.axis_index(("slab", "blk"))
    send, code = face_routes(neighbors, position)
    pad = lambda a: jnp.pad(a.reshape(NB, 1), ((0, CELLS - NB), (0, 0)))
    outs = fused(
        n_slab, n_blk,
        fine_in, cot_fine, latent.reshape(CELLS, WID), cot_coarse.reshape(CELLS, WID),
        w_fine, w_down, w_up, w_coarse, send, code, pad(pool_owner), pad(pool_cell), *tables())
    fine_out, c_out, grad_fine, g_lat, grads = outs
    weight_grads = grads.reshape(-1)[:SHARD]
    return (fine_out, c_out.reshape(latent.shape), grad_fine, g_lat.reshape(latent.shape),
            weight_grads)


def solution(mesh):
    n_slab, n_blk = mesh.shape["slab"], mesh.shape["blk"]
    return jax.shard_map(
        functools.partial(shards, n_slab, n_blk),
        mesh=mesh,
        in_specs=(
            P(("slab", "blk"), None, None), P("slab", "blk", None, None), P(), P(), P(), P(),
            P(("slab", "blk"), None), P(("slab", "blk"), None), P(("slab", "blk")),
            P(("slab", "blk"), None, None), P("slab", "blk", None, None),
        ),
        out_specs=(
            P(("slab", "blk"), None, None), P("slab", "blk", None, None),
            P(("slab", "blk"), None, None), P("slab", "blk", None, None), P(("slab", "blk")),
        ),
        check_vma=False,
    )
```

```python
import functools
import math

import jax
import jax.numpy as jnp
import numpy as np
from jax import lax
from jax.experimental import pallas as pl
from jax.experimental.pallas import tpu as pltpu
from jax.sharding import PartitionSpec as P

NB = 12
CH = 64
VOX = 512
WID = 256
CELLS = 16
FB = 6
OPPOSITE = (1, 0, 3, 2, 5, 4)
STRIDES = (64, 8, 1)
FACES = NB * 6
PREV0 = FACES
NEXT0 = FACES + 3
ZERO = FACES + 6
SLOTS = FACES + 7
OFFSETS = ((-1, -1), (-1, 0), (-1, 1), (0, -1), (0, 1), (1, -1), (1, 0), (1, 1))
SHARD = 8048
SLAB_ROWS = 1006
MESH = pl.DeviceIdType.MESH
F32 = jnp.float32
BF16 = jnp.bfloat16


def tables():
    voxel = np.arange(VOX)
    coords = (voxel // 64, voxel // 8 % 8, voxel % 8)
    octant = 4 * (coords[0] // 4) + 2 * (coords[1] // 4) + coords[2] // 4
    pull = np.zeros((VOX, 6 * 128), np.float32)
    place = np.zeros((6, 128, VOX), np.float32)
    keep = np.ones((6, 1, VOX), np.float32)
    for axis in range(3):
        others = [coords[other] for other in range(3) if other != axis]
        index = others[0] * 8 + others[1]
        for side in range(2):
            d = 2 * axis + side
            on = coords[axis] == 7 * side
            keep[d, 0, on] = 0.0
            for half in range(2):
                pull[voxel[on], 128 * d + 64 * half + index[on]] = 1.0
                place[d, 64 * half + index[on], voxel[on]] = 1.0
    spread = (octant[:, None] == np.arange(VOX)[None, :] // 64).astype(np.float32)
    major = np.arange(VOX)
    perm = np.zeros((VOX, VOX), np.float32)
    perm[major, 8 * (major % 64) + major // 64] = 1.0
    bf = lambda a: jnp.asarray(a, BF16)
    return bf(pull), bf(place.reshape(6 * 128, VOX)), jnp.asarray(keep), bf(spread), bf(spread.T), bf(perm), bf(perm.T)


def dot(a, b):
    return jnp.dot(a, b, preferred_element_type=F32)


def dot_nt(a, b):
    return lax.dot_general(a, b, (((1,), (1,)), ((), ())), preferred_element_type=F32)


def dot_tn(a, b):
    return lax.dot_general(a, b, (((0,), (0,)), ((), ())), preferred_element_type=F32)


def iota(shape, dim):
    return lax.broadcasted_iota(jnp.int32, shape, dim)


def kernel(
    n_slab, n_blk,
    fine_hbm, cot_hbm, latent, cotc, w_fwd, w_down_hbm, w_up_hbm, w_coarse_hbm, nbr, owner, cell,
    pull_hbm, place_hbm, keep, spread_hbm, spread_t_hbm, perm_hbm, perm_t_hbm,
    fine_out_hbm, coarse_out, grad_fine_hbm, grad_latent, grads_out,
    fine, cot, w_down, w_up, w_coarse, pull, place, spread, spread_t, perm, perm_t,
    fine_out, grad_fine, faces1, faces2, faces_wide, pack1, pack2, land1, land2, half, near, zall,
    taps, pre, mid, dpf, big, ysum, yrow, w_bwd, route_pk, arr_a, arr_b, pk_a, pk_b, rpk, rarr,
    rim1, rim2, rimsrc1, rimsrc2, gacc, xsrc, dsrc, upsrc, downsrc, xgat, dgat, upgat, downgat,
    dco, xq, gbuf, wland, fsrc, fland, unit_ref, uland, gsum, idx_v, idx_s,
    wsem, isem, osem, fsend, frecv, asend, arecv, rsend, rrecv, csend, crecv, vsend, vrecv,
    usend, urecv,
):
    me_s = lax.axis_index("slab")
    me_b = lax.axis_index("blk")
    total = n_slab * n_blk
    pos = me_s * n_blk + me_b
    after = lax.rem(pos + 1, total)
    before = lax.rem(pos + total - 1, total)
    rel = lambda i: (me_s, lax.rem(me_b + i, n_blk))
    column = lambda i: (lax.rem(me_s + i, n_slab), me_b)
    flat = lambda k: (lax.div(k, n_blk), lax.rem(k, n_blk))
    near_id = lambda a, b: (lax.rem(me_s + a + n_slab, n_slab), lax.rem(me_b + b + n_blk, n_blk))

    loads = {}
    for i, (name, src, dst) in enumerate((
        ("fine", fine_hbm, fine), ("pull", pull_hbm, pull), ("cot", cot_hbm, cot),
        ("spread", spread_hbm, spread), ("perm", perm_hbm, perm), ("place", place_hbm, place),
        ("up", w_up_hbm, w_up), ("down", w_down_hbm, w_down), ("coarse", w_coarse_hbm, w_coarse),
        ("perm_t", perm_t_hbm, perm_t), ("spread_t", spread_t_hbm, spread_t),
    )):
        loads[name] = pltpu.make_async_copy(src, dst, wsem.at[i])
        loads[name].start()

    barrier = pltpu.get_barrier_semaphore()

    def greet(i, carry):
        pl.semaphore_signal(barrier, inc=1, device_id=rel(i), device_id_type=MESH)
        return carry

    lax.fori_loop(1, n_blk, greet, 0)
    for i in range(1, n_slab):
        pl.semaphore_signal(barrier, inc=1, device_id=column(i), device_id_type=MESH)
    for a, b in OFFSETS:
        if a != 0 and b != 0:
            pl.semaphore_signal(barrier, inc=1, device_id=near_id(a, b), device_id_type=MESH)
    for k in (before, after):
        pl.semaphore_signal(barrier, inc=1, device_id=flat(k), device_id_type=MESH)

    lane1 = iota((1, 128), 1)
    lane = iota((128, 128), 1)
    sub = iota((128, 128), 0)
    diagonal = lane == sub
    ints = lambda m: m.astype(jnp.int32)
    as_col = lambda row: jnp.sum(jnp.where(diagonal, row, 0), axis=1, keepdims=True)
    down_sum = lambda m: jnp.sum(ints(m), axis=0, keepdims=True)
    number = jnp.full((1, 128), -1, jnp.int32)
    key = jnp.full((1, 128), 0, jnp.int32)
    for d in range(6):
        for b in range(NB):
            value = nbr[d, b]
            here = lane1 == d * NB + b
            number = jnp.where(here, value, number)
            key = jnp.where(here, value + NB * OPPOSITE[d], key)
    low = NB * pos
    code = jnp.full((1, 128), 2 * ZERO, jnp.int32)
    code = jnp.where((number >= low) & (number < low + NB), 2 * (key - low), code)
    for i, base in ((-1, PREV0), (1, NEXT0)):
        first = low + i * NB
        chosen = (number >= first) & (number < first + NB) & (number >= 0)
        ranked = jnp.where(chosen, key - first, 10000)
        rank = down_sum(as_col(ranked) < ranked)
        code = jnp.where(chosen, 2 * base + rank, code)
        mine = down_sum((as_col(ints(chosen)) == 1) & (sub < lane))
        order = as_col(jnp.where(chosen, mine, -1))
        sends = jnp.sum(jnp.where(order == lane, sub - ZERO, 0), axis=0, keepdims=True) + ZERO
        row = 1 if i == -1 else 2
        idx_v[row : row + 1, :] = jnp.clip(sends, 0, ZERO)
    idx_v[0:1, :] = jnp.clip(code, 0, 2 * ZERO)
    load_idx = pltpu.make_async_copy(idx_v, idx_s, isem)
    load_idx.start()

    lane64 = iota((CH, 128), 1) // 64
    half[0] = (lane64 == 0).astype(BF16)
    half[1] = (lane64 == 1).astype(BF16)
    eye = (iota((CH, VOX), 1) % 64 == iota((CH, VOX), 0)).astype(F32)

    def make_faces(src, faces, wide):
        faces[ZERO] = jnp.zeros((CH, 128), BF16)
        for g in range(NB // 4):
            rows = src[4 * g : 4 * g + 4].reshape(4 * CH, VOX)
            out = dot(rows, pull[...]).astype(BF16)
            for bb in range(4):
                b = 4 * g + bb
                for d in range(6):
                    part = out[CH * bb : CH * bb + CH, 128 * d : 128 * d + 128]
                    faces[d * NB + b] = part
                    if wide is not None:
                        wide[d, :, 128 * b : 128 * b + 128] = part

    def make_packs(faces, pack):
        for s in range(2):
            for q in range(3):
                first = faces[idx_s[1 + s, 2 * q]]
                second = faces[idx_s[1 + s, 2 * q + 1]]
                pack[s, q] = first * half[0] + second * half[1]

    def face_copies(land, pack, k):
        return [
            pltpu.make_async_remote_copy(
                src_ref=pack.at[0], dst_ref=land.at[pl.ds(3, 3)],
                send_sem=fsend.at[2 * k], recv_sem=frecv.at[2 * k],
                device_id=flat(before), device_id_type=MESH,
            ),
            pltpu.make_async_remote_copy(
                src_ref=pack.at[1], dst_ref=land.at[pl.ds(0, 3)],
                send_sem=fsend.at[2 * k + 1], recv_sem=frecv.at[2 * k + 1],
                device_id=flat(after), device_id_type=MESH,
            ),
        ]

    def roll_taps(src, b):
        x = src[b]
        wide = x.astype(F32)
        taps[b, 0:CH, :] = x
        for d in range(6):
            stride = STRIDES[d // 2]
            moved = pltpu.roll(wide, stride if d % 2 == 0 else VOX - stride, 1)
            taps[b, CH * (d + 1) : CH * (d + 2), :] = (moved * keep[d]).astype(BF16)

    def gather_faces(faces, land):
        faces[PREV0 : PREV0 + 6] = land[...]
        for d in range(6):
            for b in range(NB):
                at = idx_s[0, d * NB + b]
                near[d, :, 128 * b : 128 * b + 128] = (
                    faces[lax.shift_right_logical(at, 1)] * half[lax.bitwise_and(at, 1)])

    def weigh_faces(w):
        for d in range(6):
            z = dot(w[:, CH * (d + 1) : CH * (d + 2)], near[d]).astype(BF16)
            for b in range(NB):
                zall[b, :, 128 * d : 128 * d + 128] = z[:, 128 * b : 128 * b + 128]

    def placed(g):
        return dot(zall[pl.ds(4 * g, 4)].reshape(4 * CH, 6 * 128), place[...])

    def octant_rows(src):
        for g in range(NB // 4):
            rows = src[4 * g : 4 * g + 4].reshape(4 * CH, VOX)
            sums = dot(rows, spread[...])
            for bb in range(4):
                part = sums[CH * bb : CH * bb + CH] * eye
                ysum[4 * g + bb : 4 * g + bb + 1, :] = jnp.sum(part, axis=0, keepdims=True)
        return ysum[...]

    def expand(g):
        parts = []
        for bb in range(4):
            row = yrow[pl.ds(4 * g + bb, 1), :]
            parts.append((row * eye).astype(BF16))
        return dot(jnp.concatenate(parts, axis=0), spread_t[...])

    def row_wait(buf, sem):
        pltpu.make_async_copy(buf.at[pl.ds(1, n_blk - 1)], buf.at[pl.ds(1, n_blk - 1)], sem).wait()

    def send_rows(src, dst, back, k):
        def body(i, carry):
            pltpu.make_async_remote_copy(
                src_ref=src.at[i], dst_ref=dst.at[i], send_sem=asend.at[k], recv_sem=arecv.at[k],
                device_id=rel(n_blk - i if back else i), device_id_type=MESH,
            ).start()
            return carry

        lax.fori_loop(1, n_blk, body, 0)

    loads["fine"].wait()
    loads["pull"].wait()
    make_faces(fine, faces1, faces_wide)
    load_idx.wait()
    make_packs(faces1, pack1)
    pl.semaphore_wait(barrier, n_blk - 1 + n_slab - 1 + 4 + 2)
    copies1 = face_copies(land1, pack1, 0)
    for copy in copies1:
        copy.start()

    packet_rows = n_blk * 16
    sub16 = iota((CELLS, 128), 0)
    lane16 = iota((CELLS, 128), 1)
    own_col = jnp.full((CELLS, 128), 0, jnp.int32)
    cell_col = jnp.full((CELLS, 128), -1, jnp.int32)
    for b in range(NB):
        own_col = jnp.where(sub16 == b, owner[b], own_col)
        cell_col = jnp.where(sub16 == b, cell[b], cell_col)
    own_row = jnp.sum(jnp.where(sub16 == lane16, own_col, 0), axis=0, keepdims=True)
    same = (own_col == own_row) & (lane16 < sub16)
    slot = jnp.sum(same.astype(jnp.int32), axis=1, keepdims=True)
    gap = own_col[:, :1] - me_b
    ahead = jnp.where(gap < 0, gap + n_blk, gap)
    start = jnp.where(iota((CELLS, 1), 0) < NB, ahead * 16 + 5 * slot, -1000)
    start_col = jnp.concatenate([start + j for j in range(5)] + [start * 0 - 1000] * 3, axis=0)
    route_t = (iota((128, packet_rows), 1) == start_col).astype(BF16)
    start_row = jnp.sum(jnp.where(diagonal, start_col, 0), axis=0, keepdims=True)
    route_pk[...] = (iota((packet_rows, 128), 0) == start_row).astype(BF16)
    cell_hot = (lane16 == cell_col).astype(F32)

    def packets(rows, last):
        wide = rows.astype(F32)
        payload = jnp.concatenate(
            [wide[:, 128 * j : 128 * j + 128] for j in range(4)]
            + [last, jnp.zeros((48, 128), F32)], axis=0).astype(BF16)
        return dot(route_pk[...], payload).astype(BF16).reshape(n_blk, 16, 128)

    ysum[...] = jnp.zeros((CELLS, VOX), F32)
    loads["cot"].wait()
    loads["spread"].wait()
    loads["perm"].wait()
    d_raised = dot(octant_rows(cot).astype(BF16), perm[...]).astype(BF16)
    pk_a[...] = packets(d_raised, cell_hot)
    arr_a[0] = pk_a[0]
    send_rows(pk_a, arr_a, False, 0)

    for e in range(7):
        d = 0 if e == 0 else OPPOSITE[e - 1] + 1
        w_bwd[:, CH * e : CH * e + CH] = w_fwd[:, CH * d : CH * d + CH].astype(F32).T

    def own_forward(b, carry):
        roll_taps(fine, b)
        pre[b] = dot(w_fwd[...], taps[b])
        return carry

    lax.fori_loop(0, NB, own_forward, 0)
    loads["place"].wait()
    for copy in copies1:
        copy.wait_recv()
    gather_faces(faces1, land1)
    weigh_faces(w_fwd[...])

    def fine_forward(g, carry):
        more = placed(g).reshape(4, CH, VOX)
        for bb in range(4):
            b = 4 * g + bb
            value = pre[b] + more[bb]
            pre[b] = value
            mid[b] = (fine[b].astype(F32) + value * jax.nn.sigmoid(value)).astype(BF16)
        return carry

    lax.fori_loop(0, NB // 4, fine_forward, 0)
    means = dot((octant_rows(mid) * (1.0 / 64.0)).astype(BF16), perm[...]).astype(BF16)
    pk_b[...] = packets(means, jnp.zeros((CELLS, 128), F32))
    arr_b[0] = pk_b[0]
    send_rows(pk_b, arr_b, False, 1)

    def lined(arr):
        wide = arr[...].reshape(packet_rows, 128).astype(F32)
        return jnp.concatenate([pltpu.roll(wide, 4 - j, 0) for j in range(4)], axis=1).astype(BF16)

    def two_parts(x):
        high = x.astype(BF16)
        return high, (x - high.astype(F32)).astype(BF16)

    row_wait(arr_a, arecv.at[0])
    row_of = iota((packet_rows, 128), 0) % 16
    hot = jnp.where(
        (row_of == 4) | (row_of == 9), arr_a[...].reshape(packet_rows, 128).astype(F32), 0.0)
    hot_t = hot.T[:CELLS].astype(BF16)
    hot16 = hot.astype(BF16)
    raised_hi, raised_lo = two_parts(dot(hot_t, lined(arr_a)))
    loads["up"].wait()
    lift = dot_nt(jnp.concatenate([raised_hi, raised_lo], axis=0), w_up[...])
    dco[...] = cotc[...].astype(F32) + lift[:CELLS] + lift[CELLS:]
    loads["down"].wait()

    row_wait(arr_b, arecv.at[1])
    means_hi, means_lo = two_parts(dot(hot_t, lined(arr_b)))
    pooled = dot(jnp.concatenate([means_hi, means_lo], axis=0), w_down[...])
    c_in = (latent[...].astype(F32) + pooled[:CELLS] + pooled[CELLS:]).astype(BF16)

    def rim_copies(src, dst, k):
        return [
            pltpu.make_async_remote_copy(
                src_ref=src, dst_ref=dst.at[7 - i], send_sem=rsend.at[8 * k + i],
                recv_sem=rrecv.at[8 * k + 7 - i], device_id=near_id(a, b), device_id_type=MESH,
            )
            for i, (a, b) in enumerate(OFFSETS)
        ]

    def rim_tile(dst, own, a, b):
        if a == 0 and b == 0:
            return own.astype(F32)
        zz, yy = me_s + a, me_b + b
        inside = (zz >= 0) & (zz < n_slab) & (yy >= 0) & (yy < n_blk)
        tile = dst[OFFSETS.index((a, b))].astype(F32)
        return tile * jnp.where(inside, 1.0, 0.0)

    sub_x = iota((CELLS, WID), 0)

    def along_x(tile, step):
        if step == 0:
            return tile
        moved = pltpu.roll(tile, 1 if step == -1 else CELLS - 1, 0)
        return jnp.where(sub_x == (0 if step == -1 else CELLS - 1), 0.0, moved)

    def column_copies(src, dst, k):
        made = [
            pltpu.make_async_remote_copy(
                src_ref=src, dst_ref=dst.at[me_s], send_sem=csend.at[8 * k + i],
                recv_sem=crecv.at[k], device_id=column(i), device_id_type=MESH,
            )
            for i in range(1, n_slab)
        ]
        pltpu.make_async_copy(src, dst.at[me_s], crecv.at[k]).start()
        for copy in made:
            copy.start()
        return made

    def plane_copy(src, dst, slab, k):
        copy = pltpu.make_async_remote_copy(
            src_ref=src, dst_ref=dst.at[me_s], send_sem=csend.at[8 * k], recv_sem=crecv.at[k],
            device_id=(slab, me_b), device_id_type=MESH,
        )
        pl.when(me_s != slab)(copy.start)
        pl.when(me_s == slab)(pltpu.make_async_copy(src, dst.at[me_s], crecv.at[k]).start)
        return copy

    rimsrc1[...] = c_in
    copies2 = rim_copies(rimsrc1, rim1, 0)
    for copy in copies2:
        copy.start()
    loads["coarse"].wait()
    for copy in copies2:
        copy.wait_recv()
    xsrc[...] = jnp.concatenate(
        [rim_tile(rim1, c_in, 0, q - 1) for q in range(3)], axis=1).astype(BF16)
    x_sent = column_copies(xsrc, xgat, 0)
    acc = jnp.zeros((CELLS, WID), F32)
    for p in range(3):
        for q in range(3):
            tile = rim_tile(rim1, c_in, p - 1, q - 1)
            row = jnp.concatenate([along_x(tile, r - 1) for r in range(3)], axis=1).astype(BF16)
            base = (p * 3 + q) * 3 * WID
            acc = acc + dot(row, w_coarse[base : base + 3 * WID, :])
    sig = jax.nn.sigmoid(acc)
    d_pre = (dco[...] * (sig * (1.0 + acc * (1.0 - sig)))).astype(BF16)
    rimsrc2[...] = d_pre
    copies3 = rim_copies(rimsrc2, rim2, 1)
    for copy in copies3:
        copy.start()
    c_out = (c_in.astype(F32) + acc * sig).astype(BF16)
    coarse_out[...] = c_out
    dsrc[...] = d_pre
    d_sent = column_copies(dsrc, dgat, 1)
    upsrc[...] = jnp.concatenate([c_out.astype(F32), raised_hi.astype(F32)], axis=1).astype(BF16)
    up_sent = plane_copy(upsrc, upgat, n_slab - 1, 2)
    for copy in copies3:
        copy.wait_recv()
    acc = jnp.zeros((CELLS, WID), F32)
    for p in range(3):
        for q in range(3):
            tile = rim_tile(rim2, d_pre, 1 - p, 1 - q)
            for r in range(3):
                base = ((p * 3 + q) * 3 + r) * WID
                moved = along_x(tile, 1 - r).astype(BF16)
                acc = acc + dot_nt(moved, w_coarse[base : base + WID, :])
    g_lat = (dco[...] + acc).astype(BF16)
    grad_latent[...] = g_lat

    grid = jnp.concatenate([c_out.astype(F32), g_lat.astype(F32)], axis=1)
    grid = jnp.concatenate([grid, jnp.zeros((128 - CELLS, 2 * WID), F32)], axis=0).astype(BF16)
    picked = dot(hot16, grid)
    back = jnp.zeros((packet_rows, 128), F32)
    for j in range(4):
        back = back + pltpu.roll(picked[:, 128 * j : 128 * j + 128], packet_rows - 4 + j, 0)
    rpk[...] = back.astype(BF16).reshape(n_blk, 16, 128)
    rarr[0] = rpk[0]
    send_rows(rpk, rarr, True, 2)
    downsrc[...] = jnp.concatenate([g_lat.astype(F32), means_hi.astype(F32)], axis=1).astype(BF16)
    down_sent = plane_copy(downsrc, downgat, 0, 3)

    base_row = me_s * SLAB_ROWS + 144
    first_tap = base_row // WID - 3
    skew = base_row % WID
    pltpu.make_async_copy(xgat, xgat, crecv.at[0]).wait()
    everything = xgat[...].reshape(n_slab * CELLS, 3 * WID).astype(F32)
    for q in range(3):
        xq[q] = everything[:, q * WID : q * WID + WID].T.astype(BF16)
    pltpu.make_async_copy(dgat, dgat, crecv.at[1]).wait()
    d_all = dgat[...].reshape(n_slab * CELLS, WID)

    def tap_rows(i, carry):
        t = first_tap + i
        inside = (t >= 0) & (t < 27)
        tc = jnp.clip(t, 0, 26)
        p, q, r = tc // 9, tc // 3 % 3, tc % 3
        shift = (sub // 16 == lane // 16 + p - 1) & (sub % 16 == lane % 16 + r - 1)
        moved = dot(xq[q], shift.astype(BF16)).astype(BF16)
        gbuf[pl.ds(pl.multiple_of(i * WID, WID), WID), :] = (
            dot(moved, d_all) * jnp.where(inside, 1.0 / math.sqrt(CELLS * total), 0.0)
        ).astype(BF16)
        return carry

    lax.fori_loop(0, 5, tap_rows, 0)
    rows_scale = 1.0 / math.sqrt(NB * total)

    @pl.when(me_s == n_slab - 1)
    def _():
        pltpu.make_async_copy(upgat, upgat, crecv.at[2]).wait()
        left = upgat[:, :, :WID].reshape(n_slab * CELLS, WID)
        twice = (iota((WID, VOX), 1) // 2 == iota((WID, VOX), 0)).astype(BF16)
        left = dot(left, twice).astype(BF16)
        right = upgat[:, :, WID:].reshape(n_slab * CELLS, VOX)
        up = jnp.where(iota((VOX, WID), 0) % 2 == 0, dot_tn(left, right[:, :WID]),
                       dot_tn(left, right[:, WID:]))
        gbuf[512:1024, :] = (up * rows_scale).astype(BF16)

    @pl.when(me_s == 0)
    def _():
        pltpu.make_async_copy(downgat, downgat, crecv.at[3]).wait()
        left = downgat[:, :, WID:].reshape(n_slab * CELLS, VOX)
        right = downgat[:, :, :WID].reshape(n_slab * CELLS, WID)
        gbuf[256:768, :] = (dot_tn(left, right) * rows_scale).astype(BF16)

    def window_of(k):
        unit = (16 * skew + 503 * k) // 256
        return gbuf.at[pl.ds(pl.multiple_of(16 * unit, 16), 48)]

    def send_window(i, carry):
        pltpu.make_async_remote_copy(
            src_ref=window_of(lax.rem(me_b + i, n_blk)), dst_ref=wland.at[i],
            send_sem=vsend, recv_sem=vrecv.at[0], device_id=rel(i), device_id_type=MESH,
        ).start()
        return carry

    lax.fori_loop(1, n_blk, send_window, 0)
    loads["perm_t"].wait()
    loads["spread_t"].wait()
    row_wait(rarr, arecv.at[2])
    rows = dot(route_t, rarr[...].reshape(packet_rows, 128))
    lifted = jnp.concatenate([rows[0:16], rows[16:32]], axis=1).astype(BF16)
    d_pooled = jnp.concatenate([rows[32:48], rows[48:64]], axis=1).astype(BF16)

    d_means = dot_nt(d_pooled, w_down[...]) * (1.0 / 64.0)
    yrow[...] = dot(d_means.astype(BF16), perm_t[...])

    def fine_slope(g, carry):
        spreadv = expand(g).reshape(4, CH, VOX)
        for bb in range(4):
            b = 4 * g + bb
            d_mid = cot[b].astype(F32) + spreadv[bb]
            big[b] = d_mid
            value = pre[b]
            s = jax.nn.sigmoid(value)
            dpf[b] = (d_mid * (s * (1.0 + value * (1.0 - s)))).astype(BF16)
        return carry

    lax.fori_loop(0, NB // 4, fine_slope, 0)
    make_faces(dpf, faces2, None)
    make_packs(faces2, pack2)
    copies4 = face_copies(land2, pack2, 1)
    for copy in copies4:
        copy.start()
    w_back = w_bwd[...].astype(BF16)
    gacc[...] = jnp.zeros((7 * CH, CH), F32)

    def own_backward(b, carry):
        roll_taps(dpf, b)
        t = taps[b]
        big[b] += dot(w_back, t)
        gacc[...] += dot_nt(t, fine[b])
        return carry

    lax.fori_loop(0, NB, own_backward, 0)
    for copy in copies4:
        copy.wait_recv()
    gather_faces(faces2, land2)
    for e in range(6):
        gacc[CH * (e + 1) : CH * (e + 2), :] += dot_nt(near[e], faces_wide[e])
    fine_bf = (gacc[...] * (1.0 / math.sqrt(NB * total * VOX))).astype(BF16)
    quarters = []
    for m in range(4):
        pick = (iota((16, CH), 1) == 4 * iota((16, CH), 0) + m).astype(BF16)
        quarters.append(dot_nt(pick, fine_bf))
    for e in range(7):
        d = 0 if e == 0 else OPPOSITE[e - 1] + 1
        fsrc[d] = jnp.concatenate(
            [quarter[:, CH * e : CH * e + CH] for quarter in quarters], axis=1).astype(BF16)
    fine_copies = [
        pltpu.make_async_remote_copy(
            src_ref=fsrc.at[t], dst_ref=fland.at[me_b], send_sem=usend.at[2 + t],
            recv_sem=vrecv.at[1], device_id=(me_s, t), device_id_type=MESH,
        )
        for t in range(7)
    ]
    for t in range(7):
        pl.when(me_b != t)(fine_copies[t].start)

    @pl.when(me_b < 7)
    def _():
        pltpu.make_async_copy(fsrc.at[lax.rem(me_b, 7)], fland.at[me_b], vrecv.at[1]).start()

    weigh_faces(w_back)

    def fine_backward(g, carry):
        more = placed(g).reshape(4, CH, VOX)
        for bb in range(4):
            b = 4 * g + bb
            grad_fine[b] = (big[b] + more[bb]).astype(BF16)
        return carry

    lax.fori_loop(0, NB // 4, fine_backward, 0)
    store_grad = pltpu.make_async_copy(grad_fine, grad_fine_hbm, osem.at[0])
    store_grad.start()

    @pl.when(me_b < 7)
    def _():
        pltpu.make_async_copy(fland, fland, vrecv.at[1]).wait()
        unit_ref[...] = lax.fori_loop(
            1, n_blk, lambda i, c: c + fland[i].astype(F32), fland[0].astype(F32)).astype(BF16)

    unit = me_b + 9
    low = (256 * (unit - 2) - 2304 + 502 + 503 * 8) // 503 - 8
    sent = []
    for i in range(2):
        k = low + i
        begin = (2304 + 503 * k + 2560) // 256 - 10
        good = (me_b < 7) & (k >= 0) & (k < n_blk) & (begin <= unit)
        mine = (me_s == 0) & (me_b == k)
        at = jnp.clip(unit - begin, 0, 2)
        away = pltpu.make_async_remote_copy(
            src_ref=unit_ref, dst_ref=uland.at[at, me_s], send_sem=usend.at[i],
            recv_sem=urecv.at[at], device_id=(0, jnp.clip(k, 0, n_blk - 1)), device_id_type=MESH,
        )
        home = pltpu.make_async_copy(unit_ref, uland.at[at, me_s], urecv.at[at])
        pl.when(good & mine)(home.start)
        pl.when(good & jnp.logical_not(mine))(away.start)
        sent.append((good & jnp.logical_not(mine), away))

    yrow[...] = dot(dot(lifted, w_up[...]).astype(BF16), perm_t[...])

    def fine_up(g, carry):
        spreadv = expand(g).reshape(4, CH, VOX)
        for bb in range(4):
            b = 4 * g + bb
            fine_out[b] = (mid[b].astype(F32) + spreadv[bb]).astype(BF16)
        return carry

    lax.fori_loop(0, NB // 4, fine_up, 0)
    store_out = pltpu.make_async_copy(fine_out, fine_out_hbm, osem.at[1])
    store_out.start()
    row_wait(wland, vrecv.at[0])
    gsum[...] = lax.fori_loop(
        1, n_blk, lambda i, c: c + wland[i].astype(F32), window_of(me_b)[...].astype(F32))

    my_unit = (16 * skew + 503 * me_b) // 256
    for u in range(3):
        @pl.when((me_s == 0) & (my_unit + u < 16))
        def _():
            pltpu.make_async_copy(uland.at[u], uland.at[u], urecv.at[u]).wait()
            rows = slice(16 * u, 16 * u + 16)
            gsum[rows, :] += jnp.sum(uland[u].astype(F32), axis=0)

    down_by = skew + 503 * me_b // 16 - 16 * my_unit
    left_by = 16 * (503 * me_b % 16)
    value = pltpu.roll(gsum[...], lax.rem(48 - down_by, 48), 0)
    value = pltpu.roll(value, lax.rem(WID - left_by, WID), 1)
    below = pltpu.roll(value, 47, 0)
    grads_out[...] = jnp.where(
        iota((32, WID), 1) < WID - left_by, value[:32], below[:32])

    for copy in copies1 + copies4 + copies2 + copies3 + x_sent + d_sent:
        copy.wait_send()
    pl.when(me_s != n_slab - 1)(up_sent.wait_send)
    pl.when(me_s != 0)(down_sent.wait_send)
    row_wait(pk_a, asend.at[0])
    row_wait(pk_b, asend.at[1])
    row_wait(rpk, asend.at[2])
    row_wait(wland, vsend)
    for t in range(7):
        pl.when(me_b != t)(fine_copies[t].wait_send)
    for good, copy in sent:
        pl.when(good)(copy.wait_send)
    store_grad.wait()
    store_out.wait()


def fused(n_slab, n_blk, *operands):
    vmem = pl.BlockSpec(memory_space=pltpu.VMEM)
    smem = pl.BlockSpec(memory_space=pltpu.SMEM)
    hbm = pl.BlockSpec(memory_space=pl.ANY)
    sds = jax.ShapeDtypeStruct
    fine_like = sds((NB, CH, VOX), BF16)
    cells = sds((CELLS, WID), BF16)
    dma = pltpu.SemaphoreType.DMA
    rows = (n_blk, 16, 128)
    bf = lambda *shape: pltpu.VMEM(shape, BF16)
    f32 = lambda *shape: pltpu.VMEM(shape, F32)
    return pl.pallas_call(
        functools.partial(kernel, n_slab, n_blk),
        name="window",
        out_shape=(fine_like, cells, fine_like, cells, sds((32, WID), F32)),
        in_specs=[hbm] * 2 + [vmem] * 3 + [hbm] * 3 + [smem] * 3 + [hbm] * 2 + [vmem] + [hbm] * 4,
        out_specs=(hbm, vmem, hbm, vmem, vmem),
        scratch_shapes=[
            bf(NB, CH, VOX), bf(NB, CH, VOX), bf(VOX, WID), bf(WID, VOX), bf(27 * WID, WID),
            bf(VOX, 6 * 128), bf(6 * 128, VOX), bf(VOX, VOX), bf(VOX, VOX), bf(VOX, VOX),
            bf(VOX, VOX),
            bf(NB, CH, VOX), bf(NB, CH, VOX), bf(SLOTS, CH, 128), bf(SLOTS, CH, 128),
            bf(6, CH, NB * 128), bf(2, 3, CH, 128), bf(2, 3, CH, 128), bf(6, CH, 128),
            bf(6, CH, 128), bf(2, CH, 128), bf(6, CH, NB * 128), bf(NB, CH, 6 * 128),
            bf(NB, 7 * CH, VOX), f32(NB, CH, VOX), bf(NB, CH, VOX), bf(NB, CH, VOX),
            f32(NB, CH, VOX), f32(CELLS, VOX), f32(CELLS, VOX), f32(CH, 7 * CH),
            bf(n_blk * 16, 128), bf(*rows), bf(*rows), bf(*rows), bf(*rows), bf(*rows), bf(*rows),
            bf(8, CELLS, WID), bf(8, CELLS, WID), bf(CELLS, WID), bf(CELLS, WID), f32(7 * CH, CH),
            bf(CELLS, 3 * WID), bf(CELLS, WID), bf(CELLS, 3 * WID), bf(CELLS, 3 * WID),
            bf(n_slab, CELLS, 3 * WID), bf(n_slab, CELLS, WID), bf(n_slab, CELLS, 3 * WID),
            bf(n_slab, CELLS, 3 * WID),
            f32(CELLS, WID), bf(3, WID, 128), bf(5 * WID, WID), bf(n_blk, 48, WID), bf(7, 16, WID),
            bf(n_blk, 16, WID), bf(16, WID), bf(3, n_slab, 16, WID), f32(48, WID),
            pltpu.VMEM((8, 128), jnp.int32), pltpu.SMEM((8, 128), jnp.int32),
            dma((11,)), dma, dma((2,)), dma((4,)), dma((4,)), dma((3,)), dma((3,)), dma((16,)),
            dma((16,)), dma((32,)), dma((4,)), dma, dma((2,)), dma((9,)), dma((3,)),
        ],
        compiler_params=pltpu.CompilerParams(
            collective_id=0, has_side_effects=True, vmem_limit_bytes=56 * 1024 * 1024
        ),
    )(*operands)


def finish_kernel(fine_in, grad_in, coarse_in, latent_in, flat_in, fine_to, grad_to, coarse_to,
                  latent_to, flat_to):
    fine_to[...] = fine_in[...]
    grad_to[...] = grad_in[...]
    coarse_to[...] = coarse_in[...]
    latent_to[...] = latent_in[...]
    for r in range(SHARD // WID):
        flat_to[WID * r : WID * r + WID] = flat_in[r, :]
    rest = SHARD % WID
    flat_to[SHARD - rest : SHARD] = flat_in[SHARD // WID, :rest]


def finish(fine_out, coarse_out, grad_fine, grad_latent, flat):
    blocks = pl.BlockSpec((4, CH, VOX), lambda i: (i, 0, 0))
    cells = pl.BlockSpec((CELLS, WID), lambda i: (0, 0))
    like = lambda a: jax.ShapeDtypeStruct(a.shape, a.dtype)
    fine_out, grad_fine, coarse_out, grad_latent, flat = pl.pallas_call(
        finish_kernel,
        name="finish",
        grid=(NB // 4,),
        out_shape=(like(fine_out), like(grad_fine), like(coarse_out), like(grad_latent),
                   jax.ShapeDtypeStruct((SHARD,), F32)),
        in_specs=[blocks, blocks, cells, cells, pl.BlockSpec((32, WID), lambda i: (0, 0))],
        out_specs=(blocks, blocks, cells, cells, pl.BlockSpec((SHARD,), lambda i: (0,))),
    )(fine_out, grad_fine, coarse_out, grad_latent, flat)
    return fine_out, coarse_out, grad_fine, grad_latent, flat


def shards(
    n_slab, n_blk,
    fine_in, latent, w_fine, w_down, w_coarse, w_up, neighbors, pool_owner, pool_cell, cot_fine,
    cot_coarse,
):
    outs = fused(
        n_slab, n_blk,
        fine_in, cot_fine, latent.reshape(CELLS, WID), cot_coarse.reshape(CELLS, WID),
        w_fine.T, w_down, w_up, w_coarse, neighbors.T, pool_owner.reshape(NB), pool_cell,
        *tables())
    fine_out, c_out, grad_fine, g_lat, weight_grads = finish(*outs)
    return (fine_out, c_out.reshape(latent.shape), grad_fine, g_lat.reshape(latent.shape),
            weight_grads)


def solution(mesh):
    n_slab, n_blk = mesh.shape["slab"], mesh.shape["blk"]
    return jax.shard_map(
        functools.partial(shards, n_slab, n_blk),
        mesh=mesh,
        in_specs=(
            P(("slab", "blk"), None, None), P("slab", "blk", None, None), P(), P(), P(), P(),
            P(("slab", "blk"), None), P(("slab", "blk"), None), P(("slab", "blk")),
            P(("slab", "blk"), None, None), P("slab", "blk", None, None),
        ),
        out_specs=(
            P(("slab", "blk"), None, None), P("slab", "blk", None, None),
            P(("slab", "blk"), None, None), P("slab", "blk", None, None), P(("slab", "blk")),
        ),
        check_vma=False,
    )
```

```python
import functools
import math

import jax
import jax.numpy as jnp
import numpy as np
from jax import lax
from jax.experimental import pallas as pl
from jax.experimental.pallas import tpu as pltpu
from jax.sharding import PartitionSpec as P

NB = 12
CH = 64
VOX = 512
WID = 256
CELLS = 16
FB = 6
OPPOSITE = (1, 0, 3, 2, 5, 4)
STRIDES = (64, 8, 1)
FACES = NB * 6
PREV0 = FACES
NEXT0 = FACES + 3
ZERO = FACES + 6
SLOTS = FACES + 7
OFFSETS = ((-1, -1), (-1, 0), (-1, 1), (0, -1), (0, 1), (1, -1), (1, 0), (1, 1))
WIDE = tuple((a, b) for a in range(-2, 3) for b in range(-2, 3) if (a, b) != (0, 0))
BOXES = tuple((a, b) for a in range(-1, 2) for b in range(-1, 2))
SHARD = 8048
SLAB_ROWS = 1006
MESH = pl.DeviceIdType.MESH
F32 = jnp.float32
BF16 = jnp.bfloat16


def tables():
    voxel = np.arange(VOX)
    coords = (voxel // 64, voxel // 8 % 8, voxel % 8)
    octant = 4 * (coords[0] // 4) + 2 * (coords[1] // 4) + coords[2] // 4
    pull = np.zeros((VOX, 6 * 128), np.float32)
    place = np.zeros((6, 128, VOX), np.float32)
    keep = np.ones((6, 1, VOX), np.float32)
    for axis in range(3):
        others = [coords[other] for other in range(3) if other != axis]
        index = others[0] * 8 + others[1]
        for side in range(2):
            d = 2 * axis + side
            on = coords[axis] == 7 * side
            keep[d, 0, on] = 0.0
            for half in range(2):
                pull[voxel[on], 128 * d + 64 * half + index[on]] = 1.0
                place[d, 64 * half + index[on], voxel[on]] = 1.0
    spread = (octant[:, None] == np.arange(VOX)[None, :] // 64).astype(np.float32)
    major = np.arange(VOX)
    perm = np.zeros((VOX, VOX), np.float32)
    perm[major, 8 * (major % 64) + major // 64] = 1.0
    bf = lambda a: jnp.asarray(a, BF16)
    return bf(pull), bf(place.reshape(6 * 128, VOX)), jnp.asarray(keep), bf(spread), bf(spread.T), bf(perm), bf(perm.T)


def dot(a, b):
    return jnp.dot(a, b, preferred_element_type=F32)


def dot_nt(a, b):
    return lax.dot_general(a, b, (((1,), (1,)), ((), ())), preferred_element_type=F32)


def dot_tn(a, b):
    return lax.dot_general(a, b, (((0,), (0,)), ((), ())), preferred_element_type=F32)


def iota(shape, dim):
    return lax.broadcasted_iota(jnp.int32, shape, dim)


def kernel(
    n_slab, n_blk,
    fine_hbm, cot_hbm, latent, cotc, w_fwd, w_down_hbm, w_up_hbm, w_coarse_hbm, nbr, owner, cell,
    pull_hbm, place_hbm, keep, spread_hbm, spread_t_hbm, perm_hbm, perm_t_hbm,
    fine_out_hbm, coarse_out, grad_fine_hbm, grad_latent, grads_out,
    fine, cot, w_down, w_up, w_coarse, pull, place, spread, spread_t, perm, perm_t,
    fine_out, grad_fine, faces1, faces2, faces_wide, pack1, pack2, land1, land2, half, near1, near2, zall,
    own_taps, back_taps, pre, mid, dpf, big, ysum, yrow, w_bwd, route_pk, arr_a, arr_b, pk_a, pk_b, rpk, rarr,
    rim1, rim2, rimsrc1, rimsrc2, triple, boxes, d_box, d_all, gacc, xsrc, dsrc, upsrc, downsrc, xgat, dgat, upgat, downgat,
    dco, xq, gbuf, wland, fsrc, fland, unit_ref, uland, gsum, idx_v, idx_s,
    wsem, isem, osem, fsend, frecv, asend, arecv, rsend, rrecv, csend, crecv, vsend, vrecv,
    usend, urecv,
):
    me_s = lax.axis_index("slab")
    me_b = lax.axis_index("blk")
    total = n_slab * n_blk
    pos = me_s * n_blk + me_b
    after = lax.rem(pos + 1, total)
    before = lax.rem(pos + total - 1, total)
    rel = lambda i: (me_s, lax.rem(me_b + i, n_blk))
    column = lambda i: (lax.rem(me_s + i, n_slab), me_b)
    flat = lambda k: (lax.div(k, n_blk), lax.rem(k, n_blk))
    near_id = lambda a, b: (lax.rem(me_s + a + n_slab, n_slab), lax.rem(me_b + b + n_blk, n_blk))

    loads = {}
    for i, (name, src, dst) in enumerate((
        ("fine", fine_hbm, fine), ("pull", pull_hbm, pull), ("cot", cot_hbm, cot),
        ("spread", spread_hbm, spread), ("perm", perm_hbm, perm), ("place", place_hbm, place),
        ("up", w_up_hbm, w_up), ("down", w_down_hbm, w_down), ("coarse", w_coarse_hbm, w_coarse),
        ("perm_t", perm_t_hbm, perm_t), ("spread_t", spread_t_hbm, spread_t),
    )):
        loads[name] = pltpu.make_async_copy(src, dst, wsem.at[i])
        loads[name].start()

    barrier = pltpu.get_barrier_semaphore()

    def greet(i, carry):
        pl.semaphore_signal(barrier, inc=1, device_id=rel(i), device_id_type=MESH)
        return carry

    lax.fori_loop(1, n_blk, greet, 0)
    for i in range(1, n_slab):
        pl.semaphore_signal(barrier, inc=1, device_id=column(i), device_id_type=MESH)
    for a, b in WIDE:
        if a != 0 and b != 0:
            pl.semaphore_signal(barrier, inc=1, device_id=near_id(a, b), device_id_type=MESH)
    for k in (before, after):
        pl.semaphore_signal(barrier, inc=1, device_id=flat(k), device_id_type=MESH)

    lane1 = iota((1, 128), 1)
    lane = iota((128, 128), 1)
    sub = iota((128, 128), 0)
    diagonal = lane == sub
    ints = lambda m: m.astype(jnp.int32)
    as_col = lambda row: jnp.sum(jnp.where(diagonal, row, 0), axis=1, keepdims=True)
    down_sum = lambda m: jnp.sum(ints(m), axis=0, keepdims=True)
    number = jnp.full((1, 128), -1, jnp.int32)
    key = jnp.full((1, 128), 0, jnp.int32)
    for d in range(6):
        for b in range(NB):
            value = nbr[d, b]
            here = lane1 == d * NB + b
            number = jnp.where(here, value, number)
            key = jnp.where(here, value + NB * OPPOSITE[d], key)
    low = NB * pos
    code = jnp.full((1, 128), 2 * ZERO, jnp.int32)
    code = jnp.where((number >= low) & (number < low + NB), 2 * (key - low), code)
    for i, base in ((-1, PREV0), (1, NEXT0)):
        first = low + i * NB
        chosen = (number >= first) & (number < first + NB) & (number >= 0)
        ranked = jnp.where(chosen, key - first, 10000)
        rank = down_sum(as_col(ranked) < ranked)
        code = jnp.where(chosen, 2 * base + rank, code)
        mine = down_sum((as_col(ints(chosen)) == 1) & (sub < lane))
        order = as_col(jnp.where(chosen, mine, -1))
        sends = jnp.sum(jnp.where(order == lane, sub - ZERO, 0), axis=0, keepdims=True) + ZERO
        row = 1 if i == -1 else 2
        idx_v[row : row + 1, :] = jnp.clip(sends, 0, ZERO)
    idx_v[0:1, :] = jnp.clip(code, 0, 2 * ZERO)
    load_idx = pltpu.make_async_copy(idx_v, idx_s, isem)
    load_idx.start()

    lane64 = iota((CH, 128), 1) // 64
    half[0] = (lane64 == 0).astype(BF16)
    half[1] = (lane64 == 1).astype(BF16)
    eye = (iota((CH, VOX), 1) % 64 == iota((CH, VOX), 0)).astype(F32)

    def make_faces(src, faces, wide):
        faces[ZERO] = jnp.zeros((CH, 128), BF16)
        for g in range(NB // 4):
            rows = src[4 * g : 4 * g + 4].reshape(4 * CH, VOX)
            out = dot(rows, pull[...]).astype(BF16)
            for bb in range(4):
                b = 4 * g + bb
                for d in range(6):
                    part = out[CH * bb : CH * bb + CH, 128 * d : 128 * d + 128]
                    faces[d * NB + b] = part
                    if wide is not None:
                        wide[d, :, 128 * b : 128 * b + 128] = part

    def make_packs(faces, pack):
        for s in range(2):
            for q in range(3):
                first = faces[idx_s[1 + s, 2 * q]]
                second = faces[idx_s[1 + s, 2 * q + 1]]
                pack[s, q] = first * half[0] + second * half[1]

    def face_copies(land, pack, k):
        return [
            pltpu.make_async_remote_copy(
                src_ref=pack.at[0], dst_ref=land.at[pl.ds(3, 3)],
                send_sem=fsend.at[2 * k], recv_sem=frecv.at[2 * k],
                device_id=flat(before), device_id_type=MESH,
            ),
            pltpu.make_async_remote_copy(
                src_ref=pack.at[1], dst_ref=land.at[pl.ds(0, 3)],
                send_sem=fsend.at[2 * k + 1], recv_sem=frecv.at[2 * k + 1],
                device_id=flat(after), device_id_type=MESH,
            ),
        ]

    def roll_taps(src, b, taps, at):
        x = src[b]
        wide = x.astype(F32)
        taps[at, 0:CH, :] = x
        for d in range(6):
            stride = STRIDES[d // 2]
            moved = pltpu.roll(wide, stride if d % 2 == 0 else VOX - stride, 1)
            taps[at, CH * (d + 1) : CH * (d + 2), :] = (moved * keep[d]).astype(BF16)

    def gather_faces(faces, land, near):
        faces[PREV0 : PREV0 + 6] = land[...]
        for d in range(6):
            for b in range(NB):
                at = idx_s[0, d * NB + b]
                near[d, :, 128 * b : 128 * b + 128] = (
                    faces[lax.shift_right_logical(at, 1)] * half[lax.bitwise_and(at, 1)])

    def weigh_faces(w, near):
        for d in range(6):
            z = dot(w[:, CH * (d + 1) : CH * (d + 2)], near[d]).astype(BF16)
            for b in range(NB):
                zall[b, :, 128 * d : 128 * d + 128] = z[:, 128 * b : 128 * b + 128]

    def placed(g):
        return dot(zall[pl.ds(4 * g, 4)].reshape(4 * CH, 6 * 128), place[...])

    def octant_rows(src):
        for g in range(NB // 4):
            rows = src[4 * g : 4 * g + 4].reshape(4 * CH, VOX)
            sums = dot(rows, spread[...])
            for bb in range(4):
                part = sums[CH * bb : CH * bb + CH] * eye
                ysum[4 * g + bb : 4 * g + bb + 1, :] = jnp.sum(part, axis=0, keepdims=True)
        return ysum[...]

    def expand(g):
        parts = []
        for bb in range(4):
            row = yrow[pl.ds(4 * g + bb, 1), :]
            parts.append((row * eye).astype(BF16))
        return dot(jnp.concatenate(parts, axis=0), spread_t[...])

    def row_wait(buf, sem, count=n_blk - 1):
        pltpu.make_async_copy(buf.at[pl.ds(1, count)], buf.at[pl.ds(1, count)], sem).wait()

    def send_rows(src, dst, back, k):
        def body(i, carry):
            pltpu.make_async_remote_copy(
                src_ref=src.at[i], dst_ref=dst.at[i], send_sem=asend.at[k], recv_sem=arecv.at[k],
                device_id=rel(n_blk - i if back else i), device_id_type=MESH,
            ).start()
            return carry

        lax.fori_loop(1, n_blk, body, 0)

    loads["fine"].wait()
    loads["pull"].wait()
    make_faces(fine, faces1, None)
    load_idx.wait()
    make_packs(faces1, pack1)
    pl.semaphore_wait(barrier, n_blk - 1 + n_slab - 1 + 16 + 2)
    copies1 = face_copies(land1, pack1, 0)
    for copy in copies1:
        copy.start()

    packet_rows = n_blk * 16
    sub16 = iota((CELLS, 128), 0)
    lane16 = iota((CELLS, 128), 1)
    own_col = jnp.full((CELLS, 128), 0, jnp.int32)
    cell_col = jnp.full((CELLS, 128), -1, jnp.int32)
    for b in range(NB):
        own_col = jnp.where(sub16 == b, owner[b], own_col)
        cell_col = jnp.where(sub16 == b, cell[b], cell_col)
    own_row = jnp.sum(jnp.where(sub16 == lane16, own_col, 0), axis=0, keepdims=True)
    same = (own_col == own_row) & (lane16 < sub16)
    slot = jnp.sum(same.astype(jnp.int32), axis=1, keepdims=True)
    gap = own_col[:, :1] - me_b
    ahead = jnp.where(gap < 0, gap + n_blk, gap)
    start = jnp.where(iota((CELLS, 1), 0) < NB, ahead * 16 + 5 * slot, -1000)
    start_col = jnp.concatenate([start + j for j in range(5)] + [start * 0 - 1000] * 3, axis=0)
    route_t = (iota((128, packet_rows), 1) == start_col).astype(BF16)
    start_row = jnp.sum(jnp.where(diagonal, start_col, 0), axis=0, keepdims=True)
    route_pk[...] = (iota((packet_rows, 128), 0) == start_row).astype(BF16)
    cell_hot = (lane16 == cell_col).astype(F32)

    def packets(rows, last):
        wide = rows.astype(F32)
        payload = jnp.concatenate(
            [wide[:, 128 * j : 128 * j + 128] for j in range(4)]
            + [last, jnp.zeros((48, 128), F32)], axis=0).astype(BF16)
        return dot(route_pk[...], payload).astype(BF16).reshape(n_blk, 16, 128)

    ysum[...] = jnp.zeros((CELLS, VOX), F32)
    loads["cot"].wait()
    loads["spread"].wait()
    loads["perm"].wait()
    d_raised = dot(octant_rows(cot).astype(BF16), perm[...]).astype(BF16)
    pk_a[...] = packets(d_raised, cell_hot)
    arr_a[0] = pk_a[0]
    send_rows(pk_a, arr_a, False, 0)

    for e in range(7):
        d = 0 if e == 0 else OPPOSITE[e - 1] + 1
        w_bwd[:, CH * e : CH * e + CH] = w_fwd[:, CH * d : CH * d + CH].astype(F32).T

    def own_forward(b, carry):
        roll_taps(fine, b, own_taps, b)
        pre[b] = dot(w_fwd[...], own_taps[b])
        return carry

    lax.fori_loop(0, NB, own_forward, 0)
    loads["place"].wait()
    for copy in copies1:
        copy.wait_recv()
    gather_faces(faces1, land1, near1)
    weigh_faces(w_fwd[...], near1)

    def fine_forward(g, carry):
        more = placed(g).reshape(4, CH, VOX)
        for bb in range(4):
            b = 4 * g + bb
            value = pre[b] + more[bb]
            pre[b] = value
            mid[b] = (fine[b].astype(F32) + value * jax.nn.sigmoid(value)).astype(BF16)
        return carry

    lax.fori_loop(0, NB // 4, fine_forward, 0)
    means = dot((octant_rows(mid) * (1.0 / 64.0)).astype(BF16), perm[...]).astype(BF16)
    pk_b[...] = packets(means, jnp.zeros((CELLS, 128), F32))
    arr_b[0] = pk_b[0]
    send_rows(pk_b, arr_b, False, 1)

    def lined(arr):
        wide = arr[...].reshape(packet_rows, 128).astype(F32)
        return jnp.concatenate([pltpu.roll(wide, 4 - j, 0) for j in range(4)], axis=1).astype(BF16)

    def two_parts(x):
        high = x.astype(BF16)
        return high, (x - high.astype(F32)).astype(BF16)

    row_wait(arr_a, arecv.at[0])
    row_of = iota((packet_rows, 128), 0) % 16
    hot = jnp.where(
        (row_of == 4) | (row_of == 9), arr_a[...].reshape(packet_rows, 128).astype(F32), 0.0)
    hot_t = hot.T[:CELLS].astype(BF16)
    hot16 = hot.astype(BF16)
    raised_hi, raised_lo = two_parts(dot(hot_t, lined(arr_a)))
    loads["up"].wait()
    lift = dot_nt(jnp.concatenate([raised_hi, raised_lo], axis=0), w_up[...])
    dco[...] = cotc[...].astype(F32) + lift[:CELLS] + lift[CELLS:]
    loads["down"].wait()

    def rim_copies(src, dst, offsets, base):
        count = len(offsets)
        return [
            pltpu.make_async_remote_copy(
                src_ref=src, dst_ref=dst.at[count - 1 - i], send_sem=rsend.at[base + i],
                recv_sem=rrecv.at[base + count - 1 - i], device_id=near_id(a, b),
                device_id_type=MESH,
            )
            for i, (a, b) in enumerate(offsets)
        ]

    def inside(a, b):
        zz, yy = me_s + a, me_b + b
        within = (zz >= 0) & (zz < n_slab) & (yy >= 0) & (yy < n_blk)
        return jnp.where(within, 1.0, 0.0)

    rimsrc2[...] = dco[...]
    copies3 = rim_copies(rimsrc2, rim2, OFFSETS, len(WIDE))
    for copy in copies3:
        copy.start()
    row_wait(arr_b, arecv.at[1])
    means_hi, means_lo = two_parts(dot(hot_t, lined(arr_b)))
    pooled = dot(jnp.concatenate([means_hi, means_lo], axis=0), w_down[...])
    c_in = (latent[...].astype(F32) + pooled[:CELLS] + pooled[CELLS:]).astype(BF16)

    sub_x = iota((CELLS, WID), 0)

    def along_x(tile, step):
        if step == 0:
            return tile
        moved = pltpu.roll(tile, 1 if step == -1 else CELLS - 1, 0)
        return jnp.where(sub_x == (0 if step == -1 else CELLS - 1), 0.0, moved)

    def column_copies(src, dst, k):
        made = [
            pltpu.make_async_remote_copy(
                src_ref=src, dst_ref=dst.at[me_s], send_sem=csend.at[8 * k + i],
                recv_sem=crecv.at[k], device_id=column(i), device_id_type=MESH,
            )
            for i in range(1, n_slab)
        ]
        pltpu.make_async_copy(src, dst.at[me_s], crecv.at[k]).start()
        for copy in made:
            copy.start()
        return made

    odd = lax.rem(me_b, 2)
    even_row = me_b - odd

    def plane_copies(src, dst, slab, k):
        made = []
        for i in range(2):
            k_blk = even_row + i
            copy = pltpu.make_async_remote_copy(
                src_ref=src, dst_ref=dst.at[odd, me_s], send_sem=csend.at[8 * k + i],
                recv_sem=crecv.at[k], device_id=(slab, k_blk), device_id_type=MESH,
            )
            mine = (me_s == slab) & (me_b == k_blk)
            pl.when(jnp.logical_not(mine))(copy.start)
            pl.when(mine)(pltpu.make_async_copy(src, dst.at[odd, me_s], crecv.at[k]).start)
            made.append((jnp.logical_not(mine), copy))
        return made

    rimsrc1[...] = c_in
    copies2 = rim_copies(rimsrc1, rim1, WIDE, 0)
    for copy in copies2:
        copy.start()
    loads["coarse"].wait()
    for copy in copies2:
        copy.wait_recv()

    for a in range(-2, 3):
        for b in range(-2, 3):
            if a == 0 and b == 0:
                tile = c_in.astype(F32)
            else:
                tile = rim1[WIDE.index((a, b))].astype(F32) * inside(a, b)
            triple[5 * (a + 2) + b + 2] = jnp.concatenate(
                [along_x(tile, r - 1) for r in range(3)], axis=1).astype(BF16)
    plane_row = lambda b: triple[12 + b, :, WID : 2 * WID]
    xsrc[...] = jnp.concatenate(
        [jnp.where(odd == 0, plane_row(i - 1).astype(F32), plane_row(i - 2).astype(F32))
         for i in range(4)], axis=1).astype(BF16)
    x_sent = column_copies(xsrc, xgat, 0)
    acc = jnp.zeros((9 * CELLS, WID), F32)
    for p in range(3):
        for q in range(3):
            rows = jnp.concatenate(
                [triple[5 * (a + p + 1) + b + q + 1] for a, b in BOXES], axis=0)
            base = (p * 3 + q) * 3 * WID
            acc = acc + dot(rows, w_coarse[base : base + 3 * WID, :])
    boxes[...] = acc
    for copy in copies3:
        copy.wait_recv()
    for i, (a, b) in enumerate(BOXES):
        value = boxes[CELLS * i : CELLS * i + CELLS]
        sig = jax.nn.sigmoid(value)
        slope = sig * (1.0 + value * (1.0 - sig))
        if i == 4:
            d_pre = dco[...] * slope
            c_out = (c_in.astype(F32) + value * sig).astype(BF16)
        else:
            d_pre = rim2[OFFSETS.index((a, b))] * slope * inside(a, b)
        d_box[i] = d_pre.astype(BF16).astype(F32)
    coarse_out[...] = c_out
    dsrc[...] = jnp.concatenate(
        [jnp.where(odd == 0, d_box[4 + i], d_box[3 + i]) for i in range(2)], axis=1).astype(BF16)
    d_sent = column_copies(dsrc, dgat, 1)
    upsrc[...] = jnp.concatenate([c_out.astype(F32), raised_hi.astype(F32)], axis=1).astype(BF16)
    up_sent = plane_copies(upsrc, upgat, n_slab - 1, 2)
    acc = jnp.zeros((CELLS, WID), F32)
    for p in range(3):
        for q in range(3):
            tile = d_box[3 * (2 - p) + 2 - q]
            for r in range(3):
                base = ((p * 3 + q) * 3 + r) * WID
                moved = along_x(tile, 1 - r).astype(BF16)
                acc = acc + dot_nt(moved, w_coarse[base : base + WID, :])
    g_lat = (dco[...] + acc).astype(BF16)
    grad_latent[...] = g_lat

    grid = jnp.concatenate([c_out.astype(F32), g_lat.astype(F32)], axis=1)
    grid = jnp.concatenate([grid, jnp.zeros((128 - CELLS, 2 * WID), F32)], axis=0).astype(BF16)
    picked = dot(hot16, grid)
    back = jnp.zeros((packet_rows, 128), F32)
    for j in range(4):
        back = back + pltpu.roll(picked[:, 128 * j : 128 * j + 128], packet_rows - 4 + j, 0)
    rpk[...] = back.astype(BF16).reshape(n_blk, 16, 128)
    rarr[0] = rpk[0]
    send_rows(rpk, rarr, True, 2)
    downsrc[...] = jnp.concatenate([g_lat.astype(F32), means_hi.astype(F32)], axis=1).astype(BF16)
    down_sent = plane_copies(downsrc, downgat, 0, 3)

    base_row = me_s * SLAB_ROWS + 144
    first_tap = base_row // WID - 3
    skew = base_row % WID
    pltpu.make_async_copy(xgat, xgat, crecv.at[0]).wait()
    everything = xgat[...].reshape(n_slab * CELLS, 4 * WID).astype(F32)
    for q in range(4):
        xq[q] = everything[:, q * WID : q * WID + WID].T.astype(BF16)
    pltpu.make_async_copy(dgat, dgat, crecv.at[1]).wait()
    pair = dgat[...].reshape(n_slab * CELLS, 2 * WID)
    d_all[...] = jnp.concatenate([pair[:, :WID], pair[:, WID:]], axis=0)

    def tap_rows(i, carry):
        t = first_tap + i
        good = (t >= 0) & (t < 27)
        tc = jnp.clip(t, 0, 26)
        p, q, r = tc // 9, tc // 3 % 3, tc % 3
        shift = ((sub // 16 == lane // 16 + p - 1) & (sub % 16 == lane % 16 + r - 1)).astype(BF16)
        moved = jnp.concatenate([dot(xq[q], shift), dot(xq[q + 1], shift)], axis=1).astype(BF16)
        gbuf[pl.ds(pl.multiple_of(i * WID, WID), WID), :] = (
            dot(moved, d_all[...]) * jnp.where(good, 1.0 / math.sqrt(CELLS * total), 0.0)
        ).astype(BF16)
        return carry

    lax.fori_loop(0, 5, tap_rows, 0)
    rows_scale = 1.0 / math.sqrt(NB * total)

    @pl.when(me_s == n_slab - 1)
    def _():
        pltpu.make_async_copy(upgat, upgat, crecv.at[2]).wait()
        left = upgat[:, :, :, :WID].reshape(2 * n_slab * CELLS, WID)
        twice = (iota((WID, VOX), 1) // 2 == iota((WID, VOX), 0)).astype(BF16)
        left = dot(left, twice).astype(BF16)
        right = upgat[:, :, :, WID:].reshape(2 * n_slab * CELLS, VOX)
        up = jnp.where(iota((VOX, WID), 0) % 2 == 0, dot_tn(left, right[:, :WID]),
                       dot_tn(left, right[:, WID:]))
        gbuf[512:1024, :] = (up * rows_scale).astype(BF16)

    @pl.when(me_s == 0)
    def _():
        pltpu.make_async_copy(downgat, downgat, crecv.at[3]).wait()
        left = downgat[:, :, :, WID:].reshape(2 * n_slab * CELLS, VOX)
        right = downgat[:, :, :, :WID].reshape(2 * n_slab * CELLS, WID)
        gbuf[256:768, :] = (dot_tn(left, right) * rows_scale).astype(BF16)

    def window_of(k):
        unit = (16 * skew + 503 * k) // 256
        return gbuf.at[pl.ds(pl.multiple_of(16 * unit, 16), 48)]

    def send_window(i, carry):
        pltpu.make_async_remote_copy(
            src_ref=window_of(lax.rem(me_b + 2 * i, n_blk)), dst_ref=wland.at[i],
            send_sem=vsend, recv_sem=vrecv.at[0], device_id=rel(2 * i), device_id_type=MESH,
        ).start()
        return carry

    lax.fori_loop(1, n_blk // 2, send_window, 0)
    loads["perm_t"].wait()
    loads["spread_t"].wait()
    row_wait(rarr, arecv.at[2])
    rows = dot(route_t, rarr[...].reshape(packet_rows, 128))
    lifted = jnp.concatenate([rows[0:16], rows[16:32]], axis=1).astype(BF16)
    d_pooled = jnp.concatenate([rows[32:48], rows[48:64]], axis=1).astype(BF16)

    d_means = dot_nt(d_pooled, w_down[...]) * (1.0 / 64.0)
    yrow[...] = dot(d_means.astype(BF16), perm_t[...])

    def fine_slope(g, carry):
        spreadv = expand(g).reshape(4, CH, VOX)
        for bb in range(4):
            b = 4 * g + bb
            d_mid = cot[b].astype(F32) + spreadv[bb]
            big[b] = d_mid
            value = pre[b]
            s = jax.nn.sigmoid(value)
            dpf[b] = (d_mid * (s * (1.0 + value * (1.0 - s)))).astype(BF16)
        return carry

    lax.fori_loop(0, NB // 4, fine_slope, 0)
    make_faces(dpf, faces2, faces_wide)
    make_packs(faces2, pack2)
    copies4 = face_copies(land2, pack2, 1)
    for copy in copies4:
        copy.start()
    w_back = w_bwd[...].astype(BF16)
    gacc[...] = jnp.zeros((7 * CH, CH), F32)

    def weight_grad(b, carry):
        gacc[...] += dot_nt(own_taps[b], dpf[b])
        return carry

    lax.fori_loop(0, NB, weight_grad, 0)
    for d in range(6):
        gacc[CH * (d + 1) : CH * (d + 2), :] += dot_nt(near1[d], faces_wide[d])
    fine_bf = (gacc[...] * (1.0 / math.sqrt(NB * total * VOX))).astype(BF16)
    row_to = iota((7 * 16, 7 * CH), 0)
    quarters = []
    for m in range(4):
        pick = iota((7 * 16, 7 * CH), 1) == 64 * (row_to // 16) + 4 * (row_to % 16) + m
        quarters.append(dot(pick.astype(BF16), fine_bf))
    fsrc[...] = jnp.concatenate(quarters, axis=1).astype(BF16).reshape(7, 16, WID)
    fine_copies = [
        pltpu.make_async_remote_copy(
            src_ref=fsrc.at[t], dst_ref=fland.at[me_b], send_sem=usend.at[2 + t],
            recv_sem=vrecv.at[1], device_id=(me_s, t), device_id_type=MESH,
        )
        for t in range(7)
    ]
    for t in range(7):
        pl.when(me_b != t)(fine_copies[t].start)

    @pl.when(me_b < 7)
    def _():
        pltpu.make_async_copy(fsrc.at[lax.rem(me_b, 7)], fland.at[me_b], vrecv.at[1]).start()

    def own_backward(b, carry):
        buf = lax.rem(b, 2)
        roll_taps(dpf, b, back_taps, buf)
        big[b] += dot(w_back, back_taps[buf])
        return carry

    lax.fori_loop(0, NB, own_backward, 0)
    for copy in copies4:
        copy.wait_recv()
    gather_faces(faces2, land2, near2)
    weigh_faces(w_back, near2)

    def fine_backward(g, carry):
        more = placed(g).reshape(4, CH, VOX)
        for bb in range(4):
            b = 4 * g + bb
            grad_fine[b] = (big[b] + more[bb]).astype(BF16)
        return carry

    lax.fori_loop(0, NB // 4, fine_backward, 0)
    store_grad = pltpu.make_async_copy(grad_fine, grad_fine_hbm, osem.at[0])
    store_grad.start()

    @pl.when(me_b < 7)
    def _():
        pltpu.make_async_copy(fland, fland, vrecv.at[1]).wait()
        unit_ref[...] = lax.fori_loop(
            1, n_blk, lambda i, c: c + fland[i].astype(F32), fland[0].astype(F32)).astype(BF16)

    unit = me_b + 9
    low = (256 * (unit - 2) - 2304 + 502 + 503 * 8) // 503 - 8
    sent = []
    for i in range(2):
        k = low + i
        begin = (2304 + 503 * k + 2560) // 256 - 10
        good = (me_b < 7) & (k >= 0) & (k < n_blk) & (begin <= unit)
        mine = (me_s == 0) & (me_b == k)
        at = jnp.clip(unit - begin, 0, 2)
        away = pltpu.make_async_remote_copy(
            src_ref=unit_ref, dst_ref=uland.at[at, me_s], send_sem=usend.at[i],
            recv_sem=urecv.at[at], device_id=(0, jnp.clip(k, 0, n_blk - 1)), device_id_type=MESH,
        )
        home = pltpu.make_async_copy(unit_ref, uland.at[at, me_s], urecv.at[at])
        pl.when(good & mine)(home.start)
        pl.when(good & jnp.logical_not(mine))(away.start)
        sent.append((good & jnp.logical_not(mine), away))

    yrow[...] = dot(dot(lifted, w_up[...]).astype(BF16), perm_t[...])

    def fine_up(g, carry):
        spreadv = expand(g).reshape(4, CH, VOX)
        for bb in range(4):
            b = 4 * g + bb
            fine_out[b] = (mid[b].astype(F32) + spreadv[bb]).astype(BF16)
        return carry

    lax.fori_loop(0, NB // 4, fine_up, 0)
    store_out = pltpu.make_async_copy(fine_out, fine_out_hbm, osem.at[1])
    store_out.start()
    row_wait(wland, vrecv.at[0], n_blk // 2 - 1)
    gsum[...] = lax.fori_loop(
        1, n_blk // 2, lambda i, c: c + wland[i].astype(F32), window_of(me_b)[...].astype(F32))

    my_unit = (16 * skew + 503 * me_b) // 256
    for u in range(3):
        @pl.when((me_s == 0) & (my_unit + u < 16))
        def _():
            pltpu.make_async_copy(uland.at[u], uland.at[u], urecv.at[u]).wait()
            rows = slice(16 * u, 16 * u + 16)
            gsum[rows, :] += jnp.sum(uland[u].astype(F32), axis=0)

    down_by = skew + 503 * me_b // 16 - 16 * my_unit
    left_by = 16 * (503 * me_b % 16)
    value = pltpu.roll(gsum[...], lax.rem(48 - down_by, 48), 0)
    value = pltpu.roll(value, lax.rem(WID - left_by, WID), 1)
    below = pltpu.roll(value, 47, 0)
    grads_out[...] = jnp.where(
        iota((32, WID), 1) < WID - left_by, value[:32], below[:32])

    for copy in copies1 + copies4 + copies2 + copies3 + x_sent + d_sent:
        copy.wait_send()
    for good, copy in up_sent + down_sent:
        pl.when(good)(copy.wait_send)
    row_wait(pk_a, asend.at[0])
    row_wait(pk_b, asend.at[1])
    row_wait(rpk, asend.at[2])
    row_wait(wland, vsend, n_blk // 2 - 1)
    for t in range(7):
        pl.when(me_b != t)(fine_copies[t].wait_send)
    for good, copy in sent:
        pl.when(good)(copy.wait_send)
    store_grad.wait()
    store_out.wait()


def fused(n_slab, n_blk, *operands):
    vmem = pl.BlockSpec(memory_space=pltpu.VMEM)
    smem = pl.BlockSpec(memory_space=pltpu.SMEM)
    hbm = pl.BlockSpec(memory_space=pl.ANY)
    sds = jax.ShapeDtypeStruct
    fine_like = sds((NB, CH, VOX), BF16)
    cells = sds((CELLS, WID), BF16)
    dma = pltpu.SemaphoreType.DMA
    rows = (n_blk, 16, 128)
    bf = lambda *shape: pltpu.VMEM(shape, BF16)
    f32 = lambda *shape: pltpu.VMEM(shape, F32)
    return pl.pallas_call(
        functools.partial(kernel, n_slab, n_blk),
        name="window",
        out_shape=(fine_like, cells, fine_like, cells, sds((32, WID), F32)),
        in_specs=[hbm] * 2 + [vmem] * 3 + [hbm] * 3 + [smem] * 3 + [hbm] * 2 + [vmem] + [hbm] * 4,
        out_specs=(hbm, vmem, hbm, vmem, vmem),
        scratch_shapes=[
            bf(NB, CH, VOX), bf(NB, CH, VOX), bf(VOX, WID), bf(WID, VOX), bf(27 * WID, WID),
            bf(VOX, 6 * 128), bf(6 * 128, VOX), bf(VOX, VOX), bf(VOX, VOX), bf(VOX, VOX),
            bf(VOX, VOX),
            bf(NB, CH, VOX), bf(NB, CH, VOX), bf(SLOTS, CH, 128), bf(SLOTS, CH, 128),
            bf(6, CH, NB * 128), bf(2, 3, CH, 128), bf(2, 3, CH, 128), bf(6, CH, 128),
            bf(6, CH, 128), bf(2, CH, 128), bf(6, CH, NB * 128), bf(6, CH, NB * 128),
            bf(NB, CH, 6 * 128), bf(NB, 7 * CH, VOX), bf(2, 7 * CH, VOX), f32(NB, CH, VOX), bf(NB, CH, VOX), bf(NB, CH, VOX),
            f32(NB, CH, VOX), f32(CELLS, VOX), f32(CELLS, VOX), f32(CH, 7 * CH),
            bf(n_blk * 16, 128), bf(*rows), bf(*rows), bf(*rows), bf(*rows), bf(*rows), bf(*rows),
            bf(24, CELLS, WID), f32(8, CELLS, WID), bf(CELLS, WID), f32(CELLS, WID),
            bf(25, CELLS, 3 * WID), f32(9 * CELLS, WID), f32(9, CELLS, WID), bf(WID, WID),
            f32(7 * CH, CH),
            bf(CELLS, 4 * WID), bf(CELLS, 2 * WID), bf(CELLS, 3 * WID), bf(CELLS, 3 * WID),
            bf(n_slab, CELLS, 4 * WID), bf(n_slab, CELLS, 2 * WID), bf(2, n_slab, CELLS, 3 * WID),
            bf(2, n_slab, CELLS, 3 * WID),
            f32(CELLS, WID), bf(4, WID, 128), bf(5 * WID, WID), bf(n_blk // 2, 48, WID), bf(7, 16, WID),
            bf(n_blk, 16, WID), bf(16, WID), bf(3, n_slab, 16, WID), f32(48, WID),
            pltpu.VMEM((8, 128), jnp.int32), pltpu.SMEM((8, 128), jnp.int32),
            dma((11,)), dma, dma((2,)), dma((4,)), dma((4,)), dma((3,)), dma((3,)), dma((32,)),
            dma((32,)), dma((32,)), dma((4,)), dma, dma((2,)), dma((9,)), dma((3,)),
        ],
        compiler_params=pltpu.CompilerParams(
            collective_id=0, has_side_effects=True, vmem_limit_bytes=56 * 1024 * 1024
        ),
    )(*operands)


def finish_kernel(fine_in, grad_in, coarse_in, latent_in, flat_in, fine_to, grad_to, coarse_to,
                  latent_to, flat_to, held, in_sems, out_sems):
    takes, gives = [], []
    for i, (src, dst) in enumerate(((fine_in, fine_to), (grad_in, grad_to))):
        for j in range(4):
            rows = pl.ds(3 * j, 3)
            n = 4 * i + j
            takes.append(pltpu.make_async_copy(src.at[rows], held.at[i, rows], in_sems.at[n]))
            gives.append(pltpu.make_async_copy(held.at[i, rows], dst.at[rows], out_sems.at[n]))
    for copy in takes:
        copy.start()
    coarse_to[...] = coarse_in[...]
    latent_to[...] = latent_in[...]
    for r in range(SHARD // WID):
        flat_to[WID * r : WID * r + WID] = flat_in[r, :]
    rest = SHARD % WID
    flat_to[SHARD - rest : SHARD] = flat_in[SHARD // WID, :rest]
    for take, give in zip(takes, gives):
        take.wait()
        give.start()
    for give in gives:
        give.wait()


def finish(fine_out, coarse_out, grad_fine, grad_latent, flat):
    hbm = pl.BlockSpec(memory_space=pl.ANY)
    vmem = pl.BlockSpec(memory_space=pltpu.VMEM)
    like = lambda a: jax.ShapeDtypeStruct(a.shape, a.dtype)
    fine_out, grad_fine, coarse_out, grad_latent, flat = pl.pallas_call(
        finish_kernel,
        name="finish",
        out_shape=(like(fine_out), like(grad_fine), like(coarse_out), like(grad_latent),
                   jax.ShapeDtypeStruct((SHARD,), F32)),
        in_specs=[hbm, hbm, vmem, vmem, vmem],
        out_specs=(hbm, hbm, vmem, vmem, vmem),
        scratch_shapes=[pltpu.VMEM((2, NB, CH, VOX), BF16), pltpu.SemaphoreType.DMA((8,)),
                        pltpu.SemaphoreType.DMA((8,))],
    )(fine_out, grad_fine, coarse_out, grad_latent, flat)
    return fine_out, coarse_out, grad_fine, grad_latent, flat


def shards(
    n_slab, n_blk,
    fine_in, latent, w_fine, w_down, w_coarse, w_up, neighbors, pool_owner, pool_cell, cot_fine,
    cot_coarse,
):
    outs = fused(
        n_slab, n_blk,
        fine_in, cot_fine, latent.reshape(CELLS, WID), cot_coarse.reshape(CELLS, WID),
        w_fine.T, w_down, w_up, w_coarse, neighbors.T, pool_owner.reshape(NB), pool_cell,
        *tables())
    fine_out, c_out, grad_fine, g_lat, weight_grads = finish(*outs)
    return (fine_out, c_out.reshape(latent.shape), grad_fine, g_lat.reshape(latent.shape),
            weight_grads)


def solution(mesh):
    n_slab, n_blk = mesh.shape["slab"], mesh.shape["blk"]
    return jax.shard_map(
        functools.partial(shards, n_slab, n_blk),
        mesh=mesh,
        in_specs=(
            P(("slab", "blk"), None, None), P("slab", "blk", None, None), P(), P(), P(), P(),
            P(("slab", "blk"), None), P(("slab", "blk"), None), P(("slab", "blk")),
            P(("slab", "blk"), None, None), P("slab", "blk", None, None),
        ),
        out_specs=(
            P(("slab", "blk"), None, None), P("slab", "blk", None, None),
            P(("slab", "blk"), None, None), P("slab", "blk", None, None), P(("slab", "blk")),
        ),
        check_vma=False,
    )
```

```python
import functools
import math

import jax
import jax.numpy as jnp
import numpy as np
from jax import lax
from jax.experimental import pallas as pl
from jax.experimental.pallas import tpu as pltpu
from jax.sharding import PartitionSpec as P

NB = 12
CH = 64
VOX = 512
WID = 256
CELLS = 16
FB = 6
OPPOSITE = (1, 0, 3, 2, 5, 4)
STRIDES = (64, 8, 1)
FACES = NB * 6
PREV0 = FACES
NEXT0 = FACES + 3
ZERO = FACES + 6
SLOTS = FACES + 7
OFFSETS = ((-1, -1), (-1, 0), (-1, 1), (0, -1), (0, 1), (1, -1), (1, 0), (1, 1))
WIDE = tuple((a, b) for a in range(-2, 3) for b in range(-2, 3) if (a, b) != (0, 0))
BOXES = tuple((a, b) for a in range(-1, 2) for b in range(-1, 2))
SHARD = 8048
FAR_FIRST = sorted(range(1, 32), key=lambda i: -(min(i // 8, 4 - i // 8) + min(i % 8, 8 - i % 8)))
SLAB_ROWS = 1006
MESH = pl.DeviceIdType.MESH
F32 = jnp.float32
BF16 = jnp.bfloat16


def tables():
    voxel = np.arange(VOX)
    coords = (voxel // 64, voxel // 8 % 8, voxel % 8)
    octant = 4 * (coords[0] // 4) + 2 * (coords[1] // 4) + coords[2] // 4
    pull = np.zeros((VOX, 6 * 128), np.float32)
    place = np.zeros((6, 128, VOX), np.float32)
    keep = np.ones((6, 1, VOX), np.float32)
    for axis in range(3):
        others = [coords[other] for other in range(3) if other != axis]
        index = others[0] * 8 + others[1]
        for side in range(2):
            d = 2 * axis + side
            on = coords[axis] == 7 * side
            keep[d, 0, on] = 0.0
            for half in range(2):
                pull[voxel[on], 128 * d + 64 * half + index[on]] = 1.0
                place[d, 64 * half + index[on], voxel[on]] = 1.0
    spread = (octant[:, None] == np.arange(VOX)[None, :] // 64).astype(np.float32)
    major = np.arange(VOX)
    perm = np.zeros((VOX, VOX), np.float32)
    perm[major, 8 * (major % 64) + major // 64] = 1.0
    bf = lambda a: jnp.asarray(a, BF16)
    return bf(pull), bf(place.reshape(6 * 128, VOX)), jnp.asarray(keep), bf(spread), bf(spread.T), bf(perm), bf(perm.T)


def dot(a, b):
    return jnp.dot(a, b, preferred_element_type=F32)


def dot_nt(a, b):
    return lax.dot_general(a, b, (((1,), (1,)), ((), ())), preferred_element_type=F32)


def dot_tn(a, b):
    return lax.dot_general(a, b, (((0,), (0,)), ((), ())), preferred_element_type=F32)


def iota(shape, dim):
    return lax.broadcasted_iota(jnp.int32, shape, dim)


def kernel(
    n_slab, n_blk,
    fine_hbm, cot_hbm, latent, cotc, w_fwd, w_down_hbm, w_up_hbm, w_coarse_hbm, nbr, owner, cell,
    pull_hbm, place_hbm, keep, spread_hbm, spread_t_hbm, perm_hbm, perm_t_hbm,
    fine_out_hbm, coarse_out, grad_fine_hbm, grad_latent, grads_out,
    fine, cot, w_down, w_up, w_coarse, pull, place, spread, spread_t, perm, perm_t,
    fine_out, grad_fine, faces1, faces2, faces_wide, pack1, pack2, land1, land2, half, near1, near2, zall,
    own_taps, back_taps, pre, mid, dpf, big, ysum, yrow, w_bwd, route_pk, arr_a, arr_b, pk_a, pk_b, rpk, rarr,
    rim1, rim2, rimsrc1, rimsrc2, triple, boxes, d_box, d_all, gacc, xsrc, dsrc, upsrc, downsrc, xgat, dgat, upgat, downgat,
    dco, xq, gbuf, wland, fsrc, fland, unit_ref, uland, gsum, idx_v, idx_s,
    wsem, isem, osem, fsend, frecv, asend, arecv, rsend, rrecv, csend, crecv, vsend, vrecv,
    usend, urecv,
):
    me_s = lax.axis_index("slab")
    me_b = lax.axis_index("blk")
    total = n_slab * n_blk
    pos = me_s * n_blk + me_b
    after = lax.rem(pos + 1, total)
    before = lax.rem(pos + total - 1, total)
    rel = lambda i: (me_s, lax.rem(me_b + i, n_blk))
    me_x, me_z = lax.div(me_b, 8), lax.rem(me_b, 8)
    apart = lambda dx, dz: (me_s, lax.rem(me_x + dx, 4) * 8 + lax.rem(me_z + dz, 8))
    column = lambda i: (lax.rem(me_s + i, n_slab), me_b)
    flat = lambda k: (lax.div(k, n_blk), lax.rem(k, n_blk))
    near_id = lambda a, b: (lax.rem(me_s + a + n_slab, n_slab), lax.rem(me_b + b + n_blk, n_blk))

    loads = {}

    def load(name, src, dst, parts=1):
        size = src.shape[0] // parts
        loads[name] = []
        for i in range(parts):
            rows = pl.ds(size * i, size)
            copy = pltpu.make_async_copy(src.at[rows], dst.at[rows], wsem.at[len(taken)])
            taken.append(name)
            loads[name].append(copy)
            copy.start()

    def loaded(name):
        for copy in loads[name]:
            copy.wait()

    taken = []
    load("fine", fine_hbm, fine, 3)
    load("pull", pull_hbm, pull, 2)

    barrier = pltpu.get_barrier_semaphore()

    def greet(i, carry):
        pl.semaphore_signal(barrier, inc=1, device_id=rel(i), device_id_type=MESH)
        return carry

    lax.fori_loop(1, n_blk, greet, 0)
    for i in range(1, n_slab):
        pl.semaphore_signal(barrier, inc=1, device_id=column(i), device_id_type=MESH)
    for a, b in WIDE:
        if a != 0 and b != 0:
            pl.semaphore_signal(barrier, inc=1, device_id=near_id(a, b), device_id_type=MESH)
    for k in (before, after):
        pl.semaphore_signal(barrier, inc=1, device_id=flat(k), device_id_type=MESH)

    lane1 = iota((1, 128), 1)
    lane = iota((128, 128), 1)
    sub = iota((128, 128), 0)
    diagonal = lane == sub
    ints = lambda m: m.astype(jnp.int32)
    as_col = lambda row: jnp.sum(jnp.where(diagonal, row, 0), axis=1, keepdims=True)
    down_sum = lambda m: jnp.sum(ints(m), axis=0, keepdims=True)
    number = jnp.full((1, 128), -1, jnp.int32)
    key = jnp.full((1, 128), 0, jnp.int32)
    for d in range(6):
        for b in range(NB):
            value = nbr[d, b]
            here = lane1 == d * NB + b
            number = jnp.where(here, value, number)
            key = jnp.where(here, value + NB * OPPOSITE[d], key)
    low = NB * pos
    code = jnp.full((1, 128), 2 * ZERO, jnp.int32)
    code = jnp.where((number >= low) & (number < low + NB), 2 * (key - low), code)
    for i, base in ((-1, PREV0), (1, NEXT0)):
        first = low + i * NB
        chosen = (number >= first) & (number < first + NB) & (number >= 0)
        ranked = jnp.where(chosen, key - first, 10000)
        rank = down_sum(as_col(ranked) < ranked)
        code = jnp.where(chosen, 2 * base + rank, code)
        mine = down_sum((as_col(ints(chosen)) == 1) & (sub < lane))
        order = as_col(jnp.where(chosen, mine, -1))
        sends = jnp.sum(jnp.where(order == lane, sub - ZERO, 0), axis=0, keepdims=True) + ZERO
        row = 1 if i == -1 else 2
        idx_v[row : row + 1, :] = jnp.clip(sends, 0, ZERO)
    idx_v[0:1, :] = jnp.clip(code, 0, 2 * ZERO)
    load_idx = pltpu.make_async_copy(idx_v, idx_s, isem)
    load_idx.start()

    lane64 = iota((CH, 128), 1) // 64
    half[0] = (lane64 == 0).astype(BF16)
    half[1] = (lane64 == 1).astype(BF16)
    eye = (iota((CH, VOX), 1) % 64 == iota((CH, VOX), 0)).astype(F32)

    def make_faces(src, faces, wide):
        faces[ZERO] = jnp.zeros((CH, 128), BF16)
        for g in range(NB // 4):
            rows = src[4 * g : 4 * g + 4].reshape(4 * CH, VOX)
            out = dot(rows, pull[...]).astype(BF16)
            for bb in range(4):
                b = 4 * g + bb
                for d in range(6):
                    part = out[CH * bb : CH * bb + CH, 128 * d : 128 * d + 128]
                    faces[d * NB + b] = part
                    if wide is not None:
                        wide[d, :, 128 * b : 128 * b + 128] = part

    def make_packs(faces, pack):
        for s in range(2):
            for q in range(3):
                first = faces[idx_s[1 + s, 2 * q]]
                second = faces[idx_s[1 + s, 2 * q + 1]]
                pack[s, q] = first * half[0] + second * half[1]

    def face_copies(land, pack, k):
        return [
            pltpu.make_async_remote_copy(
                src_ref=pack.at[0], dst_ref=land.at[pl.ds(3, 3)],
                send_sem=fsend.at[2 * k], recv_sem=frecv.at[2 * k],
                device_id=flat(before), device_id_type=MESH,
            ),
            pltpu.make_async_remote_copy(
                src_ref=pack.at[1], dst_ref=land.at[pl.ds(0, 3)],
                send_sem=fsend.at[2 * k + 1], recv_sem=frecv.at[2 * k + 1],
                device_id=flat(after), device_id_type=MESH,
            ),
        ]

    def roll_taps(src, b, taps, at):
        x = src[b]
        taps[at, 0:CH, :] = x
        for d in range(6):
            stride = STRIDES[d // 2]
            moved = pltpu.roll(x, stride if d % 2 == 0 else VOX - stride, 1)
            taps[at, CH * (d + 1) : CH * (d + 2), :] = moved * keep[d].astype(BF16)

    def gather_faces(faces, land, near):
        faces[PREV0 : PREV0 + 6] = land[...]
        for d in range(6):
            for b in range(NB):
                at = idx_s[0, d * NB + b]
                near[d, :, 128 * b : 128 * b + 128] = (
                    faces[lax.shift_right_logical(at, 1)] * half[lax.bitwise_and(at, 1)])

    def weigh_faces(w, near):
        for d in range(6):
            z = dot(w[:, CH * (d + 1) : CH * (d + 2)], near[d]).astype(BF16)
            for b in range(NB):
                zall[b, :, 128 * d : 128 * d + 128] = z[:, 128 * b : 128 * b + 128]

    def placed(g):
        return dot(zall[pl.ds(4 * g, 4)].reshape(4 * CH, 6 * 128), place[...])

    def octant_rows(src):
        for g in range(NB // 4):
            rows = src[4 * g : 4 * g + 4].reshape(4 * CH, VOX)
            sums = dot(rows, spread[...])
            for bb in range(4):
                part = sums[CH * bb : CH * bb + CH] * eye
                ysum[4 * g + bb : 4 * g + bb + 1, :] = jnp.sum(part, axis=0, keepdims=True)
        return ysum[...]

    def expand(g):
        parts = []
        for bb in range(4):
            row = yrow[pl.ds(4 * g + bb, 1), :]
            parts.append((row * eye).astype(BF16))
        return dot(jnp.concatenate(parts, axis=0), spread_t[...])

    def row_wait(buf, sem, count=n_blk - 1):
        pltpu.make_async_copy(buf.at[pl.ds(1, count)], buf.at[pl.ds(1, count)], sem).wait()

    def send_rows(src, dst, back, k):
        for i in FAR_FIRST:
            dx, dz = i // 8, i % 8
            pltpu.make_async_remote_copy(
                src_ref=src.at[i], dst_ref=dst.at[i], send_sem=asend.at[k], recv_sem=arecv.at[k],
                device_id=apart(4 - dx, 8 - dz) if back else apart(dx, dz), device_id_type=MESH,
            ).start()

    load("cot", cot_hbm, cot)
    load("spread", spread_hbm, spread)
    load("perm", perm_hbm, perm)
    load("place", place_hbm, place)
    load("up", w_up_hbm, w_up)
    load("down", w_down_hbm, w_down)
    load("coarse", w_coarse_hbm, w_coarse, 3)
    load("perm_t", perm_t_hbm, perm_t)
    load("spread_t", spread_t_hbm, spread_t)

    loaded("fine")
    loaded("pull")
    make_faces(fine, faces1, None)
    load_idx.wait()
    make_packs(faces1, pack1)
    pl.semaphore_wait(barrier, n_blk - 1 + n_slab - 1 + 16 + 2)
    copies1 = face_copies(land1, pack1, 0)
    for copy in copies1:
        copy.start()

    packet_rows = n_blk * 16
    sub16 = iota((CELLS, 128), 0)
    lane16 = iota((CELLS, 128), 1)
    own_col = jnp.full((CELLS, 128), 0, jnp.int32)
    cell_col = jnp.full((CELLS, 128), -1, jnp.int32)
    for b in range(NB):
        own_col = jnp.where(sub16 == b, owner[b], own_col)
        cell_col = jnp.where(sub16 == b, cell[b], cell_col)
    own_row = jnp.sum(jnp.where(sub16 == lane16, own_col, 0), axis=0, keepdims=True)
    same = (own_col == own_row) & (lane16 < sub16)
    slot = jnp.sum(same.astype(jnp.int32), axis=1, keepdims=True)
    own_at = own_col[:, :1]
    ahead = 8 * lax.bitwise_and(lax.shift_right_logical(own_at, 3) + 4 - me_x, 3) + (
        lax.bitwise_and(own_at + 8 - me_z, 7))
    start = jnp.where(iota((CELLS, 1), 0) < NB, ahead * 16 + 5 * slot, -1000)
    start_col = jnp.concatenate([start + j for j in range(5)] + [start * 0 - 1000] * 3, axis=0)
    route_t = (iota((128, packet_rows), 1) == start_col).astype(BF16)
    start_row = jnp.sum(jnp.where(diagonal, start_col, 0), axis=0, keepdims=True)
    route_pk[...] = (iota((packet_rows, 128), 0) == start_row).astype(BF16)
    cell_hot = (lane16 == cell_col).astype(F32)

    def packets(rows, last):
        wide = rows.astype(F32)
        payload = jnp.concatenate(
            [wide[:, 128 * j : 128 * j + 128] for j in range(4)]
            + [last, jnp.zeros((48, 128), F32)], axis=0).astype(BF16)
        return dot(route_pk[...], payload).astype(BF16).reshape(n_blk, 16, 128)

    ysum[...] = jnp.zeros((CELLS, VOX), F32)
    loaded("cot")
    loaded("spread")
    loaded("perm")
    d_raised = dot(octant_rows(cot).astype(BF16), perm[...]).astype(BF16)
    pk_a[...] = packets(d_raised, cell_hot)
    arr_a[0] = pk_a[0]
    send_rows(pk_a, arr_a, False, 0)

    for e in range(7):
        d = 0 if e == 0 else OPPOSITE[e - 1] + 1
        w_bwd[:, CH * e : CH * e + CH] = w_fwd[:, CH * d : CH * d + CH].astype(F32).T

    def own_forward(b, carry):
        roll_taps(fine, b, own_taps, b)
        pre[b] = dot(w_fwd[...], own_taps[b])
        return carry

    lax.fori_loop(0, NB, own_forward, 0, unroll=NB)
    loaded("place")
    for copy in copies1:
        copy.wait_recv()
    gather_faces(faces1, land1, near1)
    weigh_faces(w_fwd[...], near1)

    def fine_forward(g, carry):
        more = placed(g).reshape(4, CH, VOX)
        for bb in range(4):
            b = 4 * g + bb
            value = pre[b] + more[bb]
            pre[b] = value
            mid[b] = (fine[b].astype(F32) + value * jax.nn.sigmoid(value)).astype(BF16)
        return carry

    lax.fori_loop(0, NB // 4, fine_forward, 0, unroll=NB // 4)
    means = dot((octant_rows(mid) * (1.0 / 64.0)).astype(BF16), perm[...]).astype(BF16)
    pk_b[...] = packets(means, jnp.zeros((CELLS, 128), F32))
    arr_b[0] = pk_b[0]
    send_rows(pk_b, arr_b, False, 1)

    def lined(arr):
        wide = arr[...].reshape(packet_rows, 128).astype(F32)
        return jnp.concatenate([pltpu.roll(wide, 4 - j, 0) for j in range(4)], axis=1).astype(BF16)

    def two_parts(x):
        high = x.astype(BF16)
        return high, (x - high.astype(F32)).astype(BF16)

    row_wait(arr_a, arecv.at[0])
    row_of = iota((packet_rows, 128), 0) % 16
    hot = jnp.where(
        (row_of == 4) | (row_of == 9), arr_a[...].reshape(packet_rows, 128).astype(F32), 0.0)
    hot_t = hot.T[:CELLS].astype(BF16)
    hot16 = hot.astype(BF16)
    raised_hi, raised_lo = two_parts(dot(hot_t, lined(arr_a)))
    loaded("up")
    lift = dot_nt(jnp.concatenate([raised_hi, raised_lo], axis=0), w_up[...])
    dco[...] = cotc[...].astype(F32) + lift[:CELLS] + lift[CELLS:]
    loaded("down")

    def rim_copies(src, dst, offsets, base):
        count = len(offsets)
        return [
            pltpu.make_async_remote_copy(
                src_ref=src, dst_ref=dst.at[count - 1 - i], send_sem=rsend.at[base + i],
                recv_sem=rrecv.at[base + count - 1 - i], device_id=near_id(a, b),
                device_id_type=MESH,
            )
            for i, (a, b) in enumerate(offsets)
        ]

    def inside(a, b):
        zz, yy = me_s + a, me_b + b
        within = (zz >= 0) & (zz < n_slab) & (yy >= 0) & (yy < n_blk)
        return jnp.where(within, 1.0, 0.0)

    rimsrc2[...] = dco[...]
    copies3 = rim_copies(rimsrc2, rim2, OFFSETS, len(WIDE))
    for copy in copies3:
        copy.start()
    row_wait(arr_b, arecv.at[1])
    means_hi, means_lo = two_parts(dot(hot_t, lined(arr_b)))
    pooled = dot(jnp.concatenate([means_hi, means_lo], axis=0), w_down[...])
    c_in = (latent[...].astype(F32) + pooled[:CELLS] + pooled[CELLS:]).astype(BF16)

    sub_x = iota((CELLS, WID), 0)

    def along_x(tile, step):
        if step == 0:
            return tile
        moved = pltpu.roll(tile, 1 if step == -1 else CELLS - 1, 0)
        return jnp.where(sub_x == (0 if step == -1 else CELLS - 1), 0.0, moved)

    def column_copies(src, dst, k):
        made = [
            pltpu.make_async_remote_copy(
                src_ref=src, dst_ref=dst.at[me_s], send_sem=csend.at[8 * k + i],
                recv_sem=crecv.at[k], device_id=column(i), device_id_type=MESH,
            )
            for i in range(1, n_slab)
        ]
        pltpu.make_async_copy(src, dst.at[me_s], crecv.at[k]).start()
        for copy in made:
            copy.start()
        return made

    odd = lax.rem(me_b, 2)
    even_row = me_b - odd

    def plane_copies(src, dst, slab, k):
        made = []
        for i in range(2):
            k_blk = even_row + i
            copy = pltpu.make_async_remote_copy(
                src_ref=src, dst_ref=dst.at[odd, me_s], send_sem=csend.at[8 * k + i],
                recv_sem=crecv.at[k], device_id=(slab, k_blk), device_id_type=MESH,
            )
            mine = (me_s == slab) & (me_b == k_blk)
            pl.when(jnp.logical_not(mine))(copy.start)
            pl.when(mine)(pltpu.make_async_copy(src, dst.at[odd, me_s], crecv.at[k]).start)
            made.append((jnp.logical_not(mine), copy))
        return made

    rimsrc1[...] = c_in
    copies2 = rim_copies(rimsrc1, rim1, WIDE, 0)
    for copy in copies2:
        copy.start()
    loaded("coarse")
    for copy in copies2:
        copy.wait_recv()

    for a in range(-2, 3):
        for b in range(-2, 3):
            if a == 0 and b == 0:
                tile = c_in.astype(F32)
            else:
                tile = rim1[WIDE.index((a, b))].astype(F32) * inside(a, b)
            triple[5 * (a + 2) + b + 2] = jnp.concatenate(
                [along_x(tile, r - 1) for r in range(3)], axis=1).astype(BF16)
    plane_row = lambda b: triple[12 + b, :, WID : 2 * WID]
    xsrc[...] = jnp.concatenate(
        [jnp.where(odd == 0, plane_row(i - 1).astype(F32), plane_row(i - 2).astype(F32))
         for i in range(4)], axis=1).astype(BF16)
    x_sent = column_copies(xsrc, xgat, 0)
    acc = jnp.zeros((9 * CELLS, WID), F32)
    for p in range(3):
        for q in range(3):
            rows = jnp.concatenate(
                [triple[5 * (a + p + 1) + b + q + 1] for a, b in BOXES], axis=0)
            base = (p * 3 + q) * 3 * WID
            acc = acc + dot(rows, w_coarse[base : base + 3 * WID, :])
    boxes[...] = acc
    for copy in copies3:
        copy.wait_recv()
    for i, (a, b) in enumerate(BOXES):
        value = boxes[CELLS * i : CELLS * i + CELLS]
        sig = jax.nn.sigmoid(value)
        slope = sig * (1.0 + value * (1.0 - sig))
        if i == 4:
            d_pre = dco[...] * slope
            c_out = (c_in.astype(F32) + value * sig).astype(BF16)
        else:
            d_pre = rim2[OFFSETS.index((a, b))] * slope * inside(a, b)
        d_box[i] = d_pre.astype(BF16).astype(F32)
    coarse_out[...] = c_out
    dsrc[...] = jnp.concatenate(
        [jnp.where(odd == 0, d_box[4 + i], d_box[3 + i]) for i in range(2)], axis=1).astype(BF16)
    d_sent = column_copies(dsrc, dgat, 1)
    upsrc[...] = jnp.concatenate([c_out.astype(F32), raised_hi.astype(F32)], axis=1).astype(BF16)
    up_sent = plane_copies(upsrc, upgat, n_slab - 1, 2)
    acc = jnp.zeros((CELLS, WID), F32)
    for p in range(3):
        for q in range(3):
            tile = d_box[3 * (2 - p) + 2 - q]
            for r in range(3):
                base = ((p * 3 + q) * 3 + r) * WID
                moved = along_x(tile, 1 - r).astype(BF16)
                acc = acc + dot_nt(moved, w_coarse[base : base + WID, :])
    g_lat = (dco[...] + acc).astype(BF16)
    grad_latent[...] = g_lat

    grid = jnp.concatenate([c_out.astype(F32), g_lat.astype(F32)], axis=1)
    grid = jnp.concatenate([grid, jnp.zeros((128 - CELLS, 2 * WID), F32)], axis=0).astype(BF16)
    picked = dot(hot16, grid)
    back = jnp.zeros((packet_rows, 128), F32)
    for j in range(4):
        back = back + pltpu.roll(picked[:, 128 * j : 128 * j + 128], packet_rows - 4 + j, 0)
    rpk[...] = back.astype(BF16).reshape(n_blk, 16, 128)
    rarr[0] = rpk[0]
    send_rows(rpk, rarr, True, 2)
    downsrc[...] = jnp.concatenate([g_lat.astype(F32), means_hi.astype(F32)], axis=1).astype(BF16)
    down_sent = plane_copies(downsrc, downgat, 0, 3)

    base_row = me_s * SLAB_ROWS + 144
    first_tap = base_row // WID - 3
    skew = base_row % WID
    pltpu.make_async_copy(xgat, xgat, crecv.at[0]).wait()
    everything = xgat[...].reshape(n_slab * CELLS, 4 * WID).astype(F32)
    for q in range(4):
        xq[q] = everything[:, q * WID : q * WID + WID].T.astype(BF16)
    pltpu.make_async_copy(dgat, dgat, crecv.at[1]).wait()
    pair = dgat[...].reshape(n_slab * CELLS, 2 * WID)
    d_all[...] = jnp.concatenate([pair[:, :WID], pair[:, WID:]], axis=0)

    def tap_rows(i, carry):
        t = first_tap + i
        good = (t >= 0) & (t < 27)
        tc = jnp.clip(t, 0, 26)
        p, q, r = tc // 9, tc // 3 % 3, tc % 3
        shift = ((sub // 16 == lane // 16 + p - 1) & (sub % 16 == lane % 16 + r - 1)).astype(BF16)
        moved = jnp.concatenate([dot(xq[q], shift), dot(xq[q + 1], shift)], axis=1).astype(BF16)
        gbuf[pl.ds(pl.multiple_of(i * WID, WID), WID), :] = (
            dot(moved, d_all[...]) * jnp.where(good, 1.0 / math.sqrt(CELLS * total), 0.0)
        ).astype(BF16)
        return carry

    lax.fori_loop(0, 5, tap_rows, 0, unroll=5)
    rows_scale = 1.0 / math.sqrt(NB * total)

    @pl.when(me_s == n_slab - 1)
    def _():
        pltpu.make_async_copy(upgat, upgat, crecv.at[2]).wait()
        left = upgat[:, :, :, :WID].reshape(2 * n_slab * CELLS, WID)
        twice = (iota((WID, VOX), 1) // 2 == iota((WID, VOX), 0)).astype(BF16)
        left = dot(left, twice).astype(BF16)
        right = upgat[:, :, :, WID:].reshape(2 * n_slab * CELLS, VOX)
        up = jnp.where(iota((VOX, WID), 0) % 2 == 0, dot_tn(left, right[:, :WID]),
                       dot_tn(left, right[:, WID:]))
        gbuf[512:1024, :] = (up * rows_scale).astype(BF16)

    @pl.when(me_s == 0)
    def _():
        pltpu.make_async_copy(downgat, downgat, crecv.at[3]).wait()
        left = downgat[:, :, :, WID:].reshape(2 * n_slab * CELLS, VOX)
        right = downgat[:, :, :, :WID].reshape(2 * n_slab * CELLS, WID)
        gbuf[256:768, :] = (dot_tn(left, right) * rows_scale).astype(BF16)

    def window_of(k):
        unit = (16 * skew + 503 * k) // 256
        return gbuf.at[pl.ds(pl.multiple_of(16 * unit, 16), 48)]

    def send_window(i, carry):
        pltpu.make_async_remote_copy(
            src_ref=window_of(lax.rem(me_b + 2 * i, n_blk)), dst_ref=wland.at[i],
            send_sem=vsend, recv_sem=vrecv.at[0], device_id=rel(2 * i), device_id_type=MESH,
        ).start()
        return carry

    lax.fori_loop(1, n_blk // 2, send_window, 0)
    loaded("perm_t")
    loaded("spread_t")
    row_wait(rarr, arecv.at[2])
    rows = dot(route_t, rarr[...].reshape(packet_rows, 128))
    lifted = jnp.concatenate([rows[0:16], rows[16:32]], axis=1).astype(BF16)
    d_pooled = jnp.concatenate([rows[32:48], rows[48:64]], axis=1).astype(BF16)

    d_means = dot_nt(d_pooled, w_down[...]) * (1.0 / 64.0)
    yrow[...] = dot(d_means.astype(BF16), perm_t[...])

    def fine_slope(g, carry):
        spreadv = expand(g).reshape(4, CH, VOX)
        for bb in range(4):
            b = 4 * g + bb
            d_mid = cot[b].astype(F32) + spreadv[bb]
            big[b] = d_mid
            value = pre[b]
            s = jax.nn.sigmoid(value)
            dpf[b] = (d_mid * (s * (1.0 + value * (1.0 - s)))).astype(BF16)
        return carry

    lax.fori_loop(0, NB // 4, fine_slope, 0, unroll=NB // 4)
    make_faces(dpf, faces2, faces_wide)
    make_packs(faces2, pack2)
    copies4 = face_copies(land2, pack2, 1)
    for copy in copies4:
        copy.start()
    w_back = w_bwd[...].astype(BF16)
    gacc[...] = jnp.zeros((7 * CH, CH), F32)

    def weight_grad(b, carry):
        gacc[...] += dot_nt(own_taps[b], dpf[b])
        return carry

    lax.fori_loop(0, NB, weight_grad, 0, unroll=NB)
    for d in range(6):
        gacc[CH * (d + 1) : CH * (d + 2), :] += dot_nt(near1[d], faces_wide[d])
    fine_bf = (gacc[...] * (1.0 / math.sqrt(NB * total * VOX))).astype(BF16)
    row_to = iota((7 * 16, 7 * CH), 0)
    quarters = []
    for m in range(4):
        pick = iota((7 * 16, 7 * CH), 1) == 64 * (row_to // 16) + 4 * (row_to % 16) + m
        quarters.append(dot(pick.astype(BF16), fine_bf))
    fsrc[...] = jnp.concatenate(quarters, axis=1).astype(BF16).reshape(7, 16, WID)
    fine_copies = [
        pltpu.make_async_remote_copy(
            src_ref=fsrc.at[t], dst_ref=fland.at[me_b], send_sem=usend.at[2 + t],
            recv_sem=vrecv.at[1], device_id=(me_s, t), device_id_type=MESH,
        )
        for t in range(7)
    ]
    for t in range(7):
        pl.when(me_b != t)(fine_copies[t].start)

    @pl.when(me_b < 7)
    def _():
        pltpu.make_async_copy(fsrc.at[lax.rem(me_b, 7)], fland.at[me_b], vrecv.at[1]).start()

    def own_backward(b, carry):
        buf = lax.rem(b, 2)
        roll_taps(dpf, b, back_taps, buf)
        big[b] += dot(w_back, back_taps[buf])
        return carry

    lax.fori_loop(0, NB, own_backward, 0, unroll=NB)
    for copy in copies4:
        copy.wait_recv()
    gather_faces(faces2, land2, near2)
    weigh_faces(w_back, near2)

    def fine_backward(g, carry):
        more = placed(g).reshape(4, CH, VOX)
        for bb in range(4):
            b = 4 * g + bb
            grad_fine[b] = (big[b] + more[bb]).astype(BF16)
        return carry

    lax.fori_loop(0, NB // 4, fine_backward, 0, unroll=NB // 4)
    store_grad = pltpu.make_async_copy(grad_fine, grad_fine_hbm, osem.at[0])
    store_grad.start()

    @pl.when(me_b < 7)
    def _():
        pltpu.make_async_copy(fland, fland, vrecv.at[1]).wait()
        unit_sum = fland[0].astype(F32)
        for i in range(1, n_blk):
            unit_sum = unit_sum + fland[i].astype(F32)
        unit_ref[...] = unit_sum.astype(BF16)

    unit = me_b + 9
    low = (256 * (unit - 2) - 2304 + 502 + 503 * 8) // 503 - 8
    sent = []
    for i in range(2):
        k = low + i
        begin = (2304 + 503 * k + 2560) // 256 - 10
        good = (me_b < 7) & (k >= 0) & (k < n_blk) & (begin <= unit)
        mine = (me_s == 0) & (me_b == k)
        at = jnp.clip(unit - begin, 0, 2)
        away = pltpu.make_async_remote_copy(
            src_ref=unit_ref, dst_ref=uland.at[at, me_s], send_sem=usend.at[i],
            recv_sem=urecv.at[at], device_id=(0, jnp.clip(k, 0, n_blk - 1)), device_id_type=MESH,
        )
        home = pltpu.make_async_copy(unit_ref, uland.at[at, me_s], urecv.at[at])
        pl.when(good & mine)(home.start)
        pl.when(good & jnp.logical_not(mine))(away.start)
        sent.append((good & jnp.logical_not(mine), away))

    yrow[...] = dot(dot(lifted, w_up[...]).astype(BF16), perm_t[...])

    def fine_up(g, carry):
        spreadv = expand(g).reshape(4, CH, VOX)
        for bb in range(4):
            b = 4 * g + bb
            fine_out[b] = (mid[b].astype(F32) + spreadv[bb]).astype(BF16)
        return carry

    lax.fori_loop(0, NB // 4, fine_up, 0, unroll=NB // 4)
    store_out = pltpu.make_async_copy(fine_out, fine_out_hbm, osem.at[1])
    store_out.start()
    row_wait(wland, vrecv.at[0], n_blk // 2 - 1)
    summed = window_of(me_b)[...].astype(F32)
    for i in range(1, n_blk // 2):
        summed = summed + wland[i].astype(F32)
    gsum[...] = summed

    my_unit = (16 * skew + 503 * me_b) // 256
    for u in range(3):
        @pl.when((me_s == 0) & (my_unit + u < 16))
        def _():
            pltpu.make_async_copy(uland.at[u], uland.at[u], urecv.at[u]).wait()
            rows = slice(16 * u, 16 * u + 16)
            gsum[rows, :] += jnp.sum(uland[u].astype(F32), axis=0)

    down_by = skew + 503 * me_b // 16 - 16 * my_unit
    left_by = 16 * (503 * me_b % 16)
    value = pltpu.roll(gsum[...], lax.rem(48 - down_by, 48), 0)
    value = pltpu.roll(value, lax.rem(WID - left_by, WID), 1)
    below = pltpu.roll(value, 47, 0)
    grads_out[...] = jnp.where(
        iota((32, WID), 1) < WID - left_by, value[:32], below[:32])

    for copy in copies1 + copies4 + copies2 + copies3 + x_sent + d_sent:
        copy.wait_send()
    for good, copy in up_sent + down_sent:
        pl.when(good)(copy.wait_send)
    row_wait(pk_a, asend.at[0])
    row_wait(pk_b, asend.at[1])
    row_wait(rpk, asend.at[2])
    row_wait(wland, vsend, n_blk // 2 - 1)
    for t in range(7):
        pl.when(me_b != t)(fine_copies[t].wait_send)
    for good, copy in sent:
        pl.when(good)(copy.wait_send)
    store_grad.wait()
    store_out.wait()


def fused(n_slab, n_blk, *operands):
    vmem = pl.BlockSpec(memory_space=pltpu.VMEM)
    smem = pl.BlockSpec(memory_space=pltpu.SMEM)
    hbm = pl.BlockSpec(memory_space=pl.ANY)
    sds = jax.ShapeDtypeStruct
    fine_like = sds((NB, CH, VOX), BF16)
    cells = sds((CELLS, WID), BF16)
    dma = pltpu.SemaphoreType.DMA
    rows = (n_blk, 16, 128)
    bf = lambda *shape: pltpu.VMEM(shape, BF16)
    f32 = lambda *shape: pltpu.VMEM(shape, F32)
    return pl.pallas_call(
        functools.partial(kernel, n_slab, n_blk),
        name="window",
        out_shape=(fine_like, cells, fine_like, cells, sds((32, WID), F32)),
        in_specs=[hbm] * 2 + [vmem] * 3 + [hbm] * 3 + [smem] * 3 + [hbm] * 2 + [vmem] + [hbm] * 4,
        out_specs=(hbm, vmem, hbm, vmem, vmem),
        scratch_shapes=[
            bf(NB, CH, VOX), bf(NB, CH, VOX), bf(VOX, WID), bf(WID, VOX), bf(27 * WID, WID),
            bf(VOX, 6 * 128), bf(6 * 128, VOX), bf(VOX, VOX), bf(VOX, VOX), bf(VOX, VOX),
            bf(VOX, VOX),
            bf(NB, CH, VOX), bf(NB, CH, VOX), bf(SLOTS, CH, 128), bf(SLOTS, CH, 128),
            bf(6, CH, NB * 128), bf(2, 3, CH, 128), bf(2, 3, CH, 128), bf(6, CH, 128),
            bf(6, CH, 128), bf(2, CH, 128), bf(6, CH, NB * 128), bf(6, CH, NB * 128),
            bf(NB, CH, 6 * 128), bf(NB, 7 * CH, VOX), bf(2, 7 * CH, VOX), f32(NB, CH, VOX), bf(NB, CH, VOX), bf(NB, CH, VOX),
            f32(NB, CH, VOX), f32(CELLS, VOX), f32(CELLS, VOX), f32(CH, 7 * CH),
            bf(n_blk * 16, 128), bf(*rows), bf(*rows), bf(*rows), bf(*rows), bf(*rows), bf(*rows),
            bf(24, CELLS, WID), f32(8, CELLS, WID), bf(CELLS, WID), f32(CELLS, WID),
            bf(25, CELLS, 3 * WID), f32(9 * CELLS, WID), f32(9, CELLS, WID), bf(WID, WID),
            f32(7 * CH, CH),
            bf(CELLS, 4 * WID), bf(CELLS, 2 * WID), bf(CELLS, 3 * WID), bf(CELLS, 3 * WID),
            bf(n_slab, CELLS, 4 * WID), bf(n_slab, CELLS, 2 * WID), bf(2, n_slab, CELLS, 3 * WID),
            bf(2, n_slab, CELLS, 3 * WID),
            f32(CELLS, WID), bf(4, WID, 128), bf(5 * WID, WID), bf(n_blk // 2, 48, WID), bf(7, 16, WID),
            bf(n_blk, 16, WID), bf(16, WID), bf(3, n_slab, 16, WID), f32(48, WID),
            pltpu.VMEM((8, 128), jnp.int32), pltpu.SMEM((8, 128), jnp.int32),
            dma((16,)), dma, dma((2,)), dma((4,)), dma((4,)), dma((3,)), dma((3,)), dma((32,)),
            dma((32,)), dma((32,)), dma((4,)), dma, dma((2,)), dma((9,)), dma((3,)),
        ],
        compiler_params=pltpu.CompilerParams(
            collective_id=0, has_side_effects=True, vmem_limit_bytes=56 * 1024 * 1024
        ),
    )(*operands)


def finish_kernel(fine_in, grad_in, coarse_in, latent_in, flat_in, fine_to, grad_to, coarse_to,
                  latent_to, flat_to, held, cells, flat, in_sems, out_sems):
    moves = [(flat_in, flat, None), (coarse_in, cells.at[0], coarse_to),
             (latent_in, cells.at[1], latent_to)]
    for i, (src, dst) in enumerate(((fine_in, fine_to), (grad_in, grad_to))):
        for j in range(4):
            rows = pl.ds(3 * j, 3)
            moves.append((src.at[rows], held.at[i, rows], dst.at[rows]))
    takes = [pltpu.make_async_copy(src, mid, in_sems.at[n])
             for n, (src, mid, dst) in enumerate(moves)]
    gives = [pltpu.make_async_copy(mid, dst, out_sems.at[n])
             for n, (src, mid, dst) in enumerate(moves) if dst is not None]
    for copy in takes:
        copy.start()
    for take, give in zip(takes[1:], gives):
        take.wait()
        give.start()
    takes[0].wait()
    for r in range(SHARD // WID):
        flat_to[WID * r : WID * r + WID] = flat[r, :]
    rest = SHARD % WID
    flat_to[SHARD - rest : SHARD] = flat[SHARD // WID, :rest]
    for give in gives:
        give.wait()


def finish(fine_out, coarse_out, grad_fine, grad_latent, flat):
    hbm = pl.BlockSpec(memory_space=pl.ANY)
    like = lambda a: jax.ShapeDtypeStruct(a.shape, a.dtype)
    fine_out, grad_fine, coarse_out, grad_latent, flat = pl.pallas_call(
        finish_kernel,
        name="finish",
        out_shape=(like(fine_out), like(grad_fine), like(coarse_out), like(grad_latent),
                   jax.ShapeDtypeStruct((SHARD,), F32)),
        in_specs=[hbm] * 5,
        out_specs=(hbm, hbm, hbm, hbm, pl.BlockSpec(memory_space=pltpu.VMEM)),
        scratch_shapes=[pltpu.VMEM((2, NB, CH, VOX), BF16), pltpu.VMEM((2, CELLS, WID), BF16),
                        pltpu.VMEM((32, WID), F32), pltpu.SemaphoreType.DMA((11,)),
                        pltpu.SemaphoreType.DMA((11,))],
    )(fine_out, grad_fine, coarse_out, grad_latent, flat)
    return fine_out, coarse_out, grad_fine, grad_latent, flat


def shards(
    n_slab, n_blk,
    fine_in, latent, w_fine, w_down, w_coarse, w_up, neighbors, pool_owner, pool_cell, cot_fine,
    cot_coarse,
):
    outs = fused(
        n_slab, n_blk,
        fine_in, cot_fine, latent.reshape(CELLS, WID), cot_coarse.reshape(CELLS, WID),
        w_fine.T, w_down, w_up, w_coarse, neighbors.T, pool_owner.reshape(NB), pool_cell,
        *tables())
    fine_out, c_out, grad_fine, g_lat, weight_grads = finish(*outs)
    return (fine_out, c_out.reshape(latent.shape), grad_fine, g_lat.reshape(latent.shape),
            weight_grads)


def solution(mesh):
    n_slab, n_blk = mesh.shape["slab"], mesh.shape["blk"]
    return jax.shard_map(
        functools.partial(shards, n_slab, n_blk),
        mesh=mesh,
        in_specs=(
            P(("slab", "blk"), None, None), P("slab", "blk", None, None), P(), P(), P(), P(),
            P(("slab", "blk"), None), P(("slab", "blk"), None), P(("slab", "blk")),
            P(("slab", "blk"), None, None), P("slab", "blk", None, None),
        ),
        out_specs=(
            P(("slab", "blk"), None, None), P("slab", "blk", None, None),
            P(("slab", "blk"), None, None), P("slab", "blk", None, None), P(("slab", "blk")),
        ),
        check_vma=False,
    )
```

```python
import functools
import math

import jax
import jax.numpy as jnp
import numpy as np
from jax import lax
from jax.experimental import pallas as pl
from jax.experimental.pallas import tpu as pltpu
from jax.sharding import PartitionSpec as P

NB = 12
CH = 64
VOX = 512
WID = 256
CELLS = 16
FB = 6
OPPOSITE = (1, 0, 3, 2, 5, 4)
STRIDES = (64, 8, 1)
FACES = NB * 6
PREV0 = FACES
NEXT0 = FACES + 3
ZERO = FACES + 6
SLOTS = FACES + 7
OFFSETS = ((-1, -1), (-1, 0), (-1, 1), (0, -1), (0, 1), (1, -1), (1, 0), (1, 1))
WIDE = tuple((a, b) for a in range(-2, 3) for b in range(-2, 3) if (a, b) != (0, 0))
BOXES = tuple((a, b) for a in range(-1, 2) for b in range(-1, 2))
SHARD = 8048
FAR_FIRST = sorted(range(1, 32), key=lambda i: -(min(i // 8, 4 - i // 8) + min(i % 8, 8 - i % 8)))
SLAB_ROWS = 1006
MESH = pl.DeviceIdType.MESH
F32 = jnp.float32
BF16 = jnp.bfloat16


def tables():
    voxel = np.arange(VOX)
    coords = (voxel // 64, voxel // 8 % 8, voxel % 8)
    octant = 4 * (coords[0] // 4) + 2 * (coords[1] // 4) + coords[2] // 4
    pull = np.zeros((VOX, 6 * 128), np.float32)
    place = np.zeros((6, 128, VOX), np.float32)
    keep = np.ones((6, 1, VOX), np.float32)
    for axis in range(3):
        others = [coords[other] for other in range(3) if other != axis]
        index = others[0] * 8 + others[1]
        for side in range(2):
            d = 2 * axis + side
            on = coords[axis] == 7 * side
            keep[d, 0, on] = 0.0
            for half in range(2):
                pull[voxel[on], 128 * d + 64 * half + index[on]] = 1.0
                place[d, 64 * half + index[on], voxel[on]] = 1.0
    spread = (octant[:, None] == np.arange(VOX)[None, :] // 64).astype(np.float32)
    major = np.arange(VOX)
    perm = np.zeros((VOX, VOX), np.float32)
    perm[major, 8 * (major % 64) + major // 64] = 1.0
    bf = lambda a: jnp.asarray(a, BF16)
    return bf(pull), bf(place.reshape(6 * 128, VOX)), jnp.asarray(keep), bf(spread), bf(spread.T), bf(perm), bf(perm.T)


def dot(a, b):
    return jnp.dot(a, b, preferred_element_type=F32)


def dot_nt(a, b):
    return lax.dot_general(a, b, (((1,), (1,)), ((), ())), preferred_element_type=F32)


def dot_tn(a, b):
    return lax.dot_general(a, b, (((0,), (0,)), ((), ())), preferred_element_type=F32)


def iota(shape, dim):
    return lax.broadcasted_iota(jnp.int32, shape, dim)


def kernel(
    n_slab, n_blk,
    fine_hbm, cot_hbm, latent, cotc, w_fwd, w_down_hbm, w_up_hbm, w_coarse_hbm, nbr, owner, cell,
    pull_hbm, place_hbm, keep, spread_hbm, spread_t_hbm, perm_hbm, perm_t_hbm,
    fine_out_hbm, coarse_out, grad_fine_hbm, grad_latent, grads_out,
    fine, cot, w_down, w_up, w_coarse, pull, place, spread, spread_t, perm, perm_t,
    fine_out, grad_fine, faces1, faces2, faces_wide, pack1, pack2, land1, land2, half, near1, near2, zall,
    own_taps, back_taps, pre, mid, dpf, big, ysum, yrow, w_bwd, route_pk, cells_of, arr_a, arr_b, pk_a, pk_b, rpk, rarr,
    rim1, rim2, rimsrc1, rimsrc2, triple, boxes, d_box, d_all, gacc, xsrc, dsrc, upsrc, downsrc, xgat, dgat, upgat, downgat,
    dco, xq, gbuf, wland, fsrc, fland, unit_ref, uland, gsum, idx_v, idx_s,
    wsem, isem, osem, fsend, frecv, asend, arecv, rsend, rrecv, csend, crecv, vsend, vrecv,
    usend, urecv,
):
    me_s = lax.axis_index("slab")
    me_b = lax.axis_index("blk")
    total = n_slab * n_blk
    pos = me_s * n_blk + me_b
    after = lax.rem(pos + 1, total)
    before = lax.rem(pos + total - 1, total)
    rel = lambda i: (me_s, lax.rem(me_b + i, n_blk))
    me_x, me_z = lax.div(me_b, 8), lax.rem(me_b, 8)
    apart = lambda dx, dz: (me_s, lax.rem(me_x + dx, 4) * 8 + lax.rem(me_z + dz, 8))
    column = lambda i: (lax.rem(me_s + i, n_slab), me_b)
    flat = lambda k: (lax.div(k, n_blk), lax.rem(k, n_blk))
    near_id = lambda a, b: (lax.rem(me_s + a + n_slab, n_slab), lax.rem(me_b + b + n_blk, n_blk))

    loads = {}

    def load(name, src, dst, parts=1):
        size = src.shape[0] // parts
        loads[name] = []
        for i in range(parts):
            rows = pl.ds(size * i, size)
            copy = pltpu.make_async_copy(src.at[rows], dst.at[rows], wsem.at[len(taken)])
            taken.append(name)
            loads[name].append(copy)
            copy.start()

    def loaded(name):
        for copy in loads[name]:
            copy.wait()

    taken = []
    load("fine", fine_hbm, fine, 3)
    load("pull", pull_hbm, pull, 2)

    barrier = pltpu.get_barrier_semaphore()

    def greet(i, carry):
        pl.semaphore_signal(barrier, inc=1, device_id=rel(i), device_id_type=MESH)
        return carry

    lax.fori_loop(1, n_blk, greet, 0)
    for i in range(1, n_slab):
        pl.semaphore_signal(barrier, inc=1, device_id=column(i), device_id_type=MESH)
    for a, b in WIDE:
        if a != 0 and b != 0:
            pl.semaphore_signal(barrier, inc=1, device_id=near_id(a, b), device_id_type=MESH)
    for k in (before, after):
        pl.semaphore_signal(barrier, inc=1, device_id=flat(k), device_id_type=MESH)

    lane1 = iota((1, 128), 1)
    lane = iota((128, 128), 1)
    sub = iota((128, 128), 0)
    diagonal = lane == sub
    ints = lambda m: m.astype(jnp.int32)
    as_col = lambda row: jnp.sum(jnp.where(diagonal, row, 0), axis=1, keepdims=True)
    down_sum = lambda m: jnp.sum(ints(m), axis=0, keepdims=True)
    number = jnp.full((1, 128), -1, jnp.int32)
    key = jnp.full((1, 128), 0, jnp.int32)
    for d in range(6):
        for b in range(NB):
            value = nbr[d, b]
            here = lane1 == d * NB + b
            number = jnp.where(here, value, number)
            key = jnp.where(here, value + NB * OPPOSITE[d], key)
    low = NB * pos
    code = jnp.full((1, 128), 2 * ZERO, jnp.int32)
    code = jnp.where((number >= low) & (number < low + NB), 2 * (key - low), code)
    for i, base in ((-1, PREV0), (1, NEXT0)):
        first = low + i * NB
        chosen = (number >= first) & (number < first + NB) & (number >= 0)
        ranked = jnp.where(chosen, key - first, 10000)
        rank = down_sum(as_col(ranked) < ranked)
        code = jnp.where(chosen, 2 * base + rank, code)
        mine = down_sum((as_col(ints(chosen)) == 1) & (sub < lane))
        order = as_col(jnp.where(chosen, mine, -1))
        sends = jnp.sum(jnp.where(order == lane, sub - ZERO, 0), axis=0, keepdims=True) + ZERO
        row = 1 if i == -1 else 2
        idx_v[row : row + 1, :] = jnp.clip(sends, 0, ZERO)
    idx_v[0:1, :] = jnp.clip(code, 0, 2 * ZERO)
    load_idx = pltpu.make_async_copy(idx_v, idx_s, isem)
    load_idx.start()

    lane64 = iota((CH, 128), 1) // 64
    half[0] = (lane64 == 0).astype(BF16)
    half[1] = (lane64 == 1).astype(BF16)
    eye = (iota((CH, VOX), 1) % 64 == iota((CH, VOX), 0)).astype(F32)

    def make_faces(src, faces, wide):
        faces[ZERO] = jnp.zeros((CH, 128), BF16)
        for g in range(NB // 4):
            rows = src[4 * g : 4 * g + 4].reshape(4 * CH, VOX)
            out = dot(rows, pull[...]).astype(BF16)
            for bb in range(4):
                b = 4 * g + bb
                for d in range(6):
                    part = out[CH * bb : CH * bb + CH, 128 * d : 128 * d + 128]
                    faces[d * NB + b] = part
                    if wide is not None:
                        wide[d, :, 128 * b : 128 * b + 128] = part

    def make_packs(faces, pack):
        for s in range(2):
            for q in range(3):
                first = faces[idx_s[1 + s, 2 * q]]
                second = faces[idx_s[1 + s, 2 * q + 1]]
                pack[s, q] = first * half[0] + second * half[1]

    def face_copies(land, pack, k):
        return [
            pltpu.make_async_remote_copy(
                src_ref=pack.at[0], dst_ref=land.at[pl.ds(3, 3)],
                send_sem=fsend.at[2 * k], recv_sem=frecv.at[2 * k],
                device_id=flat(before), device_id_type=MESH,
            ),
            pltpu.make_async_remote_copy(
                src_ref=pack.at[1], dst_ref=land.at[pl.ds(0, 3)],
                send_sem=fsend.at[2 * k + 1], recv_sem=frecv.at[2 * k + 1],
                device_id=flat(after), device_id_type=MESH,
            ),
        ]

    def roll_taps(src, b, taps, at):
        x = src[b]
        taps[at, 0:CH, :] = x
        for d in range(6):
            stride = STRIDES[d // 2]
            moved = pltpu.roll(x, stride if d % 2 == 0 else VOX - stride, 1)
            taps[at, CH * (d + 1) : CH * (d + 2), :] = moved * keep[d].astype(BF16)

    def gather_faces(faces, land, near):
        faces[PREV0 : PREV0 + 6] = land[...]
        for d in range(6):
            for b in range(NB):
                at = idx_s[0, d * NB + b]
                near[d, :, 128 * b : 128 * b + 128] = (
                    faces[lax.shift_right_logical(at, 1)] * half[lax.bitwise_and(at, 1)])

    def weigh_faces(w, near):
        for d in range(6):
            z = dot(w[:, CH * (d + 1) : CH * (d + 2)], near[d]).astype(BF16)
            for b in range(NB):
                zall[b, :, 128 * d : 128 * d + 128] = z[:, 128 * b : 128 * b + 128]

    def placed(g):
        return dot(zall[pl.ds(4 * g, 4)].reshape(4 * CH, 6 * 128), place[...])

    def octant_rows(src):
        for g in range(NB // 4):
            rows = src[4 * g : 4 * g + 4].reshape(4 * CH, VOX)
            sums = dot(rows, spread[...])
            for bb in range(4):
                part = sums[CH * bb : CH * bb + CH] * eye
                ysum[4 * g + bb : 4 * g + bb + 1, :] = jnp.sum(part, axis=0, keepdims=True)
        return ysum[...]

    def expand(g):
        parts = []
        for bb in range(4):
            row = yrow[pl.ds(4 * g + bb, 1), :]
            parts.append((row * eye).astype(BF16))
        return dot(jnp.concatenate(parts, axis=0), spread_t[...])

    def row_wait(buf, sem, count=n_blk - 1):
        pltpu.make_async_copy(buf.at[pl.ds(1, count)], buf.at[pl.ds(1, count)], sem).wait()

    def send_rows(src, dst, back, k):
        for i in FAR_FIRST:
            dx, dz = i // 8, i % 8
            pltpu.make_async_remote_copy(
                src_ref=src.at[i], dst_ref=dst.at[i], send_sem=asend.at[k], recv_sem=arecv.at[k],
                device_id=apart(4 - dx, 8 - dz) if back else apart(dx, dz), device_id_type=MESH,
            ).start()

    load("cot", cot_hbm, cot)
    load("spread", spread_hbm, spread)
    load("perm", perm_hbm, perm)
    load("place", place_hbm, place)
    load("up", w_up_hbm, w_up)
    load("down", w_down_hbm, w_down)
    load("coarse", w_coarse_hbm, w_coarse, 3)
    load("perm_t", perm_t_hbm, perm_t)
    load("spread_t", spread_t_hbm, spread_t)

    loaded("fine")
    loaded("pull")
    make_faces(fine, faces1, None)
    load_idx.wait()
    make_packs(faces1, pack1)
    pl.semaphore_wait(barrier, n_blk - 1 + n_slab - 1 + 16 + 2)
    copies1 = face_copies(land1, pack1, 0)
    for copy in copies1:
        copy.start()

    packet_rows = n_blk * 16
    sub16 = iota((CELLS, 128), 0)
    lane16 = iota((CELLS, 128), 1)
    own_col = jnp.full((CELLS, 128), 0, jnp.int32)
    cell_col = jnp.full((CELLS, 128), -1, jnp.int32)
    for b in range(NB):
        own_col = jnp.where(sub16 == b, owner[b], own_col)
        cell_col = jnp.where(sub16 == b, cell[b], cell_col)
    own_row = jnp.sum(jnp.where(sub16 == lane16, own_col, 0), axis=0, keepdims=True)
    same = (own_col == own_row) & (lane16 < sub16)
    slot = jnp.sum(same.astype(jnp.int32), axis=1, keepdims=True)
    own_at = own_col[:, :1]
    ahead = 8 * lax.bitwise_and(lax.shift_right_logical(own_at, 3) + 4 - me_x, 3) + (
        lax.bitwise_and(own_at + 8 - me_z, 7))
    start = jnp.where(iota((CELLS, 1), 0) < NB, ahead * 16 + 5 * slot, -1000)
    start_col = jnp.concatenate([start + j for j in range(5)] + [start * 0 - 1000] * 3, axis=0)
    route_t = (iota((128, packet_rows), 1) == start_col).astype(BF16)
    start_row = jnp.sum(jnp.where(diagonal, start_col, 0), axis=0, keepdims=True)
    route_pk[...] = (iota((packet_rows, 128), 0) == start_row).astype(BF16)
    cell_hot = (lane16 == cell_col).astype(F32)

    def packets(rows, last):
        wide = rows.astype(F32)
        payload = jnp.concatenate(
            [wide[:, 128 * j : 128 * j + 128] for j in range(4)]
            + [last, jnp.zeros((48, 128), F32)], axis=0).astype(BF16)
        return dot(route_pk[...], payload).astype(BF16).reshape(n_blk, 16, 128)

    ysum[...] = jnp.zeros((CELLS, VOX), F32)
    loaded("cot")
    loaded("spread")
    loaded("perm")
    d_raised = dot(octant_rows(cot).astype(BF16), perm[...]).astype(BF16)
    pk_a[...] = packets(d_raised, cell_hot)
    arr_a[0] = pk_a[0]
    send_rows(pk_a, arr_a, False, 0)

    for e in range(7):
        d = 0 if e == 0 else OPPOSITE[e - 1] + 1
        w_bwd[:, CH * e : CH * e + CH] = w_fwd[:, CH * d : CH * d + CH].astype(F32).T

    def own_forward(b, carry):
        roll_taps(fine, b, own_taps, b)
        pre[b] = dot(w_fwd[...], own_taps[b])
        return carry

    lax.fori_loop(0, NB, own_forward, 0, unroll=NB)
    loaded("place")
    for copy in copies1:
        copy.wait_recv()
    gather_faces(faces1, land1, near1)
    weigh_faces(w_fwd[...], near1)

    def fine_forward(g, carry):
        more = placed(g).reshape(4, CH, VOX)
        for bb in range(4):
            b = 4 * g + bb
            value = pre[b] + more[bb]
            pre[b] = value
            mid[b] = (fine[b].astype(F32) + value * jax.nn.sigmoid(value)).astype(BF16)
        return carry

    lax.fori_loop(0, NB // 4, fine_forward, 0, unroll=NB // 4)
    means = dot((octant_rows(mid) * (1.0 / 64.0)).astype(BF16), perm[...]).astype(BF16)
    pk_b[...] = packets(means, jnp.zeros((CELLS, 128), F32))
    arr_b[0] = pk_b[0]
    send_rows(pk_b, arr_b, False, 1)

    def by_cell(arr):
        parts = dot(cell_pick, arr[...].reshape(packet_rows, 128))
        return jnp.concatenate([parts[16 * j : 16 * j + 16] for j in range(4)], axis=1)

    def two_parts(x):
        high = x.astype(BF16)
        return high, (x - high.astype(F32)).astype(BF16)

    row_wait(arr_a, arecv.at[0])
    row_of = iota((packet_rows, 128), 0) % 16
    hot = jnp.where(
        (row_of == 4) | (row_of == 9), arr_a[...].reshape(packet_rows, 128).astype(F32), 0.0)
    cell_rows = jnp.zeros((packet_rows, 128), F32)
    for j in range(4):
        cell_rows = cell_rows + pltpu.roll(pltpu.roll(hot, packet_rows - 4 + j, 0), 16 * j, 1)
    cell_pick = cell_rows.T[:64].astype(BF16)
    cells_of[...] = cell_rows.astype(BF16)
    raised_hi, raised_lo = two_parts(by_cell(arr_a))
    loaded("up")
    lift = dot_nt(jnp.concatenate([raised_hi, raised_lo], axis=0), w_up[...])
    dco[...] = cotc[...].astype(F32) + lift[:CELLS] + lift[CELLS:]
    loaded("down")

    def rim_copies(src, dst, offsets, base):
        count = len(offsets)
        return [
            pltpu.make_async_remote_copy(
                src_ref=src, dst_ref=dst.at[count - 1 - i], send_sem=rsend.at[base + i],
                recv_sem=rrecv.at[base + count - 1 - i], device_id=near_id(a, b),
                device_id_type=MESH,
            )
            for i, (a, b) in enumerate(offsets)
        ]

    def inside(a, b):
        zz, yy = me_s + a, me_b + b
        within = (zz >= 0) & (zz < n_slab) & (yy >= 0) & (yy < n_blk)
        return jnp.where(within, 1.0, 0.0)

    rimsrc2[...] = dco[...]
    copies3 = rim_copies(rimsrc2, rim2, OFFSETS, len(WIDE))
    for copy in copies3:
        copy.start()
    row_wait(arr_b, arecv.at[1])
    means_hi, means_lo = two_parts(by_cell(arr_b))
    pooled = dot(jnp.concatenate([means_hi, means_lo], axis=0), w_down[...])
    c_in = (latent[...].astype(F32) + pooled[:CELLS] + pooled[CELLS:]).astype(BF16)

    sub_x = iota((CELLS, WID), 0)

    def along_x(tile, step):
        if step == 0:
            return tile
        moved = pltpu.roll(tile, 1 if step == -1 else CELLS - 1, 0)
        return jnp.where(sub_x == (0 if step == -1 else CELLS - 1), 0.0, moved)

    def column_copies(src, dst, k):
        made = [
            pltpu.make_async_remote_copy(
                src_ref=src, dst_ref=dst.at[me_s], send_sem=csend.at[8 * k + i],
                recv_sem=crecv.at[k], device_id=column(i), device_id_type=MESH,
            )
            for i in range(1, n_slab)
        ]
        pltpu.make_async_copy(src, dst.at[me_s], crecv.at[k]).start()
        for copy in made:
            copy.start()
        return made

    odd = lax.rem(me_b, 2)
    even_row = me_b - odd

    def plane_copies(src, dst, slab, k):
        made = []
        for i in range(2):
            k_blk = even_row + i
            copy = pltpu.make_async_remote_copy(
                src_ref=src, dst_ref=dst.at[odd, me_s], send_sem=csend.at[8 * k + i],
                recv_sem=crecv.at[k], device_id=(slab, k_blk), device_id_type=MESH,
            )
            mine = (me_s == slab) & (me_b == k_blk)
            pl.when(jnp.logical_not(mine))(copy.start)
            pl.when(mine)(pltpu.make_async_copy(src, dst.at[odd, me_s], crecv.at[k]).start)
            made.append((jnp.logical_not(mine), copy))
        return made

    rimsrc1[...] = c_in
    copies2 = rim_copies(rimsrc1, rim1, WIDE, 0)
    for copy in copies2:
        copy.start()
    loaded("coarse")
    for copy in copies2:
        copy.wait_recv()

    for a in range(-2, 3):
        for b in range(-2, 3):
            if a == 0 and b == 0:
                tile = c_in.astype(F32)
            else:
                tile = rim1[WIDE.index((a, b))].astype(F32) * inside(a, b)
            triple[5 * (a + 2) + b + 2] = jnp.concatenate(
                [along_x(tile, r - 1) for r in range(3)], axis=1).astype(BF16)
    plane_row = lambda b: triple[12 + b, :, WID : 2 * WID]
    xsrc[...] = jnp.concatenate(
        [jnp.where(odd == 0, plane_row(i - 1).astype(F32), plane_row(i - 2).astype(F32))
         for i in range(4)], axis=1).astype(BF16)
    x_sent = column_copies(xsrc, xgat, 0)
    acc = jnp.zeros((9 * CELLS, WID), F32)
    for p in range(3):
        for q in range(3):
            rows = jnp.concatenate(
                [triple[5 * (a + p + 1) + b + q + 1] for a, b in BOXES], axis=0)
            base = (p * 3 + q) * 3 * WID
            acc = acc + dot(rows, w_coarse[base : base + 3 * WID, :])
    boxes[...] = acc
    for copy in copies3:
        copy.wait_recv()
    for i, (a, b) in enumerate(BOXES):
        value = boxes[CELLS * i : CELLS * i + CELLS]
        sig = jax.nn.sigmoid(value)
        slope = sig * (1.0 + value * (1.0 - sig))
        if i == 4:
            d_pre = dco[...] * slope
            c_out = (c_in.astype(F32) + value * sig).astype(BF16)
        else:
            d_pre = rim2[OFFSETS.index((a, b))] * slope * inside(a, b)
        d_box[i] = d_pre.astype(BF16).astype(F32)
    coarse_out[...] = c_out
    dsrc[...] = jnp.concatenate(
        [jnp.where(odd == 0, d_box[4 + i], d_box[3 + i]) for i in range(2)], axis=1).astype(BF16)
    d_sent = column_copies(dsrc, dgat, 1)
    upsrc[...] = jnp.concatenate([c_out.astype(F32), raised_hi.astype(F32)], axis=1).astype(BF16)
    up_sent = plane_copies(upsrc, upgat, n_slab - 1, 2)
    acc = jnp.zeros((CELLS, WID), F32)
    for p in range(3):
        for q in range(3):
            tile = d_box[3 * (2 - p) + 2 - q]
            for r in range(3):
                base = ((p * 3 + q) * 3 + r) * WID
                moved = along_x(tile, 1 - r).astype(BF16)
                acc = acc + dot_nt(moved, w_coarse[base : base + WID, :])
    g_lat = (dco[...] + acc).astype(BF16)
    grad_latent[...] = g_lat

    halves = [x[:, at : at + 128].astype(F32) for x in (c_out, g_lat) for at in (0, 128)]
    grid = jnp.concatenate(halves + [jnp.zeros((64, 128), F32)], axis=0).astype(BF16)
    rpk[...] = dot(cells_of[...], grid).astype(BF16).reshape(n_blk, 16, 128)
    rarr[0] = rpk[0]
    send_rows(rpk, rarr, True, 2)
    downsrc[...] = jnp.concatenate([g_lat.astype(F32), means_hi.astype(F32)], axis=1).astype(BF16)
    down_sent = plane_copies(downsrc, downgat, 0, 3)

    base_row = me_s * SLAB_ROWS + 144
    first_tap = base_row // WID - 3
    skew = base_row % WID
    pltpu.make_async_copy(xgat, xgat, crecv.at[0]).wait()
    everything = xgat[...].reshape(n_slab * CELLS, 4 * WID).astype(F32)
    for q in range(4):
        xq[q] = everything[:, q * WID : q * WID + WID].T.astype(BF16)
    pltpu.make_async_copy(dgat, dgat, crecv.at[1]).wait()
    pair = dgat[...].reshape(n_slab * CELLS, 2 * WID)
    d_all[...] = jnp.concatenate([pair[:, :WID], pair[:, WID:]], axis=0)

    def tap_rows(i, carry):
        t = first_tap + i
        good = (t >= 0) & (t < 27)
        tc = jnp.clip(t, 0, 26)
        p, q, r = tc // 9, tc // 3 % 3, tc % 3
        shift = ((sub // 16 == lane // 16 + p - 1) & (sub % 16 == lane % 16 + r - 1)).astype(BF16)
        moved = jnp.concatenate([dot(xq[q], shift), dot(xq[q + 1], shift)], axis=1).astype(BF16)
        gbuf[pl.ds(pl.multiple_of(i * WID, WID), WID), :] = (
            dot(moved, d_all[...]) * jnp.where(good, 1.0 / math.sqrt(CELLS * total), 0.0)
        ).astype(BF16)
        return carry

    lax.fori_loop(0, 5, tap_rows, 0, unroll=5)
    rows_scale = 1.0 / math.sqrt(NB * total)

    @pl.when(me_s == n_slab - 1)
    def _():
        pltpu.make_async_copy(upgat, upgat, crecv.at[2]).wait()
        left = upgat[:, :, :, :WID].reshape(2 * n_slab * CELLS, WID)
        twice = (iota((WID, VOX), 1) // 2 == iota((WID, VOX), 0)).astype(BF16)
        left = dot(left, twice).astype(BF16)
        right = upgat[:, :, :, WID:].reshape(2 * n_slab * CELLS, VOX)
        up = jnp.where(iota((VOX, WID), 0) % 2 == 0, dot_tn(left, right[:, :WID]),
                       dot_tn(left, right[:, WID:]))
        gbuf[512:1024, :] = (up * rows_scale).astype(BF16)

    @pl.when(me_s == 0)
    def _():
        pltpu.make_async_copy(downgat, downgat, crecv.at[3]).wait()
        left = downgat[:, :, :, WID:].reshape(2 * n_slab * CELLS, VOX)
        right = downgat[:, :, :, :WID].reshape(2 * n_slab * CELLS, WID)
        gbuf[256:768, :] = (dot_tn(left, right) * rows_scale).astype(BF16)

    def window_of(k):
        unit = (16 * skew + 503 * k) // 256
        return gbuf.at[pl.ds(pl.multiple_of(16 * unit, 16), 48)]

    def send_window(i, carry):
        pltpu.make_async_remote_copy(
            src_ref=window_of(lax.rem(me_b + 2 * i, n_blk)), dst_ref=wland.at[i],
            send_sem=vsend, recv_sem=vrecv.at[0], device_id=rel(2 * i), device_id_type=MESH,
        ).start()
        return carry

    lax.fori_loop(1, n_blk // 2, send_window, 0)
    loaded("perm_t")
    loaded("spread_t")
    row_wait(rarr, arecv.at[2])
    rows = dot(route_t, rarr[...].reshape(packet_rows, 128))
    lifted = jnp.concatenate([rows[0:16], rows[16:32]], axis=1).astype(BF16)
    d_pooled = jnp.concatenate([rows[32:48], rows[48:64]], axis=1).astype(BF16)

    d_means = dot_nt(d_pooled, w_down[...]) * (1.0 / 64.0)
    yrow[...] = dot(d_means.astype(BF16), perm_t[...])

    def fine_slope(g, carry):
        spreadv = expand(g).reshape(4, CH, VOX)
        for bb in range(4):
            b = 4 * g + bb
            d_mid = cot[b].astype(F32) + spreadv[bb]
            big[b] = d_mid
            value = pre[b]
            s = jax.nn.sigmoid(value)
            dpf[b] = (d_mid * (s * (1.0 + value * (1.0 - s)))).astype(BF16)
        return carry

    lax.fori_loop(0, NB // 4, fine_slope, 0, unroll=NB // 4)
    make_faces(dpf, faces2, faces_wide)
    make_packs(faces2, pack2)
    copies4 = face_copies(land2, pack2, 1)
    for copy in copies4:
        copy.start()
    w_back = w_bwd[...].astype(BF16)
    gacc[...] = jnp.zeros((7 * CH, CH), F32)

    def weight_grad(b, carry):
        gacc[...] += dot_nt(own_taps[b], dpf[b])
        return carry

    lax.fori_loop(0, NB, weight_grad, 0, unroll=NB)
    for d in range(6):
        gacc[CH * (d + 1) : CH * (d + 2), :] += dot_nt(near1[d], faces_wide[d])
    fine_bf = (gacc[...] * (1.0 / math.sqrt(NB * total * VOX))).astype(BF16)
    row_to = iota((7 * 16, 7 * CH), 0)
    quarters = []
    for m in range(4):
        pick = iota((7 * 16, 7 * CH), 1) == 64 * (row_to // 16) + 4 * (row_to % 16) + m
        quarters.append(dot(pick.astype(BF16), fine_bf))
    fsrc[...] = jnp.concatenate(quarters, axis=1).astype(BF16).reshape(7, 16, WID)
    fine_copies = [
        pltpu.make_async_remote_copy(
            src_ref=fsrc.at[t], dst_ref=fland.at[me_b], send_sem=usend.at[2 + t],
            recv_sem=vrecv.at[1], device_id=(me_s, t), device_id_type=MESH,
        )
        for t in range(7)
    ]
    for t in range(7):
        pl.when(me_b != t)(fine_copies[t].start)

    @pl.when(me_b < 7)
    def _():
        pltpu.make_async_copy(fsrc.at[lax.rem(me_b, 7)], fland.at[me_b], vrecv.at[1]).start()

    def own_backward(b, carry):
        buf = lax.rem(b, 2)
        roll_taps(dpf, b, back_taps, buf)
        big[b] += dot(w_back, back_taps[buf])
        return carry

    lax.fori_loop(0, NB, own_backward, 0, unroll=NB)
    for copy in copies4:
        copy.wait_recv()
    gather_faces(faces2, land2, near2)
    weigh_faces(w_back, near2)

    def fine_backward(g, carry):
        more = placed(g).reshape(4, CH, VOX)
        for bb in range(4):
            b = 4 * g + bb
            grad_fine[b] = (big[b] + more[bb]).astype(BF16)
        return carry

    lax.fori_loop(0, NB // 4, fine_backward, 0, unroll=NB // 4)
    store_grad = pltpu.make_async_copy(grad_fine, grad_fine_hbm, osem.at[0])
    store_grad.start()

    @pl.when(me_b < 7)
    def _():
        pltpu.make_async_copy(fland, fland, vrecv.at[1]).wait()
        unit_sum = fland[0].astype(F32)
        for i in range(1, n_blk):
            unit_sum = unit_sum + fland[i].astype(F32)
        unit_ref[...] = unit_sum.astype(BF16)

    unit = me_b + 9
    low = (256 * (unit - 2) - 2304 + 502 + 503 * 8) // 503 - 8
    sent = []
    for i in range(2):
        k = low + i
        begin = (2304 + 503 * k + 2560) // 256 - 10
        good = (me_b < 7) & (k >= 0) & (k < n_blk) & (begin <= unit)
        mine = (me_s == 0) & (me_b == k)
        at = jnp.clip(unit - begin, 0, 2)
        away = pltpu.make_async_remote_copy(
            src_ref=unit_ref, dst_ref=uland.at[at, me_s], send_sem=usend.at[i],
            recv_sem=urecv.at[at], device_id=(0, jnp.clip(k, 0, n_blk - 1)), device_id_type=MESH,
        )
        home = pltpu.make_async_copy(unit_ref, uland.at[at, me_s], urecv.at[at])
        pl.when(good & mine)(home.start)
        pl.when(good & jnp.logical_not(mine))(away.start)
        sent.append((good & jnp.logical_not(mine), away))

    yrow[...] = dot(dot(lifted, w_up[...]).astype(BF16), perm_t[...])

    def fine_up(g, carry):
        spreadv = expand(g).reshape(4, CH, VOX)
        for bb in range(4):
            b = 4 * g + bb
            fine_out[b] = (mid[b].astype(F32) + spreadv[bb]).astype(BF16)
        return carry

    lax.fori_loop(0, NB // 4, fine_up, 0, unroll=NB // 4)
    store_out = pltpu.make_async_copy(fine_out, fine_out_hbm, osem.at[1])
    store_out.start()
    row_wait(wland, vrecv.at[0], n_blk // 2 - 1)
    summed = window_of(me_b)[...].astype(F32)
    for i in range(1, n_blk // 2):
        summed = summed + wland[i].astype(F32)
    gsum[...] = summed

    my_unit = (16 * skew + 503 * me_b) // 256
    for u in range(3):
        @pl.when((me_s == 0) & (my_unit + u < 16))
        def _():
            pltpu.make_async_copy(uland.at[u], uland.at[u], urecv.at[u]).wait()
            rows = slice(16 * u, 16 * u + 16)
            gsum[rows, :] += jnp.sum(uland[u].astype(F32), axis=0)

    down_by = skew + 503 * me_b // 16 - 16 * my_unit
    left_by = 16 * (503 * me_b % 16)
    value = pltpu.roll(gsum[...], lax.rem(48 - down_by, 48), 0)
    value = pltpu.roll(value, lax.rem(WID - left_by, WID), 1)
    below = pltpu.roll(value, 47, 0)
    grads_out[...] = jnp.where(
        iota((32, WID), 1) < WID - left_by, value[:32], below[:32])

    for copy in copies1 + copies4 + copies2 + copies3 + x_sent + d_sent:
        copy.wait_send()
    for good, copy in up_sent + down_sent:
        pl.when(good)(copy.wait_send)
    row_wait(pk_a, asend.at[0])
    row_wait(pk_b, asend.at[1])
    row_wait(rpk, asend.at[2])
    row_wait(wland, vsend, n_blk // 2 - 1)
    for t in range(7):
        pl.when(me_b != t)(fine_copies[t].wait_send)
    for good, copy in sent:
        pl.when(good)(copy.wait_send)
    store_grad.wait()
    store_out.wait()


def fused(n_slab, n_blk, *operands):
    vmem = pl.BlockSpec(memory_space=pltpu.VMEM)
    smem = pl.BlockSpec(memory_space=pltpu.SMEM)
    hbm = pl.BlockSpec(memory_space=pl.ANY)
    sds = jax.ShapeDtypeStruct
    fine_like = sds((NB, CH, VOX), BF16)
    cells = sds((CELLS, WID), BF16)
    dma = pltpu.SemaphoreType.DMA
    rows = (n_blk, 16, 128)
    bf = lambda *shape: pltpu.VMEM(shape, BF16)
    f32 = lambda *shape: pltpu.VMEM(shape, F32)
    return pl.pallas_call(
        functools.partial(kernel, n_slab, n_blk),
        name="window",
        out_shape=(fine_like, cells, fine_like, cells, sds((32, WID), F32)),
        in_specs=[hbm] * 2 + [vmem] * 3 + [hbm] * 3 + [smem] * 3 + [hbm] * 2 + [vmem] + [hbm] * 4,
        out_specs=(hbm, vmem, hbm, vmem, vmem),
        scratch_shapes=[
            bf(NB, CH, VOX), bf(NB, CH, VOX), bf(VOX, WID), bf(WID, VOX), bf(27 * WID, WID),
            bf(VOX, 6 * 128), bf(6 * 128, VOX), bf(VOX, VOX), bf(VOX, VOX), bf(VOX, VOX),
            bf(VOX, VOX),
            bf(NB, CH, VOX), bf(NB, CH, VOX), bf(SLOTS, CH, 128), bf(SLOTS, CH, 128),
            bf(6, CH, NB * 128), bf(2, 3, CH, 128), bf(2, 3, CH, 128), bf(6, CH, 128),
            bf(6, CH, 128), bf(2, CH, 128), bf(6, CH, NB * 128), bf(6, CH, NB * 128),
            bf(NB, CH, 6 * 128), bf(NB, 7 * CH, VOX), bf(2, 7 * CH, VOX), f32(NB, CH, VOX), bf(NB, CH, VOX), bf(NB, CH, VOX),
            f32(NB, CH, VOX), f32(CELLS, VOX), f32(CELLS, VOX), f32(CH, 7 * CH),
            bf(n_blk * 16, 128), bf(n_blk * 16, 128), bf(*rows), bf(*rows), bf(*rows), bf(*rows), bf(*rows), bf(*rows),
            bf(24, CELLS, WID), f32(8, CELLS, WID), bf(CELLS, WID), f32(CELLS, WID),
            bf(25, CELLS, 3 * WID), f32(9 * CELLS, WID), f32(9, CELLS, WID), bf(WID, WID),
            f32(7 * CH, CH),
            bf(CELLS, 4 * WID), bf(CELLS, 2 * WID), bf(CELLS, 3 * WID), bf(CELLS, 3 * WID),
            bf(n_slab, CELLS, 4 * WID), bf(n_slab, CELLS, 2 * WID), bf(2, n_slab, CELLS, 3 * WID),
            bf(2, n_slab, CELLS, 3 * WID),
            f32(CELLS, WID), bf(4, WID, 128), bf(5 * WID, WID), bf(n_blk // 2, 48, WID), bf(7, 16, WID),
            bf(n_blk, 16, WID), bf(16, WID), bf(3, n_slab, 16, WID), f32(48, WID),
            pltpu.VMEM((8, 128), jnp.int32), pltpu.SMEM((8, 128), jnp.int32),
            dma((16,)), dma, dma((2,)), dma((4,)), dma((4,)), dma((3,)), dma((3,)), dma((32,)),
            dma((32,)), dma((32,)), dma((4,)), dma, dma((2,)), dma((9,)), dma((3,)),
        ],
        compiler_params=pltpu.CompilerParams(
            collective_id=0, has_side_effects=True, vmem_limit_bytes=56 * 1024 * 1024
        ),
    )(*operands)


def finish_kernel(fine_in, grad_in, coarse_in, latent_in, flat_in, fine_to, grad_to, coarse_to,
                  latent_to, flat_to, held, cells, flat, in_sems, out_sems):
    moves = [(flat_in, flat, None), (coarse_in, cells.at[0], coarse_to),
             (latent_in, cells.at[1], latent_to)]
    for i, (src, dst) in enumerate(((fine_in, fine_to), (grad_in, grad_to))):
        for j in range(4):
            rows = pl.ds(3 * j, 3)
            moves.append((src.at[rows], held.at[i, rows], dst.at[rows]))
    takes = [pltpu.make_async_copy(src, mid, in_sems.at[n])
             for n, (src, mid, dst) in enumerate(moves)]
    gives = [pltpu.make_async_copy(mid, dst, out_sems.at[n])
             for n, (src, mid, dst) in enumerate(moves) if dst is not None]
    for copy in takes:
        copy.start()
    takes[0].wait()
    for r in range(SHARD // WID):
        flat_to[WID * r : WID * r + WID] = flat[r, :]
    rest = SHARD % WID
    flat_to[SHARD - rest : SHARD] = flat[SHARD // WID, :rest]
    for take, give in zip(takes[1:], gives):
        take.wait()
        give.start()
    for give in gives:
        give.wait()


def finish(fine_out, coarse_out, grad_fine, grad_latent, flat):
    hbm = pl.BlockSpec(memory_space=pl.ANY)
    like = lambda a: jax.ShapeDtypeStruct(a.shape, a.dtype)
    fine_out, grad_fine, coarse_out, grad_latent, flat = pl.pallas_call(
        finish_kernel,
        name="finish",
        out_shape=(like(fine_out), like(grad_fine), like(coarse_out), like(grad_latent),
                   jax.ShapeDtypeStruct((SHARD,), F32)),
        in_specs=[hbm] * 5,
        out_specs=(hbm, hbm, hbm, hbm, pl.BlockSpec(memory_space=pltpu.VMEM)),
        scratch_shapes=[pltpu.VMEM((2, NB, CH, VOX), BF16), pltpu.VMEM((2, CELLS, WID), BF16),
                        pltpu.VMEM((32, WID), F32), pltpu.SemaphoreType.DMA((11,)),
                        pltpu.SemaphoreType.DMA((11,))],
    )(fine_out, grad_fine, coarse_out, grad_latent, flat)
    return fine_out, coarse_out, grad_fine, grad_latent, flat


def shards(
    n_slab, n_blk,
    fine_in, latent, w_fine, w_down, w_coarse, w_up, neighbors, pool_owner, pool_cell, cot_fine,
    cot_coarse,
):
    outs = fused(
        n_slab, n_blk,
        fine_in, cot_fine, latent.reshape(CELLS, WID), cot_coarse.reshape(CELLS, WID),
        w_fine.T, w_down, w_up, w_coarse, neighbors.T, pool_owner.reshape(NB), pool_cell,
        *tables())
    fine_out, c_out, grad_fine, g_lat, weight_grads = finish(*outs)
    return (fine_out, c_out.reshape(latent.shape), grad_fine, g_lat.reshape(latent.shape),
            weight_grads)


def solution(mesh):
    n_slab, n_blk = mesh.shape["slab"], mesh.shape["blk"]
    return jax.shard_map(
        functools.partial(shards, n_slab, n_blk),
        mesh=mesh,
        in_specs=(
            P(("slab", "blk"), None, None), P("slab", "blk", None, None), P(), P(), P(), P(),
            P(("slab", "blk"), None), P(("slab", "blk"), None), P(("slab", "blk")),
            P(("slab", "blk"), None, None), P("slab", "blk", None, None),
        ),
        out_specs=(
            P(("slab", "blk"), None, None), P("slab", "blk", None, None),
            P(("slab", "blk"), None, None), P("slab", "blk", None, None), P(("slab", "blk")),
        ),
        check_vma=False,
    )
```
